256 devices in a mesh: tm: 4 (over y_lo, core), space: 64 (over z, x, y_hi).
Axes of the slice: x: 4, y: 4 (y_hi: 2, y_lo: 2; y = y_hi * 2 + y_lo), z: 8, core: 2. Of those that a mesh axis runs over, the one named last changes fastest.
Arguments:
- slab_states: float32 [4, 2, 512, 32, 512], P('tm', None, 'space'), may hold values from -6 to 6
- velocity: float32 [2, 3, 512, 32, 512], P(None, None, 'space'), may hold values from -0.9 to 0.9
- snap_of_step: int32 [4, 2], P('tm'), may hold values from 0 to 1
Outputs:
- slab_starts: float32 [4, 2, 512, 32, 512], P('tm', None, 'space')
- heater_grad: float32 [512, 32, 512], P('space', 'tm')
The draws below stay inside these ranges and needn't reach their ends.
All inputs are finite; a program needn't handle non-finite values.
Results may differ from the reference program's by a relative error of at most 0.00002.
Values sent between devices are 32-bit elements; how exact they have to be, the bound alone decides.
No kernel may reach another device: no remote copies, remote signals or barrier semaphores. Data moves between devices by JAX's collectives and lax.ppermute only.
A program may use at most 64 MiB of HBM per device.

```python
import jax
import jax.numpy as jnp
from jax import lax

NY = 32
NZ = 512
STEPS = 2
SNAPS = 2
NX = 512
SLABS = 4


def place_ends(array, key, low, high):
    place = [jax.random.randint(jax.random.fold_in(key, axis), (), 0, length) for axis, length in enumerate(array.shape)]
    longest = array.shape.index(max(array.shape))
    next_to = place[:longest] + [(place[longest] + 1) % array.shape[longest]] + place[longest + 1:]
    return array.at[tuple(place)].set(low).at[tuple(next_to)].set(high)


def level_of(rng, shape, shards, smallest, top_value):
    loudness = 1.0
    for axis_at, shards_of in shards:
        draws = jax.random.uniform(jax.random.fold_in(jax.random.fold_in(rng, 6), axis_at), (shards_of,), jnp.float32, smallest / len(shards), top_value / len(shards))
        loudness = loudness * jnp.repeat(jnp.exp(draws), shape[axis_at] // shards_of).reshape((-1,) + (1,) * (len(shape) - 1 - axis_at))
    return loudness


def gaussian(key, extent, width, most, cuts=(), held_as=jnp.bfloat16):
    values = jax.random.normal(key, extent, jnp.float32) * width
    if len(cuts) > 0:
        values = level_of(key, extent, cuts, -0.22, 0.18) * values
    return jnp.clip(values, min=-most, max=most).astype(held_as)


def setup_inputs(seed: int = 0) -> dict:
    key_list = jax.random.split(jax.random.key(seed), 4)
    return {
        "slab_states": gaussian(key_list[0], (SLABS, 2, NX, NY, NZ), 1.0, 6.0, ((0, 4), (2, 64)), jnp.float32),
        "velocity": gaussian(key_list[1], (SNAPS, 3, NX, NY, NZ), 0.3, 0.9, ((2, 64),), jnp.float32),
        "snap_of_step": place_ends(jax.random.randint(key_list[2], (SLABS, STEPS), 0, SNAPS), jax.random.fold_in(key_list[2], 1), 0, SNAPS - 1).astype(jnp.int32),
    }


coupling = 0.3


def advance(widened, flow):
    centre = widened[:, 1:-1]
    east_side = widened[:, 2:]
    west_side = widened[:, :-2]
    north_side = jnp.pad(centre, ((0, 0), (0, 0), (0, 1), (0, 0)))[:, :, 1:]
    south_side = jnp.pad(centre, ((0, 0), (0, 0), (1, 0), (0, 0)))[:, :, :-1]
    upper_side = jnp.pad(centre, ((0, 0), (0, 0), (0, 0), (0, 1)))[:, :, :, 1:]
    lower_side = jnp.pad(centre, ((0, 0), (0, 0), (0, 0), (1, 0)))[:, :, :, :-1]
    laplace = east_side + west_side + north_side + south_side + upper_side + lower_side - 6.0 * centre
    transport = flow[0] * (east_side - west_side) + flow[1] * (north_side - south_side) + flow[2] * (upper_side - lower_side)
    temper = centre[0] + 0.14 * laplace[0] + 0.25 * transport[0] + coupling * centre[1]
    dopant = centre[1] + 0.06 * laplace[1] + 0.25 * transport[1]
    return jnp.stack([temper, dopant])


def sweep_slab(adjoint, flow_bank, snaps):
    total = jnp.zeros(adjoint.shape[1:], jnp.float32)
    for step_index in reversed(range(STEPS)):
        flow = lax.dynamic_index_in_dim(flow_bank, snaps[step_index], 0, keepdims=False)
        widened = jnp.pad(adjoint, ((0, 0), (1, 1), (0, 0), (0, 0)))
        adjoint = advance(widened, flow)
        total = total + adjoint[0]
    return adjoint, total


def reference(slab_states, velocity, snap_of_step):
    first = [sweep_slab(slab_states[slab_index], velocity, snap_of_step[slab_index])[0] for slab_index in range(SLABS)]
    carried = first[1:] + [slab_states[SLABS - 1]]
    starts = []
    grand = jnp.zeros(slab_states.shape[2:], jnp.float32)
    for slab_index in range(SLABS):
        result, total = sweep_slab(carried[slab_index], velocity, snap_of_step[slab_index])
        starts.append(result)
        grand = grand + total
    return jnp.stack(starts), grand / STEPS
```

```python
import functools

import jax
import jax.numpy as jnp
from jax import lax
from jax.experimental import pallas as pl
from jax.experimental.pallas import tpu as pltpu
from jax.sharding import PartitionSpec as P

coupling = 0.3
diffusion = (0.14, 0.06)
sub, lanes = 8, 128


def tiles(shape):
    rows, cols = shape
    return [(i, j) for i in range(rows // sub) for j in range(cols // lanes)]


def spot(i, j):
    return (pl.ds(i * sub, sub), pl.ds(j * lanes, lanes))


def neighbours(at, i, j, shape):
    rows, cols = shape
    centre = at(i, j)
    row = lax.broadcasted_iota(jnp.int32, (sub, lanes), 0)
    col = lax.broadcasted_iota(jnp.int32, (sub, lanes), 1)
    zero = jnp.zeros_like(centre)
    after = at(i + 1, j) if (i + 1) * sub < rows else zero
    before = at(i - 1, j) if i > 0 else zero
    north = pltpu.roll(jnp.where(row == 0, after, centre), sub - 1, 0)
    south = pltpu.roll(jnp.where(row == sub - 1, before, centre), 1, 0)
    after = at(i, j + 1) if (j + 1) * lanes < cols else zero
    before = at(i, j - 1) if j > 0 else zero
    upper = pltpu.roll(jnp.where(col == 0, after, centre), lanes - 1, 1)
    lower = pltpu.roll(jnp.where(col == lanes - 1, before, centre), 1, 1)
    return centre, (north + south) + (upper + lower), north - south, upper - lower


def advanced(fields, pairs, flow, i, j, shape):
    u, v, w = flow
    out, centres = [], []
    for f in (0, 1):
        centre, total, dy, dz = neighbours(functools.partial(fields, f), i, j, shape)
        side_sum, side_diff = pairs(f, i, j)
        c = diffusion[f]
        moved = u * side_diff + v * dy + w * dz
        out.append(((1.0 - 6.0 * c) * centre + c * (side_sum + total)) + 0.25 * moved)
        centres.append(centre)
    out[0] = out[0] + coupling * centres[1]
    return out


def layer_of(ref, l):
    return lambda f, i, j: ref[(f, l) + spot(i, j)]


def flow_of(velocity, snap, l):
    return lambda i, j: [velocity[(snap, d, l) + spot(i, j)] for d in range(3)]


def full_layer(below, here, above, flow, shape, store):
    def pairs(f, i, j):
        hi, lo = above(f, i, j), below(f, i, j)
        return hi + lo, hi - lo

    for i, j in tiles(shape):
        store(i, j, advanced(here, pairs, flow(i, j), i, j, shape))


def pack(state, velocity, snap, message, layer, inner, sign, shape):
    near, here, flow = layer_of(state, inner), layer_of(state, layer), flow_of(velocity, snap, layer)

    def pairs(f, i, j):
        value = near(f, i, j)
        return value, sign * value

    for i, j in tiles(shape):
        current = flow(i, j)
        out = advanced(here, pairs, current, i, j, shape)
        for f in (0, 1):
            message[(f,) + spot(i, j)] = here(f, i, j)
            message[(2 + f,) + spot(i, j)] = out[f]
        message[(4,) + spot(i, j)] = current[0]


def sides(depth):
    parity = lax.rem(lax.axis_index("space"), 2)
    even = parity == 0
    high = (jnp.where(even, depth - 1, 0), jnp.where(even, depth - 2, 1), jnp.where(even, -1.0, 1.0))
    low = (jnp.where(even, 0, depth - 1), jnp.where(even, 1, depth - 2), jnp.where(even, 1.0, -1.0))
    return parity, high, low


def pack_both(state, velocity, snap, message_one, message_two, depth, shape):
    unused, one, two = sides(depth)
    pack(state, velocity, snap, message_one, *one, shape)
    pack(state, velocity, snap, message_two, *two, shape)


def take_halos(blocks, state, halo_one, halo_two, halos, widened, depth, shape):
    parity, one, two = sides(depth)
    place = lax.axis_index("space")
    inside = jnp.logical_and(place > 0, place < blocks - 1)
    for halo, (edge, unused, sign), shown, high in (
        (halo_one, one, None, 1 - parity),
        (halo_two, two, inside, parity),
    ):
        for i, j in tiles(shape):
            u = halo[(4,) + spot(i, j)]
            for f in (0, 1):
                now = halo[(f,) + spot(i, j)]
                own = state[(f, edge) + spot(i, j)]
                later = halo[(2 + f,) + spot(i, j)] + (diffusion[f] + (0.25 * sign) * u) * own
                if shown is not None:
                    now = jnp.where(shown, now, 0.0)
                    later = jnp.where(shown, later, 0.0)
                halos[(high, f) + spot(i, j)] = now
                widened[(f, high * (depth + 1)) + spot(i, j)] = later


def two_steps(blocks, state, halo_one, halo_two, velocity, snaps, out, total, extra, halos, widened):
    depth, shape = state.shape[1], state.shape[2:]
    take_halos(blocks, state, halo_one, halo_two, halos, widened, depth, shape)
    halo_at = lambda h: lambda f, i, j: halos[(h, f) + spot(i, j)]

    def first_step(l, below, above):
        def store(i, j, values):
            for f in (0, 1):
                widened[(f, l + 1) + spot(i, j)] = values[f]

        full_layer(below, layer_of(state, l), above, flow_of(velocity, snaps[0, 1], l), shape, store)

    first_step(0, halo_at(0), layer_of(state, 1))
    first_step(depth - 1, layer_of(state, depth - 2), halo_at(1))

    def inner(l, carry):
        first_step(l, layer_of(state, l - 1), layer_of(state, l + 1))
        return carry

    lax.fori_loop(1, depth - 1, inner, 0)

    def outer(l, carry):
        def store(i, j, values):
            for f in (0, 1):
                out[(f, l) + spot(i, j)] = values[f]
            summed = widened[(0, l + 1) + spot(i, j)] + values[0]
            if extra is not None:
                summed = summed + extra(l, i, j)
            total[(l,) + spot(i, j)] = summed

        full_layer(
            layer_of(widened, l), layer_of(widened, l + 1), layer_of(widened, l + 2),
            flow_of(velocity, snaps[0, 0], l), shape, store,
        )
        return carry

    lax.fori_loop(0, depth, outer, 0)


def pack_kernel(snaps, state, velocity, message_one, message_two):
    pack_both(state, velocity, snaps[0, 1], message_one, message_two, state.shape[1], state.shape[2:])


def first_kernel(blocks, snaps, snaps_next, state, halo_one, halo_two, velocity,
                 out, total, message_one, message_two, halos, widened):
    two_steps(blocks, state, halo_one, halo_two, velocity, snaps_next, out, total, None, halos, widened)
    pack_both(out, velocity, snaps[0, 1], message_one, message_two, state.shape[1], state.shape[2:])


def second_kernel(blocks, slabs, snaps, state, halo_one, halo_two, velocity, total_before, from_core,
                  out, *rest):
    pieces, (total, halos, widened) = rest[:slabs], rest[slabs:]
    slab = lax.axis_index("tm")
    depth, shape = state.shape[1], state.shape[2:]
    rows = shape[0] // slabs

    @pl.when(slab == slabs - 1)
    def _():
        out[...] = from_core[...]
        for piece in pieces:
            piece[...] = jnp.zeros_like(piece)

    @pl.when(slab < slabs - 1)
    def _():
        with_last = slab == slabs - 2

        def extra(l, i, j):
            return jnp.where(with_last, total_before[(l,) + spot(i, j)], 0.0)

        two_steps(blocks, state, halo_one, halo_two, velocity, snaps, out, total, extra, halos, widened)
        for by in range(slabs):
            start = pl.multiple_of(lax.rem(slab + by, slabs) * rows, rows)
            pieces[by][...] = total[:, pl.ds(start, rows), :] * 0.5


def solution(mesh):
    slabs, blocks = mesh.shape["tm"], mesh.shape["space"]
    vmem, smem = pl.BlockSpec(memory_space=pltpu.VMEM), pl.BlockSpec(memory_space=pltpu.SMEM)
    params = pltpu.CompilerParams(vmem_limit_bytes=40 * 1024 * 1024)

    def index(t, s):
        return (t % slabs) * blocks + s % blocks

    def moved(array, to):
        pairs = [(index(t, s), index(*to(t, s))) for t in range(slabs) for s in range(blocks)]
        return lax.ppermute(array, ("tm", "space"), pairs)

    def one(s):
        return s ^ 1

    def two(s):
        return (((s + 1) ^ 1) - 1) % blocks

    def body(slab_states, velocity, snap_of_step):
        start = slab_states[0]
        fields, depth, ny, nz = start.shape
        block = jax.ShapeDtypeStruct(start.shape, jnp.float32)
        layer = jax.ShapeDtypeStruct((5, ny, nz), jnp.float32)
        scalar = jax.ShapeDtypeStruct((depth, ny, nz), jnp.float32)
        piece = jax.ShapeDtypeStruct((depth, ny // slabs, nz), jnp.float32)
        scratch = [
            pltpu.VMEM((2, fields, ny, nz), jnp.float32),
            pltpu.VMEM((fields, depth + 2, ny, nz), jnp.float32),
        ]

        state = moved(start, lambda t, s: (t - 1, s))
        snaps_next = moved(snap_of_step, lambda t, s: (t - 1, s))
        message_one, message_two = pl.pallas_call(
            pack_kernel,
            out_shape=(layer, layer),
            in_specs=[smem, vmem, vmem],
            out_specs=(vmem, vmem),
            compiler_params=params,
        )(snap_of_step, start, velocity)
        halo_one = moved(message_one, lambda t, s: (t - 1, one(s)))
        halo_two = moved(message_two, lambda t, s: (t - 1, two(s)))
        first, total_first, message_one, message_two = pl.pallas_call(
            functools.partial(first_kernel, blocks),
            out_shape=(block, scalar, layer, layer),
            in_specs=[smem, smem] + [vmem] * 4,
            out_specs=(vmem,) * 4,
            scratch_shapes=scratch,
            compiler_params=params,
        )(snap_of_step, snaps_next, state, halo_one, halo_two, velocity)
        halo_one = moved(message_one, lambda t, s: (t, one(s)))
        halo_two = moved(message_two, lambda t, s: (t, two(s)))
        from_core = moved(first, lambda t, s: (t ^ 1, s))
        results = pl.pallas_call(
            functools.partial(second_kernel, blocks, slabs),
            out_shape=(block,) + (piece,) * slabs,
            in_specs=[smem] + [vmem] * 6,
            out_specs=(vmem,) * (1 + slabs),
            scratch_shapes=[pltpu.VMEM(scalar.shape, jnp.float32)] + scratch,
            compiler_params=params,
        )(snap_of_step, first, halo_one, halo_two, velocity, total_first, from_core)
        gradient = results[1]
        for by in range(1, slabs):
            gradient = gradient + moved(results[1 + by], lambda t, s, by=by: (t + by, s))
        return (results[0][None], gradient)

    return jax.shard_map(
        body,
        mesh=mesh,
        in_specs=(P("tm", None, "space", None, None), P(None, None, "space", None, None), P("tm", None)),
        out_specs=(P("tm", None, "space", None, None), P("space", "tm", None)),
        check_vma=False,
    )
```

```python
import functools

import jax
import jax.numpy as jnp
from jax import lax
from jax.experimental import pallas as pl
from jax.experimental.pallas import tpu as pltpu
from jax.sharding import PartitionSpec as P

coupling = 0.3
diffusion = (0.14, 0.06)
sub, lanes = 8, 128


def tiles(shape):
    rows, cols = shape
    return [(i, j) for i in range(rows // sub) for j in range(cols // lanes)]


def spot(i, j):
    return (pl.ds(i * sub, sub), pl.ds(j * lanes, lanes))


def neighbours(at, i, j, shape):
    rows, cols = shape
    centre = at(i, j)
    row = lax.broadcasted_iota(jnp.int32, (sub, lanes), 0)
    col = lax.broadcasted_iota(jnp.int32, (sub, lanes), 1)
    zero = jnp.zeros_like(centre)
    after = at(i + 1, j) if (i + 1) * sub < rows else zero
    before = at(i - 1, j) if i > 0 else zero
    north = pltpu.roll(jnp.where(row == 0, after, centre), sub - 1, 0)
    south = pltpu.roll(jnp.where(row == sub - 1, before, centre), 1, 0)
    after = at(i, j + 1) if (j + 1) * lanes < cols else zero
    before = at(i, j - 1) if j > 0 else zero
    upper = pltpu.roll(jnp.where(col == 0, after, centre), lanes - 1, 1)
    lower = pltpu.roll(jnp.where(col == lanes - 1, before, centre), 1, 1)
    return centre, (north + south) + (upper + lower), north - south, upper - lower


def advanced(fields, pairs, flow, i, j, shape):
    u, v, w = flow
    out, centres = [], []
    for f in (0, 1):
        centre, total, dy, dz = neighbours(functools.partial(fields, f), i, j, shape)
        side_sum, side_diff = pairs(f, i, j)
        c = diffusion[f]
        moved = u * side_diff + v * dy + w * dz
        out.append(((1.0 - 6.0 * c) * centre + c * (side_sum + total)) + 0.25 * moved)
        centres.append(centre)
    out[0] = out[0] + coupling * centres[1]
    return out


def layer_of(ref, l):
    return lambda f, i, j: ref[(f, l) + spot(i, j)]


def flow_of(velocity, snap, l):
    return lambda i, j: [velocity[(snap, d, l) + spot(i, j)] for d in range(3)]


def full_layer(below, here, above, flow, shape, store):
    def pairs(f, i, j):
        hi, lo = above(f, i, j), below(f, i, j)
        return hi + lo, hi - lo

    for i, j in tiles(shape):
        store(i, j, advanced(here, pairs, flow(i, j), i, j, shape))


def pack(state, velocity, snap, message, layer, inner, sign, at, shape):
    near, here, flow = layer_of(state, inner), layer_of(state, layer), flow_of(velocity, snap, at)

    def pairs(f, i, j):
        value = near(f, i, j)
        return value, sign * value

    for i, j in tiles(shape):
        current = flow(i, j)
        out = advanced(here, pairs, current, i, j, shape)
        for f in (0, 1):
            message[(f,) + spot(i, j)] = here(f, i, j)
            message[(2 + f,) + spot(i, j)] = out[f]
        message[(4,) + spot(i, j)] = current[0]


def sides(depth):
    parity = lax.rem(lax.axis_index("space"), 2)
    even = parity == 0
    high = (jnp.where(even, depth - 1, 0), jnp.where(even, depth - 2, 1), jnp.where(even, -1.0, 1.0))
    low = (jnp.where(even, 0, depth - 1), jnp.where(even, 1, depth - 2), jnp.where(even, 1.0, -1.0))
    return parity, high, low


def pack_both(state, velocity, snap, message_one, message_two, depth, shape):
    unused, one, two = sides(depth)
    if velocity.shape[2] == depth:
        at_one, at_two = one[0], two[0]
    else:
        at_one, at_two = one[0] // (depth - 1), two[0] // (depth - 1)
    pack(state, velocity, snap, message_one, *one, at_one, shape)
    pack(state, velocity, snap, message_two, *two, at_two, shape)


def take_halos(blocks, state, halo_one, halo_two, halos, widened, depth, shape):
    parity, one, two = sides(depth)
    place = lax.axis_index("space")
    inside = jnp.logical_and(place > 0, place < blocks - 1)
    for halo, (edge, unused, sign), shown, high in (
        (halo_one, one, None, 1 - parity),
        (halo_two, two, inside, parity),
    ):
        for i, j in tiles(shape):
            u = halo[(4,) + spot(i, j)]
            for f in (0, 1):
                now = halo[(f,) + spot(i, j)]
                own = state[(f, edge) + spot(i, j)]
                later = halo[(2 + f,) + spot(i, j)] + (diffusion[f] + (0.25 * sign) * u) * own
                if shown is not None:
                    now = jnp.where(shown, now, 0.0)
                    later = jnp.where(shown, later, 0.0)
                halos[(high, f) + spot(i, j)] = now
                widened[(f, high * (depth + 1)) + spot(i, j)] = later


def two_steps(blocks, state, halo_one, halo_two, velocity, snaps, out, total, halos, widened):
    depth, shape = state.shape[1], state.shape[2:]
    take_halos(blocks, state, halo_one, halo_two, halos, widened, depth, shape)
    halo_at = lambda h: lambda f, i, j: halos[(h, f) + spot(i, j)]

    def first_step(l, below, above):
        def store(i, j, values):
            for f in (0, 1):
                widened[(f, l + 1) + spot(i, j)] = values[f]

        full_layer(below, layer_of(state, l), above, flow_of(velocity, snaps[0, 1], l), shape, store)

    first_step(0, halo_at(0), layer_of(state, 1))
    first_step(depth - 1, layer_of(state, depth - 2), halo_at(1))

    def inner(l, carry):
        first_step(l, layer_of(state, l - 1), layer_of(state, l + 1))
        return carry

    lax.fori_loop(1, depth - 1, inner, 0)

    def outer(l, carry):
        def store(i, j, values):
            for f in (0, 1):
                out[(f, l) + spot(i, j)] = values[f]
            if total is not None:
                total[(l,) + spot(i, j)] = widened[(0, l + 1) + spot(i, j)] + values[0]

        full_layer(
            layer_of(widened, l), layer_of(widened, l + 1), layer_of(widened, l + 2),
            flow_of(velocity, snaps[0, 0], l), shape, store,
        )
        return carry

    lax.fori_loop(0, depth, outer, 0)


def pack_kernel(snaps, state, velocity, message_one, message_two, scalars, edges, flows, sems):
    depth, shape = state.shape[1], state.shape[2:]
    copies = [
        (snaps, scalars),
        (state.at[:, pl.ds(0, 2)], edges.at[:, pl.ds(0, 2)]),
        (state.at[:, pl.ds(depth - 2, 2)], edges.at[:, pl.ds(2, 2)]),
        (velocity.at[:, :, pl.ds(0, 1)], flows.at[:, :, pl.ds(0, 1)]),
        (velocity.at[:, :, pl.ds(depth - 1, 1)], flows.at[:, :, pl.ds(1, 1)]),
    ]
    copies = [pltpu.make_async_copy(*pair, sems.at[n]) for n, pair in enumerate(copies)]
    for copy in copies:
        copy.start()
    for copy in copies:
        copy.wait()
    pack_both(edges, flows, scalars[0, 1], message_one, message_two, edges.shape[1], shape)


def first_kernel(blocks, slabs, snaps, snaps_next, state, halo_one, halo_two, velocity, start, own_one, own_two,
                 out, message_one, message_two, halos, widened):
    last = lax.axis_index("tm") == slabs - 1

    @pl.when(last)
    def _():
        pltpu.sync_copy(start, out)
        message_one[...] = own_one[...]
        message_two[...] = own_two[...]

    @pl.when(jnp.logical_not(last))
    def _():
        two_steps(blocks, state, halo_one, halo_two, velocity, snaps_next, out, None, halos, widened)
        pack_both(out, velocity, snaps[0, 1], message_one, message_two, state.shape[1], state.shape[2:])


def second_kernel(blocks, slabs, snaps, state, halo_one, halo_two, velocity, out, *rest):
    pieces, (total, halos, widened) = rest[:slabs], rest[slabs:]
    rows = state.shape[2] // slabs
    two_steps(blocks, state, halo_one, halo_two, velocity, snaps, out, total, halos, widened)
    for by in range(slabs):
        start = pl.multiple_of(lax.rem(lax.axis_index("tm") + by, slabs) * rows, rows)
        pieces[by][...] = total[:, pl.ds(start, rows), :] * 0.5


def solution(mesh):
    slabs, blocks = mesh.shape["tm"], mesh.shape["space"]
    vmem, smem = pl.BlockSpec(memory_space=pltpu.VMEM), pl.BlockSpec(memory_space=pltpu.SMEM)
    anywhere = pl.BlockSpec(memory_space=pltpu.HBM)
    params = pltpu.CompilerParams(vmem_limit_bytes=40 * 1024 * 1024)

    def index(t, s):
        return (t % slabs) * blocks + s % blocks

    def moved(array, to):
        pairs = [(index(t, s), index(*to(t, s))) for t in range(slabs) for s in range(blocks)]
        return lax.ppermute(array, ("tm", "space"), pairs)

    def one(s):
        return s ^ 1

    def two(s):
        return (((s + 1) ^ 1) - 1) % blocks

    def body(slab_states, velocity, snap_of_step):
        start = slab_states[0]
        fields, depth, ny, nz = start.shape
        block = jax.ShapeDtypeStruct(start.shape, jnp.float32)
        layer = jax.ShapeDtypeStruct((5, ny, nz), jnp.float32)
        scalar = jax.ShapeDtypeStruct((depth, ny, nz), jnp.float32)
        piece = jax.ShapeDtypeStruct((depth, ny // slabs, nz), jnp.float32)
        scratch = [
            pltpu.VMEM((2, fields, ny, nz), jnp.float32),
            pltpu.VMEM((fields, depth + 2, ny, nz), jnp.float32),
        ]

        def earlier(array):
            pairs = [(index(t, s), index(t - 1, s)) for t in range(1, slabs) for s in range(blocks)]
            return lax.ppermute(array, ("tm", "space"), pairs)

        state = earlier(start)
        snaps_next = moved(snap_of_step, lambda t, s: (t - 1, s))
        own_one, own_two = pl.pallas_call(
            pack_kernel,
            out_shape=(layer, layer),
            in_specs=[anywhere] * 3,
            out_specs=(vmem, vmem),
            scratch_shapes=[
                pltpu.SMEM(snap_of_step.shape, jnp.int32),
                pltpu.VMEM((fields, 4, ny, nz), jnp.float32),
                pltpu.VMEM(velocity.shape[:2] + (2, ny, nz), jnp.float32),
                pltpu.SemaphoreType.DMA((5,)),
            ],
            compiler_params=params,
        )(snap_of_step, start, velocity)
        halo_one = moved(own_one, lambda t, s: (t - 1, one(s)))
        halo_two = moved(own_two, lambda t, s: (t - 1, two(s)))
        first, message_one, message_two = pl.pallas_call(
            functools.partial(first_kernel, blocks, slabs),
            out_shape=(block, layer, layer),
            in_specs=[smem, smem] + [vmem] * 4 + [anywhere, vmem, vmem],
            out_specs=(vmem,) * 3,
            scratch_shapes=scratch,
            compiler_params=params,
        )(snap_of_step, snaps_next, state, halo_one, halo_two, velocity, start, own_one, own_two)
        halo_one = moved(message_one, lambda t, s: (t, one(s)))
        halo_two = moved(message_two, lambda t, s: (t, two(s)))
        results = pl.pallas_call(
            functools.partial(second_kernel, blocks, slabs),
            out_shape=(block,) + (piece,) * slabs,
            in_specs=[smem] + [vmem] * 4,
            out_specs=(vmem,) * (1 + slabs),
            scratch_shapes=[pltpu.VMEM(scalar.shape, jnp.float32)] + scratch,
            compiler_params=params,
        )(snap_of_step, first, halo_one, halo_two, velocity)
        gradient = results[1]
        for by in range(1, slabs):
            gradient = gradient + moved(results[1 + by], lambda t, s, by=by: (t + by, s))
        return (results[0][None], gradient)

    return jax.shard_map(
        body,
        mesh=mesh,
        in_specs=(P("tm", None, "space", None, None), P(None, None, "space", None, None), P("tm", None)),
        out_specs=(P("tm", None, "space", None, None), P("space", "tm", None)),
        check_vma=False,
    )
```

```python
import functools

import jax
import jax.numpy as jnp
from jax import lax
from jax.experimental import pallas as pl
from jax.experimental.pallas import tpu as pltpu
from jax.sharding import PartitionSpec as P

coupling = 0.3
diffusion = (0.14, 0.06)
sub, lanes = 8, 128
edge_count = 4


def tiles(shape):
    rows, cols = shape
    return [(i, j) for i in range(rows // sub) for j in range(cols // lanes)]


def spot(i, j):
    return (pl.ds(i * sub, sub), pl.ds(j * lanes, lanes))


def neighbours(at, i, j, shape):
    rows, cols = shape
    centre = at(i, j)
    row = lax.broadcasted_iota(jnp.int32, (sub, lanes), 0)
    col = lax.broadcasted_iota(jnp.int32, (sub, lanes), 1)
    zero = jnp.zeros_like(centre)
    after = at(i + 1, j) if (i + 1) * sub < rows else zero
    before = at(i - 1, j) if i > 0 else zero
    north = pltpu.roll(jnp.where(row == 0, after, centre), sub - 1, 0)
    south = pltpu.roll(jnp.where(row == sub - 1, before, centre), 1, 0)
    after = at(i, j + 1) if (j + 1) * lanes < cols else zero
    before = at(i, j - 1) if j > 0 else zero
    upper = pltpu.roll(jnp.where(col == 0, after, centre), lanes - 1, 1)
    lower = pltpu.roll(jnp.where(col == lanes - 1, before, centre), 1, 1)
    return centre, (north + south) + (upper + lower), north - south, upper - lower


def advanced(fields, pairs, flow, i, j, shape, wanted=(0, 1)):
    u, v, w = flow
    out = []
    for f in wanted:
        centre, total, dy, dz = neighbours(functools.partial(fields, f), i, j, shape)
        side_sum, side_diff = pairs(f, i, j)
        c = diffusion[f]
        moved = u * side_diff + v * dy + w * dz
        new = ((1.0 - 6.0 * c) * centre + c * (side_sum + total)) + 0.25 * moved
        if f == 0:
            new = new + coupling * fields(1, i, j)
        out.append(new)
    return out


def layer_of(ref, l):
    return lambda f, i, j: ref[(f, l) + spot(i, j)]


def flow_of(velocity, snap, l):
    return lambda i, j: [velocity[(snap, d, l) + spot(i, j)] for d in range(3)]


def full_layer(below, here, above, flow, shape, store, wanted=(0, 1)):
    def pairs(f, i, j):
        hi, lo = above(f, i, j), below(f, i, j)
        return hi + lo, hi - lo

    for i, j in tiles(shape):
        store(i, j, advanced(here, pairs, flow(i, j), i, j, shape, wanted))


def into(ref, l):
    def store(i, j, values):
        for f, value in enumerate(values):
            ref[(f, l) + spot(i, j)] = value

    return store


def sides(depth):
    parity = lax.rem(lax.axis_index("space"), 2)
    even = parity == 0
    high = (jnp.where(even, depth - 1, 0), jnp.where(even, depth - 2, 1), jnp.where(even, -1.0, 1.0))
    low = (jnp.where(even, 0, depth - 1), jnp.where(even, 1, depth - 2), jnp.where(even, 1.0, -1.0))
    return parity, high, low


def pack(edges, velocity, snap, message, layer, inner, sign):
    shape = edges.shape[2:]
    at = (layer // (edge_count - 1)) * (velocity.shape[2] - 1)
    near, here, flow = layer_of(edges, inner), layer_of(edges, layer), flow_of(velocity, snap, at)

    def pairs(f, i, j):
        value = near(f, i, j)
        return value, sign * value

    for i, j in tiles(shape):
        current = flow(i, j)
        out = advanced(here, pairs, current, i, j, shape)
        for f in (0, 1):
            message[(f,) + spot(i, j)] = here(f, i, j)
            message[(2 + f,) + spot(i, j)] = out[f]
        message[(4,) + spot(i, j)] = current[0]


def pack_both(edges, velocity, snap, message_one, message_two):
    unused, one, two = sides(edge_count)
    pack(edges, velocity, snap, message_one, *one)
    pack(edges, velocity, snap, message_two, *two)


def take_halos(blocks, state, halo_one, halo_two, halos, after, depth):
    shape = state.shape[2:]
    parity, one, two = sides(depth)
    place = lax.axis_index("space")
    inside = jnp.logical_and(place > 0, place < blocks - 1)
    outer = after.shape[1] - 1
    for halo, (edge, unused, sign), shown, high in (
        (halo_one, one, None, 1 - parity),
        (halo_two, two, inside, parity),
    ):
        for i, j in tiles(shape):
            u = halo[(4,) + spot(i, j)]
            for f in (0, 1):
                now = halo[(f,) + spot(i, j)]
                own = state[(f, edge) + spot(i, j)]
                later = halo[(2 + f,) + spot(i, j)] + (diffusion[f] + (0.25 * sign) * u) * own
                if shown is not None:
                    now = jnp.where(shown, now, 0.0)
                    later = jnp.where(shown, later, 0.0)
                halos[(high, f) + spot(i, j)] = now
                after[(f, high * outer) + spot(i, j)] = later


def halo_at(halos, h):
    return lambda f, i, j: halos[(h, f) + spot(i, j)]


def split_rows(total, pieces):
    rows = total.shape[1] // len(pieces)
    for by, piece in enumerate(pieces):
        start = pl.multiple_of(lax.rem(lax.axis_index("tm") + by, len(pieces)) * rows, rows)
        piece[...] = total[:, pl.ds(start, rows), :] * 0.5


def each(low, high, run):
    def step(l, carry):
        run(l)
        return carry

    lax.fori_loop(low, high, step, 0)


def start_kernel(snaps, state, velocity, message_one, message_two, scalars, edges, flows, sems):
    depth = state.shape[1]
    copies = [
        (snaps, scalars),
        (state.at[:, pl.ds(0, 2)], edges.at[:, pl.ds(0, 2)]),
        (state.at[:, pl.ds(depth - 2, 2)], edges.at[:, pl.ds(2, 2)]),
        (velocity.at[:, :, pl.ds(0, 1)], flows.at[:, :, pl.ds(0, 1)]),
        (velocity.at[:, :, pl.ds(depth - 1, 1)], flows.at[:, :, pl.ds(1, 1)]),
    ]
    copies = [pltpu.make_async_copy(*pair, sems.at[n]) for n, pair in enumerate(copies)]
    for copy in copies:
        copy.start()
    for copy in copies:
        copy.wait()
    pack_both(edges, flows, scalars[0, 1], message_one, message_two)


def first_kernel(blocks, slabs, snaps, snaps_next, state, halo_one, halo_two, velocity, start,
                 widened, edges, message_one, message_two, halos):
    depth, shape = state.shape[1], state.shape[2:]
    last = lax.axis_index("tm") == slabs - 1

    @pl.when(last)
    def _():
        pltpu.sync_copy(start.at[:, pl.ds(0, 2)], edges.at[:, pl.ds(0, 2)])
        pltpu.sync_copy(start.at[:, pl.ds(depth - 2, 2)], edges.at[:, pl.ds(2, 2)])

    @pl.when(jnp.logical_not(last))
    def _():
        take_halos(blocks, state, halo_one, halo_two, halos, widened, depth)

        def first_step(l, below, above):
            flow = flow_of(velocity, snaps_next[0, 1], l)
            full_layer(below, layer_of(state, l), above, flow, shape, into(widened, l + 1))

        first_step(0, halo_at(halos, 0), layer_of(state, 1))
        first_step(depth - 1, layer_of(state, depth - 2), halo_at(halos, 1))
        each(1, depth - 1, lambda l: first_step(l, layer_of(state, l - 1), layer_of(state, l + 1)))

        def second_step(e):
            l = e + (e // 2) * (depth - edge_count)
            flow = flow_of(velocity, snaps_next[0, 0], l)
            here = layer_of(widened, l + 1)
            full_layer(layer_of(widened, l), here, layer_of(widened, l + 2), flow, shape, into(edges, e))

        each(0, edge_count, second_step)

    pack_both(edges, velocity, snaps[0, 1], message_one, message_two)


def inner_kernel(slabs, snaps, snaps_next, widened, edges, velocity, start, carried_on, inner, *rest):
    pieces, (state, final, total, sem) = rest[:slabs], rest[slabs:]
    depth, shape = state.shape[1], state.shape[2:]
    last = lax.axis_index("tm") == slabs - 1

    @pl.when(last)
    def _():
        pltpu.sync_copy(start, state)

    @pl.when(jnp.logical_not(last))
    def _():
        def second_step(l):
            flow = flow_of(velocity, snaps_next[0, 0], l)
            here = layer_of(widened, l + 1)
            full_layer(layer_of(widened, l), here, layer_of(widened, l + 2), flow, shape, into(state, l))

        each(2, depth - 2, second_step)
        state[:, 0:2] = edges[:, 0:2]
        state[:, depth - 2 : depth] = edges[:, 2:4]

    def third_step(l):
        flow = flow_of(velocity, snaps[0, 1], l)
        here = layer_of(state, l)
        full_layer(layer_of(state, l - 1), here, layer_of(state, l + 1), flow, shape, into(carried_on, l))

    each(1, depth - 1, third_step)

    def fourth_step(l):
        def store(i, j, values):
            into(final, l - 2)(i, j, values)
            total[(l - 2,) + spot(i, j)] = carried_on[(0, l) + spot(i, j)] + values[0]

        flow = flow_of(velocity, snaps[0, 0], l)
        here = layer_of(carried_on, l)
        full_layer(layer_of(carried_on, l - 1), here, layer_of(carried_on, l + 1), flow, shape, store)

    each(2, depth - 2, fourth_step)
    copy = pltpu.make_async_copy(final, inner.at[:, pl.ds(2, depth - 4)], sem)
    copy.start()
    split_rows(total, pieces)
    copy.wait()


def last_steps(snaps, carried_on, outer, velocity, store, wanted):
    depth, shape = carried_on.shape[1], carried_on.shape[2:]
    ring = [layer_of(outer, 0), layer_of(outer, 1), layer_of(carried_on, 1), layer_of(carried_on, 2)]
    ring += [layer_of(carried_on, depth - 3), layer_of(carried_on, depth - 2), layer_of(outer, 2), layer_of(outer, 3)]
    for e, at in enumerate((1, 2, 5, 6)):
        l = e + (e // 2) * (depth - edge_count)
        flow = flow_of(velocity, snaps[0, 0], l)
        full_layer(ring[at - 1], ring[at], ring[at + 1], flow, shape, functools.partial(store, e, ring[at]), wanted)


def outer_kernel(blocks, slabs, snaps, edges, halo_one, halo_two, carried_on, velocity, outer, *rest):
    pieces, (halos, total) = rest[:slabs], rest[slabs:]
    depth, shape = carried_on.shape[1], carried_on.shape[2:]
    take_halos(blocks, edges, halo_one, halo_two, halos, outer, edge_count)
    flow = flow_of(velocity, snaps[0, 1], 0)
    full_layer(halo_at(halos, 0), layer_of(edges, 0), layer_of(edges, 1), flow, shape, into(outer, 1))
    flow = flow_of(velocity, snaps[0, 1], depth - 1)
    full_layer(layer_of(edges, 2), layer_of(edges, 3), halo_at(halos, 1), flow, shape, into(outer, 2))

    def store(e, here, i, j, values):
        total[(e,) + spot(i, j)] = here(0, i, j) + values[0]

    last_steps(snaps, carried_on, outer, velocity, store, (0,))
    split_rows(total, pieces)


def finish_kernel(snaps, carried_on, outer, velocity, inner, out, final, sems):
    depth = carried_on.shape[1]

    def store(e, here, i, j, values):
        into(final, e)(i, j, values)

    last_steps(snaps, carried_on, outer, velocity, store, (0, 1))
    copies = [
        pltpu.make_async_copy(final.at[:, pl.ds(0, 2)], out.at[:, pl.ds(0, 2)], sems.at[0]),
        pltpu.make_async_copy(final.at[:, pl.ds(2, 2)], out.at[:, pl.ds(depth - 2, 2)], sems.at[1]),
    ]
    for copy in copies:
        copy.start()
    for copy in copies:
        copy.wait()


def sum_kernel(*refs):
    ins, out = refs[:-1], refs[-1]
    half = len(ins) // 2
    depth = out.shape[0]
    inner = functools.reduce(jnp.add, [ref[...] for ref in ins[:half]])
    outer = functools.reduce(jnp.add, [ref[...] for ref in ins[half:]])
    out[2 : depth - 2] = inner
    out[0:2] = outer[0:2]
    out[depth - 2 : depth] = outer[2:4]


def solution(mesh):
    slabs, blocks = mesh.shape["tm"], mesh.shape["space"]
    vmem, smem = pl.BlockSpec(memory_space=pltpu.VMEM), pl.BlockSpec(memory_space=pltpu.SMEM)
    hbm = pl.BlockSpec(memory_space=pltpu.HBM)
    sem = pltpu.SemaphoreType.DMA

    def params(mebibytes):
        return pltpu.CompilerParams(vmem_limit_bytes=mebibytes * 1024 * 1024)

    def cost(microseconds):
        return pl.CostEstimate(flops=0, bytes_accessed=int(microseconds * 3.6e6), transcendentals=0)

    def index(t, s):
        return (t % slabs) * blocks + s % blocks

    def moved(array, to):
        pairs = [(index(t, s), index(*to(t, s))) for t in range(slabs) for s in range(blocks)]
        return lax.ppermute(array, ("tm", "space"), pairs)

    def one(s):
        return s ^ 1

    def two(s):
        return (((s + 1) ^ 1) - 1) % blocks

    def body(slab_states, velocity, snap_of_step):
        start = slab_states[0]
        fields, depth, ny, nz = start.shape

        def shaped(*lead, rows=ny):
            return jax.ShapeDtypeStruct(lead + (rows, nz), jnp.float32)

        def room(*lead):
            return pltpu.VMEM(lead + (ny, nz), jnp.float32)

        layer = shaped(5)
        pieces = (shaped(4, rows=ny // slabs),) * slabs

        state = moved(start, lambda t, s: (t - 1, s))
        snaps_next = moved(snap_of_step, lambda t, s: (t - 1, s))
        message_one, message_two = pl.pallas_call(
            start_kernel,
            out_shape=(layer, layer),
            in_specs=[hbm] * 3,
            out_specs=(vmem, vmem),
            scratch_shapes=[
                pltpu.SMEM(snap_of_step.shape, jnp.int32),
                room(fields, edge_count),
                room(*velocity.shape[:2], 2),
                sem((5,)),
            ],
            compiler_params=params(56),
            cost_estimate=cost(2),
        )(snap_of_step, start, velocity)
        halo_one = moved(message_one, lambda t, s: (t - 1, one(s)))
        halo_two = moved(message_two, lambda t, s: (t - 1, two(s)))
        widened, edges, message_one, message_two = pl.pallas_call(
            functools.partial(first_kernel, blocks, slabs),
            out_shape=(shaped(fields, depth + 2), shaped(fields, edge_count), layer, layer),
            in_specs=[smem, smem] + [vmem] * 4 + [hbm],
            out_specs=(vmem,) * 4,
            scratch_shapes=[room(2, fields)],
            compiler_params=params(32),
            cost_estimate=cost(2.5),
        )(snap_of_step, snaps_next, state, halo_one, halo_two, velocity, start)
        halo_one = moved(message_one, lambda t, s: (t, one(s)))
        halo_two = moved(message_two, lambda t, s: (t, two(s)))
        carried_on, inner, *inner_pieces = pl.pallas_call(
            functools.partial(inner_kernel, slabs),
            out_shape=(shaped(fields, depth), shaped(fields, depth)) + pieces,
            in_specs=[smem, smem, vmem, vmem, vmem, hbm],
            out_specs=(vmem, hbm) + (vmem,) * slabs,
            scratch_shapes=[room(fields, depth), room(fields, depth - 4), room(depth - 4), sem(())],
            compiler_params=params(32),
            cost_estimate=cost(3),
        )(snap_of_step, snaps_next, widened, edges, velocity, start)
        inner_parts = inner_pieces[:1] + [
            moved(inner_pieces[by], lambda t, s, by=by: (t + by, s)) for by in range(1, slabs)
        ]
        outer, *outer_pieces = pl.pallas_call(
            functools.partial(outer_kernel, blocks, slabs),
            out_shape=(shaped(fields, edge_count),) + pieces,
            in_specs=[smem] + [vmem] * 5,
            out_specs=(vmem,) * (1 + slabs),
            scratch_shapes=[room(2, fields), room(edge_count)],
            compiler_params=params(32),
            cost_estimate=cost(1),
        )(snap_of_step, edges, halo_one, halo_two, carried_on, velocity)
        outer_parts = outer_pieces[:1] + [
            moved(outer_pieces[by], lambda t, s, by=by: (t + by, s)) for by in range(1, slabs)
        ]
        final = pl.pallas_call(
            finish_kernel,
            out_shape=shaped(fields, depth),
            in_specs=[smem, vmem, vmem, vmem, hbm],
            out_specs=hbm,
            scratch_shapes=[room(fields, edge_count), sem((2,))],
            input_output_aliases={4: 0},
            compiler_params=params(32),
            cost_estimate=cost(1),
        )(snap_of_step, carried_on, outer, velocity, inner)
        gradient = pl.pallas_call(
            sum_kernel,
            out_shape=shaped(depth, rows=ny // slabs),
            in_specs=[vmem] * (2 * slabs),
            out_specs=vmem,
            compiler_params=params(16),
            cost_estimate=cost(0.5),
        )(*inner_parts, *outer_parts)
        return (final[None], gradient)

    return jax.shard_map(
        body,
        mesh=mesh,
        in_specs=(P("tm", None, "space", None, None), P(None, None, "space", None, None), P("tm", None)),
        out_specs=(P("tm", None, "space", None, None), P("space", "tm", None)),
        check_vma=False,
    )
```

```python
import functools

import jax
import jax.numpy as jnp
from jax import lax
from jax.experimental import pallas as pl
from jax.experimental.pallas import tpu as pltpu
from jax.sharding import PartitionSpec as P

coupling = 0.3
diffusion = (0.14, 0.06)
sub, lanes = 8, 128
edge_count = 4


def tiles(shape):
    rows, cols = shape
    return [(i, j) for i in range(rows // sub) for j in range(cols // lanes)]


def spot(i, j):
    return (pl.ds(i * sub, sub), pl.ds(j * lanes, lanes))


def neighbours(at, i, j, shape):
    rows, cols = shape
    centre = at(i, j)
    row = lax.broadcasted_iota(jnp.int32, (sub, lanes), 0)
    col = lax.broadcasted_iota(jnp.int32, (sub, lanes), 1)
    zero = jnp.zeros_like(centre)
    after = at(i + 1, j) if (i + 1) * sub < rows else zero
    before = at(i - 1, j) if i > 0 else zero
    north = pltpu.roll(jnp.where(row == 0, after, centre), sub - 1, 0)
    south = pltpu.roll(jnp.where(row == sub - 1, before, centre), 1, 0)
    after = at(i, j + 1) if (j + 1) * lanes < cols else zero
    before = at(i, j - 1) if j > 0 else zero
    upper = pltpu.roll(jnp.where(col == 0, after, centre), lanes - 1, 1)
    lower = pltpu.roll(jnp.where(col == lanes - 1, before, centre), 1, 1)
    return centre, (north + south) + (upper + lower), north - south, upper - lower


def advanced(fields, pairs, flow, i, j, shape, wanted=(0, 1)):
    u, v, w = flow
    out = []
    for f in wanted:
        centre, total, dy, dz = neighbours(functools.partial(fields, f), i, j, shape)
        side_sum, side_diff = pairs(f, i, j)
        c = diffusion[f]
        moved = u * side_diff + v * dy + w * dz
        new = ((1.0 - 6.0 * c) * centre + c * (side_sum + total)) + 0.25 * moved
        if f == 0:
            new = new + coupling * fields(1, i, j)
        out.append(new)
    return out


def layer_of(ref, l):
    return lambda f, i, j: ref[(f, l) + spot(i, j)]


def flow_of(velocity, snap, l):
    return lambda i, j: [velocity[(snap, d, l) + spot(i, j)] for d in range(3)]


def full_layer(below, here, above, flow, shape, store, wanted=(0, 1)):
    def pairs(f, i, j):
        hi, lo = above(f, i, j), below(f, i, j)
        return hi + lo, hi - lo

    for i, j in tiles(shape):
        store(i, j, advanced(here, pairs, flow(i, j), i, j, shape, wanted))


def into(ref, l):
    def store(i, j, values):
        for f, value in enumerate(values):
            ref[(f, l) + spot(i, j)] = value

    return store


def sides(depth):
    parity = lax.rem(lax.axis_index("space"), 2)
    even = parity == 0
    high = (jnp.where(even, depth - 1, 0), jnp.where(even, depth - 2, 1), jnp.where(even, -1.0, 1.0))
    low = (jnp.where(even, 0, depth - 1), jnp.where(even, 1, depth - 2), jnp.where(even, 1.0, -1.0))
    return parity, high, low


def pack(edges, velocity, snap, message, layer, inner, sign):
    shape = edges.shape[2:]
    at = (layer // (edge_count - 1)) * (velocity.shape[2] - 1)
    near, here, flow = layer_of(edges, inner), layer_of(edges, layer), flow_of(velocity, snap, at)

    def pairs(f, i, j):
        value = near(f, i, j)
        return value, sign * value

    for i, j in tiles(shape):
        out = advanced(here, pairs, flow(i, j), i, j, shape)
        for f in (0, 1):
            message[(f,) + spot(i, j)] = here(f, i, j)
            message[(2 + f,) + spot(i, j)] = out[f]


def pack_both(edges, velocity, snap, message_one, message_two):
    unused, one, two = sides(edge_count)
    pack(edges, velocity, snap, message_one, *one)
    pack(edges, velocity, snap, message_two, *two)


def take_halos(blocks, state, halo_one, halo_two, own_flow, other_flow, snap, halos, after, depth):
    shape = state.shape[2:]
    parity, one, two = sides(depth)
    place = lax.axis_index("space")
    inside = jnp.logical_and(place > 0, place < blocks - 1)
    outer = after.shape[1] - 1
    fetched = lax.rem(lax.axis_index("tm"), 2)
    for halo, (edge, unused, sign), shown, high in (
        (halo_one, one, None, 1 - parity),
        (halo_two, two, inside, parity),
    ):
        for i, j in tiles(shape):
            u = jnp.where(high == fetched, own_flow[(snap,) + spot(i, j)], other_flow[(snap,) + spot(i, j)])
            for f in (0, 1):
                now = halo[(f,) + spot(i, j)]
                own = state[(f, edge) + spot(i, j)]
                later = halo[(2 + f,) + spot(i, j)] + (diffusion[f] + (0.25 * sign) * u) * own
                if shown is not None:
                    now = jnp.where(shown, now, 0.0)
                    later = jnp.where(shown, later, 0.0)
                halos[(high, f) + spot(i, j)] = now
                after[(f, high * outer) + spot(i, j)] = later


def halo_at(halos, h):
    return lambda f, i, j: halos[(h, f) + spot(i, j)]


def split_rows(total, pieces):
    rows = total.shape[1] // len(pieces)
    for by, piece in enumerate(pieces):
        start = pl.multiple_of(lax.rem(lax.axis_index("tm") + by, len(pieces)) * rows, rows)
        piece[...] = total[:, pl.ds(start, rows), :] * 0.5


def each(low, high, run):
    def step(l, carry):
        run(l)
        return carry

    lax.fori_loop(low, high, step, 0)


def start_kernel(snaps, state, velocity, message_one, message_two, flow_out, scalars, edges, flows, sems):
    depth = state.shape[1]
    copies = [
        (snaps, scalars),
        (state.at[:, pl.ds(0, 2)], edges.at[:, pl.ds(0, 2)]),
        (state.at[:, pl.ds(depth - 2, 2)], edges.at[:, pl.ds(2, 2)]),
        (velocity.at[:, :, pl.ds(0, 1)], flows.at[:, :, pl.ds(0, 1)]),
        (velocity.at[:, :, pl.ds(depth - 1, 1)], flows.at[:, :, pl.ds(1, 1)]),
    ]
    copies = [pltpu.make_async_copy(*pair, sems.at[n]) for n, pair in enumerate(copies)]
    for copy in copies:
        copy.start()
    for copy in copies:
        copy.wait()
    pack_both(edges, flows, scalars[0, 1], message_one, message_two)
    flow_out[...] = flows[:, 0, 1 - lax.rem(lax.axis_index("tm"), 2)]


def first_kernel(blocks, slabs, snaps, snaps_next, state, halo_one, halo_two, own_flow, other_flow, velocity, start,
                 widened, edges, message_one, message_two, halos):
    depth, shape = state.shape[1], state.shape[2:]
    last = lax.axis_index("tm") == slabs - 1

    @pl.when(last)
    def _():
        pltpu.sync_copy(start.at[:, pl.ds(0, 2)], edges.at[:, pl.ds(0, 2)])
        pltpu.sync_copy(start.at[:, pl.ds(depth - 2, 2)], edges.at[:, pl.ds(2, 2)])

    @pl.when(jnp.logical_not(last))
    def _():
        take_halos(
            blocks, state, halo_one, halo_two, own_flow, other_flow, snaps_next[0, 1], halos, widened, depth
        )

        def first_step(l, below, above):
            flow = flow_of(velocity, snaps_next[0, 1], l)
            full_layer(below, layer_of(state, l), above, flow, shape, into(widened, l + 1))

        first_step(0, halo_at(halos, 0), layer_of(state, 1))
        first_step(depth - 1, layer_of(state, depth - 2), halo_at(halos, 1))
        each(1, depth - 1, lambda l: first_step(l, layer_of(state, l - 1), layer_of(state, l + 1)))

        def second_step(e):
            l = e + (e // 2) * (depth - edge_count)
            flow = flow_of(velocity, snaps_next[0, 0], l)
            here = layer_of(widened, l + 1)
            full_layer(layer_of(widened, l), here, layer_of(widened, l + 2), flow, shape, into(edges, e))

        each(0, edge_count, second_step)

    pack_both(edges, velocity, snaps[0, 1], message_one, message_two)


def inner_kernel(slabs, snaps, snaps_next, widened, edges, velocity, start, carried_on, inner, *rest):
    pieces, (state, final, total, sem) = rest[:slabs], rest[slabs:]
    depth, shape = state.shape[1], state.shape[2:]
    last = lax.axis_index("tm") == slabs - 1

    @pl.when(last)
    def _():
        pltpu.sync_copy(start, state)

    @pl.when(jnp.logical_not(last))
    def _():
        def second_step(l):
            flow = flow_of(velocity, snaps_next[0, 0], l)
            here = layer_of(widened, l + 1)
            full_layer(layer_of(widened, l), here, layer_of(widened, l + 2), flow, shape, into(state, l))

        each(2, depth - 2, second_step)
        state[:, 0:2] = edges[:, 0:2]
        state[:, depth - 2 : depth] = edges[:, 2:4]

    def third_step(l):
        flow = flow_of(velocity, snaps[0, 1], l)
        here = layer_of(state, l)
        full_layer(layer_of(state, l - 1), here, layer_of(state, l + 1), flow, shape, into(carried_on, l))

    each(1, depth - 1, third_step)

    def fourth_step(l):
        def store(i, j, values):
            into(final, l - 2)(i, j, values)
            total[(l - 2,) + spot(i, j)] = carried_on[(0, l) + spot(i, j)] + values[0]

        flow = flow_of(velocity, snaps[0, 0], l)
        here = layer_of(carried_on, l)
        full_layer(layer_of(carried_on, l - 1), here, layer_of(carried_on, l + 1), flow, shape, store)

    each(2, depth - 2, fourth_step)
    copy = pltpu.make_async_copy(final, inner.at[:, pl.ds(2, depth - 4)], sem)
    copy.start()
    split_rows(total, pieces)
    copy.wait()


def last_steps(snaps, carried_on, outer, velocity, store, wanted):
    depth, shape = carried_on.shape[1], carried_on.shape[2:]
    ring = [layer_of(outer, 0), layer_of(outer, 1), layer_of(carried_on, 1), layer_of(carried_on, 2)]
    ring += [layer_of(carried_on, depth - 3), layer_of(carried_on, depth - 2), layer_of(outer, 2), layer_of(outer, 3)]
    for e, at in enumerate((1, 2, 5, 6)):
        l = e + (e // 2) * (depth - edge_count)
        flow = flow_of(velocity, snaps[0, 0], l)
        full_layer(ring[at - 1], ring[at], ring[at + 1], flow, shape, functools.partial(store, e, ring[at]), wanted)


def outer_kernel(blocks, slabs, snaps, edges, halo_one, halo_two, own_flow, other_flow, carried_on, velocity,
                 outer, *rest):
    pieces, (halos, total) = rest[:slabs], rest[slabs:]
    depth, shape = carried_on.shape[1], carried_on.shape[2:]
    take_halos(
        blocks, edges, halo_one, halo_two, own_flow, other_flow, snaps[0, 1], halos, outer, edge_count
    )
    flow = flow_of(velocity, snaps[0, 1], 0)
    full_layer(halo_at(halos, 0), layer_of(edges, 0), layer_of(edges, 1), flow, shape, into(outer, 1))
    flow = flow_of(velocity, snaps[0, 1], depth - 1)
    full_layer(layer_of(edges, 2), layer_of(edges, 3), halo_at(halos, 1), flow, shape, into(outer, 2))

    def store(e, here, i, j, values):
        total[(e,) + spot(i, j)] = here(0, i, j) + values[0]

    last_steps(snaps, carried_on, outer, velocity, store, (0,))
    split_rows(total, pieces)


def finish_kernel(snaps, carried_on, outer, velocity, inner, out, final, sems):
    depth = carried_on.shape[1]

    def store(e, here, i, j, values):
        into(final, e)(i, j, values)

    last_steps(snaps, carried_on, outer, velocity, store, (0, 1))
    copies = [
        pltpu.make_async_copy(final.at[:, pl.ds(0, 2)], out.at[:, pl.ds(0, 2)], sems.at[0]),
        pltpu.make_async_copy(final.at[:, pl.ds(2, 2)], out.at[:, pl.ds(depth - 2, 2)], sems.at[1]),
    ]
    for copy in copies:
        copy.start()
    for copy in copies:
        copy.wait()


def sum_kernel(*refs):
    ins, out = refs[:-1], refs[-1]
    half = len(ins) // 2
    depth = out.shape[0]
    inner = functools.reduce(jnp.add, [ref[...] for ref in ins[:half]])
    outer = functools.reduce(jnp.add, [ref[...] for ref in ins[half:]])
    out[2 : depth - 2] = inner
    out[0:2] = outer[0:2]
    out[depth - 2 : depth] = outer[2:4]


def solution(mesh):
    slabs, blocks = mesh.shape["tm"], mesh.shape["space"]
    vmem, smem = pl.BlockSpec(memory_space=pltpu.VMEM), pl.BlockSpec(memory_space=pltpu.SMEM)
    hbm = pl.BlockSpec(memory_space=pltpu.HBM)
    sem = pltpu.SemaphoreType.DMA

    def params(mebibytes):
        return pltpu.CompilerParams(vmem_limit_bytes=mebibytes * 1024 * 1024)

    def cost(microseconds):
        return pl.CostEstimate(flops=0, bytes_accessed=int(microseconds * 3.6e6), transcendentals=0)

    def index(t, s):
        return (t % slabs) * blocks + s % blocks

    def moved(array, to):
        pairs = [(index(t, s), index(*to(t, s))) for t in range(slabs) for s in range(blocks)]
        return lax.ppermute(array, ("tm", "space"), pairs)

    def one(s):
        return s ^ 1

    def two(s):
        return (((s + 1) ^ 1) - 1) % blocks

    def body(slab_states, velocity, snap_of_step):
        start = slab_states[0]
        fields, depth, ny, nz = start.shape

        def shaped(*lead, rows=ny):
            return jax.ShapeDtypeStruct(lead + (rows, nz), jnp.float32)

        def room(*lead):
            return pltpu.VMEM(lead + (ny, nz), jnp.float32)

        layer = shaped(4)
        pieces = (shaped(4, rows=ny // slabs),) * slabs

        state = moved(start, lambda t, s: (t - 1, s))
        snaps_next = moved(snap_of_step, lambda t, s: (t - 1, s))
        message_one, message_two, flow_out = pl.pallas_call(
            start_kernel,
            out_shape=(layer, layer, shaped(velocity.shape[0])),
            in_specs=[hbm] * 3,
            out_specs=(vmem,) * 3,
            scratch_shapes=[
                pltpu.SMEM(snap_of_step.shape, jnp.int32),
                room(fields, edge_count),
                room(*velocity.shape[:2], 2),
                sem((5,)),
            ],
            compiler_params=params(56),
            cost_estimate=cost(2),
        )(snap_of_step, start, velocity)
        halo_one = moved(message_one, lambda t, s: (t - 1, one(s)))
        halo_two = moved(message_two, lambda t, s: (t - 1, two(s)))
        own_flow = moved(flow_out, lambda t, s: (t ^ 2, s + 1 - 2 * (t % 2)))
        other_flow = moved(own_flow, lambda t, s: (t ^ 1, s))
        widened, edges, message_one, message_two = pl.pallas_call(
            functools.partial(first_kernel, blocks, slabs),
            out_shape=(shaped(fields, depth + 2), shaped(fields, edge_count), layer, layer),
            in_specs=[smem, smem] + [vmem] * 6 + [hbm],
            out_specs=(vmem,) * 4,
            scratch_shapes=[room(2, fields)],
            compiler_params=params(32),
            cost_estimate=cost(2.5),
        )(snap_of_step, snaps_next, state, halo_one, halo_two, own_flow, other_flow, velocity, start)
        halo_one = moved(message_one, lambda t, s: (t, one(s)))
        halo_two = moved(message_two, lambda t, s: (t, two(s)))
        carried_on, inner, *inner_pieces = pl.pallas_call(
            functools.partial(inner_kernel, slabs),
            out_shape=(shaped(fields, depth), shaped(fields, depth)) + pieces,
            in_specs=[smem, smem, vmem, vmem, vmem, hbm],
            out_specs=(vmem, hbm) + (vmem,) * slabs,
            scratch_shapes=[room(fields, depth), room(fields, depth - 4), room(depth - 4), sem(())],
            compiler_params=params(32),
            cost_estimate=cost(3),
        )(snap_of_step, snaps_next, widened, edges, velocity, start)
        inner_parts = inner_pieces[:1] + [
            moved(inner_pieces[by], lambda t, s, by=by: (t + by, s)) for by in range(1, slabs)
        ]
        outer, *outer_pieces = pl.pallas_call(
            functools.partial(outer_kernel, blocks, slabs),
            out_shape=(shaped(fields, edge_count),) + pieces,
            in_specs=[smem] + [vmem] * 7,
            out_specs=(vmem,) * (1 + slabs),
            scratch_shapes=[room(2, fields), room(edge_count)],
            compiler_params=params(32),
            cost_estimate=cost(1),
        )(snap_of_step, edges, halo_one, halo_two, own_flow, other_flow, carried_on, velocity)
        outer_parts = outer_pieces[:1] + [
            moved(outer_pieces[by], lambda t, s, by=by: (t + by, s)) for by in range(1, slabs)
        ]
        final = pl.pallas_call(
            finish_kernel,
            out_shape=shaped(fields, depth),
            in_specs=[smem, vmem, vmem, vmem, hbm],
            out_specs=hbm,
            scratch_shapes=[room(fields, edge_count), sem((2,))],
            input_output_aliases={4: 0},
            compiler_params=params(32),
            cost_estimate=cost(1),
        )(snap_of_step, carried_on, outer, velocity, inner)
        gradient = pl.pallas_call(
            sum_kernel,
            out_shape=shaped(depth, rows=ny // slabs),
            in_specs=[vmem] * (2 * slabs),
            out_specs=vmem,
            compiler_params=params(16),
            cost_estimate=cost(0.5),
        )(*inner_parts, *outer_parts)
        return (final[None], gradient)

    return jax.shard_map(
        body,
        mesh=mesh,
        in_specs=(P("tm", None, "space", None, None), P(None, None, "space", None, None), P("tm", None)),
        out_specs=(P("tm", None, "space", None, None), P("space", "tm", None)),
        check_vma=False,
    )
```

```python
import functools

import jax
import jax.numpy as jnp
from jax import lax
from jax.experimental import pallas as pl
from jax.experimental.pallas import tpu as pltpu
from jax.sharding import PartitionSpec as P

coupling = 0.3
diffusion = (0.14, 0.06)
sub, lanes = 8, 128
edge_count = 4


def tiles(shape):
    rows, cols = shape
    return [(i, j) for i in range(rows // sub) for j in range(cols // lanes)]


def spot(i, j):
    return (pl.ds(i * sub, sub), pl.ds(j * lanes, lanes))


def neighbours(at, i, j, shape):
    rows, cols = shape
    centre = at(i, j)
    row = lax.broadcasted_iota(jnp.int32, (sub, lanes), 0)
    col = lax.broadcasted_iota(jnp.int32, (sub, lanes), 1)
    zero = jnp.zeros_like(centre)
    after = at(i + 1, j) if (i + 1) * sub < rows else zero
    before = at(i - 1, j) if i > 0 else zero
    north = pltpu.roll(jnp.where(row == 0, after, centre), sub - 1, 0)
    south = pltpu.roll(jnp.where(row == sub - 1, before, centre), 1, 0)
    after = at(i, j + 1) if (j + 1) * lanes < cols else zero
    before = at(i, j - 1) if j > 0 else zero
    upper = pltpu.roll(jnp.where(col == 0, after, centre), lanes - 1, 1)
    lower = pltpu.roll(jnp.where(col == lanes - 1, before, centre), 1, 1)
    return centre, (north + south) + (upper + lower), north - south, upper - lower


def advanced(fields, pairs, flow, i, j, shape, wanted=(0, 1)):
    u, v, w = flow
    out = []
    for f in wanted:
        centre, total, dy, dz = neighbours(functools.partial(fields, f), i, j, shape)
        side_sum, side_diff = pairs(f, i, j)
        c = diffusion[f]
        moved = u * side_diff + v * dy + w * dz
        new = ((1.0 - 6.0 * c) * centre + c * (side_sum + total)) + 0.25 * moved
        if f == 0:
            new = new + coupling * fields(1, i, j)
        out.append(new)
    return out


def layer_of(ref, l):
    return lambda f, i, j: ref[(f, l) + spot(i, j)]


def flow_of(velocity, snap, l):
    return lambda i, j: [velocity[(snap, d, l) + spot(i, j)] for d in range(3)]


def full_layer(below, here, above, flow, shape, store, wanted=(0, 1)):
    def pairs(f, i, j):
        hi, lo = above(f, i, j), below(f, i, j)
        return hi + lo, hi - lo

    for i, j in tiles(shape):
        store(i, j, advanced(here, pairs, flow(i, j), i, j, shape, wanted))


def into(ref, l):
    def store(i, j, values):
        for f, value in enumerate(values):
            ref[(f, l) + spot(i, j)] = value

    return store


def sides(depth):
    parity = lax.rem(lax.axis_index("space"), 2)
    even = parity == 0
    high = (jnp.where(even, depth - 1, 0), jnp.where(even, depth - 2, 1), jnp.where(even, -1.0, 1.0))
    low = (jnp.where(even, 0, depth - 1), jnp.where(even, 1, depth - 2), jnp.where(even, 1.0, -1.0))
    return parity, high, low


def pack(edges, velocity, snap, message, layer, inner, sign):
    shape = edges.shape[2:]
    at = (layer // (edge_count - 1)) * (velocity.shape[2] - 1)
    near, here, flow = layer_of(edges, inner), layer_of(edges, layer), flow_of(velocity, snap, at)

    def pairs(f, i, j):
        value = near(f, i, j)
        return value, sign * value

    for i, j in tiles(shape):
        out = advanced(here, pairs, flow(i, j), i, j, shape)
        for f in (0, 1):
            message[(f,) + spot(i, j)] = here(f, i, j)
            message[(2 + f,) + spot(i, j)] = out[f]


def pack_both(edges, velocity, snap, message_one, message_two):
    unused, one, two = sides(edge_count)
    pack(edges, velocity, snap, message_one, *one)
    pack(edges, velocity, snap, message_two, *two)


def take_halos(blocks, state, halo_one, halo_two, own_flow, other_flow, snap, halos, after, depth):
    shape = state.shape[2:]
    parity, one, two = sides(depth)
    place = lax.axis_index("space")
    inside = jnp.logical_and(place > 0, place < blocks - 1)
    outer = after.shape[1] - 1
    fetched = lax.rem(lax.axis_index("tm"), 2)
    for halo, (edge, unused, sign), shown, high in (
        (halo_one, one, None, 1 - parity),
        (halo_two, two, inside, parity),
    ):
        for i, j in tiles(shape):
            u = jnp.where(high == fetched, own_flow[(snap,) + spot(i, j)], other_flow[(snap,) + spot(i, j)])
            for f in (0, 1):
                now = halo[(f,) + spot(i, j)]
                own = state[(f, edge) + spot(i, j)]
                later = halo[(2 + f,) + spot(i, j)] + (diffusion[f] + (0.25 * sign) * u) * own
                if shown is not None:
                    now = jnp.where(shown, now, 0.0)
                    later = jnp.where(shown, later, 0.0)
                halos[(high, f) + spot(i, j)] = now
                after[(f, high * outer) + spot(i, j)] = later


def halo_at(halos, h):
    return lambda f, i, j: halos[(h, f) + spot(i, j)]


def split_rows(total, pieces):
    rows = total.shape[1] // len(pieces)
    for by, piece in enumerate(pieces):
        start = pl.multiple_of(lax.rem(lax.axis_index("tm") + by, len(pieces)) * rows, rows)
        piece[...] = total[:, pl.ds(start, rows), :] * 0.5


def each(low, high, run):
    def step(l, carry):
        run(l)
        return carry

    lax.fori_loop(low, high, step, 0)


def start_kernel(snaps, state, velocity, message_one, message_two, flow_out, scalars, edges, flows, sems):
    depth = state.shape[1]
    copies = [
        (snaps, scalars),
        (state.at[:, pl.ds(0, 2)], edges.at[:, pl.ds(0, 2)]),
        (state.at[:, pl.ds(depth - 2, 2)], edges.at[:, pl.ds(2, 2)]),
        (velocity.at[:, :, pl.ds(0, 1)], flows.at[:, :, pl.ds(0, 1)]),
        (velocity.at[:, :, pl.ds(depth - 1, 1)], flows.at[:, :, pl.ds(1, 1)]),
    ]
    copies = [pltpu.make_async_copy(*pair, sems.at[n]) for n, pair in enumerate(copies)]
    for copy in copies:
        copy.start()
    for copy in copies:
        copy.wait()
    pack_both(edges, flows, scalars[0, 1], message_one, message_two)
    flow_out[...] = flows[:, 0, 1 - lax.rem(lax.axis_index("tm"), 2)]


def first_kernel(blocks, slabs, snaps, snaps_next, state, halo_one, halo_two, own_flow, other_flow, velocity, start,
                 widened, edges, message_one, message_two, halos):
    depth, shape = state.shape[1], state.shape[2:]
    last = lax.axis_index("tm") == slabs - 1

    @pl.when(last)
    def _():
        pltpu.sync_copy(start.at[:, pl.ds(0, 2)], edges.at[:, pl.ds(0, 2)])
        pltpu.sync_copy(start.at[:, pl.ds(depth - 2, 2)], edges.at[:, pl.ds(2, 2)])

    @pl.when(jnp.logical_not(last))
    def _():
        take_halos(
            blocks, state, halo_one, halo_two, own_flow, other_flow, snaps_next[0, 1], halos, widened, depth
        )

        def first_step(l, below, above):
            flow = flow_of(velocity, snaps_next[0, 1], l)
            full_layer(below, layer_of(state, l), above, flow, shape, into(widened, l + 1))

        first_step(0, halo_at(halos, 0), layer_of(state, 1))
        first_step(depth - 1, layer_of(state, depth - 2), halo_at(halos, 1))
        each(1, depth - 1, lambda l: first_step(l, layer_of(state, l - 1), layer_of(state, l + 1)))

        def second_step(e):
            l = e + (e // 2) * (depth - edge_count)
            flow = flow_of(velocity, snaps_next[0, 0], l)
            here = layer_of(widened, l + 1)
            full_layer(layer_of(widened, l), here, layer_of(widened, l + 2), flow, shape, into(edges, e))

        each(0, edge_count, second_step)

    pack_both(edges, velocity, snaps[0, 1], message_one, message_two)


def inner_kernel(slabs, snaps, snaps_next, widened, edges, velocity, start, carried_on, inner, *rest):
    pieces, (state, final, total, sem) = rest[:slabs], rest[slabs:]
    depth, shape = state.shape[1], state.shape[2:]
    last = lax.axis_index("tm") == slabs - 1

    @pl.when(last)
    def _():
        pltpu.sync_copy(start, state)

    @pl.when(jnp.logical_not(last))
    def _():
        def second_step(l):
            flow = flow_of(velocity, snaps_next[0, 0], l)
            here = layer_of(widened, l + 1)
            full_layer(layer_of(widened, l), here, layer_of(widened, l + 2), flow, shape, into(state, l))

        each(2, depth - 2, second_step)
        state[:, 0:2] = edges[:, 0:2]
        state[:, depth - 2 : depth] = edges[:, 2:4]

    def third_step(l):
        flow = flow_of(velocity, snaps[0, 1], l)
        here = layer_of(state, l)
        full_layer(layer_of(state, l - 1), here, layer_of(state, l + 1), flow, shape, into(carried_on, l))

    each(1, depth - 1, third_step)

    def fourth_step(l):
        def store(i, j, values):
            into(final, l - 2)(i, j, values)
            total[(l - 2,) + spot(i, j)] = carried_on[(0, l) + spot(i, j)] + values[0]

        flow = flow_of(velocity, snaps[0, 0], l)
        here = layer_of(carried_on, l)
        full_layer(layer_of(carried_on, l - 1), here, layer_of(carried_on, l + 1), flow, shape, store)

    each(2, depth - 2, fourth_step)
    copy = pltpu.make_async_copy(final, inner.at[:, pl.ds(2, depth - 4)], sem)
    copy.start()
    split_rows(total, pieces)
    copy.wait()


def last_steps(snaps, carried_on, outer, velocity, store, wanted):
    depth, shape = carried_on.shape[1], carried_on.shape[2:]
    ring = [layer_of(outer, 0), layer_of(outer, 1), layer_of(carried_on, 1), layer_of(carried_on, 2)]
    ring += [layer_of(carried_on, depth - 3), layer_of(carried_on, depth - 2), layer_of(outer, 2), layer_of(outer, 3)]
    for e, at in enumerate((1, 2, 5, 6)):
        l = e + (e // 2) * (depth - edge_count)
        flow = flow_of(velocity, snaps[0, 0], l)
        full_layer(ring[at - 1], ring[at], ring[at + 1], flow, shape, functools.partial(store, e, ring[at]), wanted)


def outer_kernel(blocks, slabs, snaps, edges, halo_one, halo_two, own_flow, other_flow, carried_on, velocity,
                 outer, *rest):
    pieces, (halos, total) = rest[:slabs], rest[slabs:]
    depth, shape = carried_on.shape[1], carried_on.shape[2:]
    take_halos(
        blocks, edges, halo_one, halo_two, own_flow, other_flow, snaps[0, 1], halos, outer, edge_count
    )
    flow = flow_of(velocity, snaps[0, 1], 0)
    full_layer(halo_at(halos, 0), layer_of(edges, 0), layer_of(edges, 1), flow, shape, into(outer, 1))
    flow = flow_of(velocity, snaps[0, 1], depth - 1)
    full_layer(layer_of(edges, 2), layer_of(edges, 3), halo_at(halos, 1), flow, shape, into(outer, 2))

    def store(e, here, i, j, values):
        total[(e,) + spot(i, j)] = here(0, i, j) + values[0]

    last_steps(snaps, carried_on, outer, velocity, store, (0,))
    split_rows(total, pieces)


def finish_kernel(snaps, carried_on, outer, velocity, inner, out, final, sems):
    depth = carried_on.shape[1]

    def store(e, here, i, j, values):
        into(final, e)(i, j, values)

    last_steps(snaps, carried_on, outer, velocity, store, (0, 1))
    copies = [
        pltpu.make_async_copy(final.at[:, pl.ds(0, 2)], out.at[:, pl.ds(0, 2)], sems.at[0]),
        pltpu.make_async_copy(final.at[:, pl.ds(2, 2)], out.at[:, pl.ds(depth - 2, 2)], sems.at[1]),
    ]
    for copy in copies:
        copy.start()
    for copy in copies:
        copy.wait()


def sum_kernel(*refs):
    ins, out = refs[:-1], refs[-1]
    half = len(ins) // 2
    depth = out.shape[0]
    inner = functools.reduce(jnp.add, [ref[...] for ref in ins[:half]])
    outer = functools.reduce(jnp.add, [ref[...] for ref in ins[half:]])
    out[2 : depth - 2] = inner
    out[0:2] = outer[0:2]
    out[depth - 2 : depth] = outer[2:4]


def solution(mesh):
    slabs, blocks = mesh.shape["tm"], mesh.shape["space"]
    vmem, smem = pl.BlockSpec(memory_space=pltpu.VMEM), pl.BlockSpec(memory_space=pltpu.SMEM)
    hbm = pl.BlockSpec(memory_space=pltpu.HBM)
    sem = pltpu.SemaphoreType.DMA

    def params(mebibytes):
        return pltpu.CompilerParams(vmem_limit_bytes=mebibytes * 1024 * 1024)

    def cost(microseconds):
        return pl.CostEstimate(flops=0, bytes_accessed=int(microseconds * 3.6e6), transcendentals=0)

    def index(t, s):
        return (t % slabs) * blocks + s % blocks

    def moved(array, to):
        pairs = [(index(t, s), index(*to(t, s))) for t in range(slabs) for s in range(blocks)]
        return lax.ppermute(array, ("tm", "space"), pairs)

    def exchanged(array, by, earlier):
        def to(t, s):
            partner = ((s + by) ^ 1) - by
            return (t - earlier, partner) if 0 <= partner < blocks else (t ^ 1, s)

        return moved(array, to)

    def fetched(t, s):
        source = s + 1 - 2 * (t % 2)
        return (t ^ 2, source) if 0 <= source < blocks else (t ^ 1, s)

    def body(slab_states, velocity, snap_of_step):
        start = slab_states[0]
        fields, depth, ny, nz = start.shape

        def shaped(*lead, rows=ny):
            return jax.ShapeDtypeStruct(lead + (rows, nz), jnp.float32)

        def room(*lead):
            return pltpu.VMEM(lead + (ny, nz), jnp.float32)

        layer = shaped(4)
        pieces = (shaped(4, rows=ny // slabs),) * slabs

        state = moved(start, lambda t, s: (t - 1, s))
        snaps_next = moved(snap_of_step, lambda t, s: (t - 1, s))
        message_one, message_two, flow_out = pl.pallas_call(
            start_kernel,
            out_shape=(layer, layer, shaped(velocity.shape[0])),
            in_specs=[hbm] * 3,
            out_specs=(vmem,) * 3,
            scratch_shapes=[
                pltpu.SMEM(snap_of_step.shape, jnp.int32),
                room(fields, edge_count),
                room(*velocity.shape[:2], 2),
                sem((5,)),
            ],
            compiler_params=params(56),
            cost_estimate=cost(2),
        )(snap_of_step, start, velocity)
        halo_one = exchanged(message_one, 0, 1)
        halo_two = exchanged(message_two, 1, 1)
        own_flow = moved(flow_out, fetched)
        other_flow = moved(own_flow, lambda t, s: (t ^ 1, s))
        widened, edges, message_one, message_two = pl.pallas_call(
            functools.partial(first_kernel, blocks, slabs),
            out_shape=(shaped(fields, depth + 2), shaped(fields, edge_count), layer, layer),
            in_specs=[smem, smem] + [vmem] * 6 + [hbm],
            out_specs=(vmem,) * 4,
            scratch_shapes=[room(2, fields)],
            compiler_params=params(32),
            cost_estimate=cost(2.5),
        )(snap_of_step, snaps_next, state, halo_one, halo_two, own_flow, other_flow, velocity, start)
        halo_one = exchanged(message_one, 0, 0)
        halo_two = exchanged(message_two, 1, 0)
        carried_on, inner, *inner_pieces = pl.pallas_call(
            functools.partial(inner_kernel, slabs),
            out_shape=(shaped(fields, depth), shaped(fields, depth)) + pieces,
            in_specs=[smem, smem, vmem, vmem, vmem, hbm],
            out_specs=(vmem, hbm) + (vmem,) * slabs,
            scratch_shapes=[room(fields, depth), room(fields, depth - 4), room(depth - 4), sem(())],
            compiler_params=params(32),
            cost_estimate=cost(3),
        )(snap_of_step, snaps_next, widened, edges, velocity, start)
        inner_parts = inner_pieces[:1] + [
            moved(inner_pieces[by], lambda t, s, by=by: (t + by, s)) for by in range(1, slabs)
        ]
        outer, *outer_pieces = pl.pallas_call(
            functools.partial(outer_kernel, blocks, slabs),
            out_shape=(shaped(fields, edge_count),) + pieces,
            in_specs=[smem] + [vmem] * 7,
            out_specs=(vmem,) * (1 + slabs),
            scratch_shapes=[room(2, fields), room(edge_count)],
            compiler_params=params(32),
            cost_estimate=cost(1),
        )(snap_of_step, edges, halo_one, halo_two, own_flow, other_flow, carried_on, velocity)
        outer_parts = outer_pieces[:1] + [
            moved(outer_pieces[by], lambda t, s, by=by: (t + by, s)) for by in range(1, slabs)
        ]
        final = pl.pallas_call(
            finish_kernel,
            out_shape=shaped(fields, depth),
            in_specs=[smem, vmem, vmem, vmem, hbm],
            out_specs=hbm,
            scratch_shapes=[room(fields, edge_count), sem((2,))],
            input_output_aliases={4: 0},
            compiler_params=params(32),
            cost_estimate=cost(1),
        )(snap_of_step, carried_on, outer, velocity, inner)
        gradient = pl.pallas_call(
            sum_kernel,
            out_shape=shaped(depth, rows=ny // slabs),
            in_specs=[vmem] * (2 * slabs),
            out_specs=vmem,
            compiler_params=params(16),
            cost_estimate=cost(0.5),
        )(*inner_parts, *outer_parts)
        return (final[None], gradient)

    return jax.shard_map(
        body,
        mesh=mesh,
        in_specs=(P("tm", None, "space", None, None), P(None, None, "space", None, None), P("tm", None)),
        out_specs=(P("tm", None, "space", None, None), P("space", "tm", None)),
        check_vma=False,
    )
```

```python
import functools

import jax
import jax.numpy as jnp
from jax import lax
from jax.experimental import pallas as pl
from jax.experimental.pallas import tpu as pltpu
from jax.sharding import PartitionSpec as P

coupling = 0.3
diffusion = (0.14, 0.06)
sub, lanes = 8, 128
edge_count = 4


def tiles(shape):
    rows, cols = shape
    return [(i, j) for i in range(rows // sub) for j in range(cols // lanes)]


def spot(i, j):
    return (pl.ds(i * sub, sub), pl.ds(j * lanes, lanes))


def neighbours(at, i, j, shape):
    rows, cols = shape
    centre = at(i, j)
    row = lax.broadcasted_iota(jnp.int32, (sub, lanes), 0)
    col = lax.broadcasted_iota(jnp.int32, (sub, lanes), 1)
    zero = jnp.zeros_like(centre)
    after = at(i + 1, j) if (i + 1) * sub < rows else zero
    before = at(i - 1, j) if i > 0 else zero
    north = pltpu.roll(jnp.where(row == 0, after, centre), sub - 1, 0)
    south = pltpu.roll(jnp.where(row == sub - 1, before, centre), 1, 0)
    after = at(i, j + 1) if (j + 1) * lanes < cols else zero
    before = at(i, j - 1) if j > 0 else zero
    upper = pltpu.roll(jnp.where(col == 0, after, centre), lanes - 1, 1)
    lower = pltpu.roll(jnp.where(col == lanes - 1, before, centre), 1, 1)
    return centre, (north + south) + (upper + lower), north - south, upper - lower


def advanced(fields, pairs, flow, i, j, shape, wanted=(0, 1)):
    u, v, w = flow
    out = []
    for f in wanted:
        centre, total, dy, dz = neighbours(functools.partial(fields, f), i, j, shape)
        side_sum, side_diff = pairs(f, i, j)
        c = diffusion[f]
        moved = u * side_diff + v * dy + w * dz
        new = ((1.0 - 6.0 * c) * centre + c * (side_sum + total)) + 0.25 * moved
        if f == 0:
            new = new + coupling * fields(1, i, j)
        out.append(new)
    return out


def layer_of(ref, l):
    return lambda f, i, j: ref[(f, l) + spot(i, j)]


def flow_of(velocity, snap, l):
    return lambda i, j: [velocity[(snap, d, l) + spot(i, j)] for d in range(3)]


def full_layer(below, here, above, flow, shape, store, wanted=(0, 1)):
    def pairs(f, i, j):
        hi, lo = above(f, i, j), below(f, i, j)
        return hi + lo, hi - lo

    for i, j in tiles(shape):
        store(i, j, advanced(here, pairs, flow(i, j), i, j, shape, wanted))


def into(ref, l):
    def store(i, j, values):
        for f, value in enumerate(values):
            ref[(f, l) + spot(i, j)] = value

    return store


def sides(depth):
    parity = lax.rem(lax.axis_index("space"), 2)
    even = parity == 0
    high = (jnp.where(even, depth - 1, 0), jnp.where(even, depth - 2, 1), jnp.where(even, -1.0, 1.0))
    low = (jnp.where(even, 0, depth - 1), jnp.where(even, 1, depth - 2), jnp.where(even, 1.0, -1.0))
    return parity, high, low


def pack(edges, velocity, snap, message, layer, inner, sign):
    shape = edges.shape[2:]
    at = (layer // (edge_count - 1)) * (velocity.shape[2] - 1)
    near, here, flow = layer_of(edges, inner), layer_of(edges, layer), flow_of(velocity, snap, at)

    def pairs(f, i, j):
        value = near(f, i, j)
        return value, sign * value

    for i, j in tiles(shape):
        out = advanced(here, pairs, flow(i, j), i, j, shape)
        for f in (0, 1):
            message[(f,) + spot(i, j)] = here(f, i, j)
            message[(2 + f,) + spot(i, j)] = out[f]


def pack_both(edges, velocity, snap, message_one, message_two):
    unused, one, two = sides(edge_count)
    pack(edges, velocity, snap, message_one, *one)
    pack(edges, velocity, snap, message_two, *two)


def take_halos(blocks, state, halo_one, halo_two, own_flow, other_flow, snap, halos, after, depth):
    shape = state.shape[2:]
    parity, one, two = sides(depth)
    place = lax.axis_index("space")
    inside = jnp.logical_and(place > 0, place < blocks - 1)
    outer = after.shape[1] - 1
    fetched = lax.rem(lax.axis_index("tm"), 2)
    for halo, (edge, unused, sign), shown, high in (
        (halo_one, one, None, 1 - parity),
        (halo_two, two, inside, parity),
    ):
        for i, j in tiles(shape):
            u = jnp.where(high == fetched, own_flow[(snap,) + spot(i, j)], other_flow[(snap,) + spot(i, j)])
            for f in (0, 1):
                now = halo[(f,) + spot(i, j)]
                own = state[(f, edge) + spot(i, j)]
                later = halo[(2 + f,) + spot(i, j)] + (diffusion[f] + (0.25 * sign) * u) * own
                if shown is not None:
                    now = jnp.where(shown, now, 0.0)
                    later = jnp.where(shown, later, 0.0)
                halos[(high, f) + spot(i, j)] = now
                after[(f, high * outer) + spot(i, j)] = later


def halo_at(halos, h):
    return lambda f, i, j: halos[(h, f) + spot(i, j)]


def split_rows(total, pieces):
    rows = total.shape[1] // len(pieces)
    for by, piece in enumerate(pieces):
        start = pl.multiple_of(lax.bitwise_xor(lax.axis_index("tm"), by) * rows, rows)
        piece[...] = total[:, pl.ds(start, rows), :] * 0.5


def each(low, high, run):
    def step(l, carry):
        run(l)
        return carry

    lax.fori_loop(low, high, step, 0)


def start_kernel(snaps, state, velocity, message_one, message_two, flow_out, scalars, edges, flows, sems):
    depth = state.shape[1]
    copies = [
        (snaps, scalars),
        (state.at[:, pl.ds(0, 2)], edges.at[:, pl.ds(0, 2)]),
        (state.at[:, pl.ds(depth - 2, 2)], edges.at[:, pl.ds(2, 2)]),
        (velocity.at[:, :, pl.ds(0, 1)], flows.at[:, :, pl.ds(0, 1)]),
        (velocity.at[:, :, pl.ds(depth - 1, 1)], flows.at[:, :, pl.ds(1, 1)]),
    ]
    copies = [pltpu.make_async_copy(*pair, sems.at[n]) for n, pair in enumerate(copies)]
    for copy in copies:
        copy.start()
    for copy in copies:
        copy.wait()
    pack_both(edges, flows, scalars[0, 1], message_one, message_two)
    flow_out[...] = flows[:, 0, 1 - lax.rem(lax.axis_index("tm"), 2)]


def first_kernel(blocks, slabs, snaps, snaps_next, state, halo_one, halo_two, own_flow, other_flow, velocity,
                 widened, edges, message_one, message_two, halos):
    depth, shape = state.shape[1], state.shape[2:]

    @pl.when(lax.axis_index("tm") < slabs - 1)
    def _():
        take_halos(
            blocks, state, halo_one, halo_two, own_flow, other_flow, snaps_next[0, 1], halos, widened, depth
        )

        def first_step(l, below, above):
            flow = flow_of(velocity, snaps_next[0, 1], l)
            full_layer(below, layer_of(state, l), above, flow, shape, into(widened, l + 1))

        first_step(0, halo_at(halos, 0), layer_of(state, 1))
        first_step(depth - 1, layer_of(state, depth - 2), halo_at(halos, 1))
        each(1, depth - 1, lambda l: first_step(l, layer_of(state, l - 1), layer_of(state, l + 1)))

        def second_step(e):
            l = e + (e // 2) * (depth - edge_count)
            flow = flow_of(velocity, snaps_next[0, 0], l)
            here = layer_of(widened, l + 1)
            full_layer(layer_of(widened, l), here, layer_of(widened, l + 2), flow, shape, into(edges, e))

        each(0, edge_count, second_step)
        pack_both(edges, velocity, snaps[0, 1], message_one, message_two)


def inner_kernel(slabs, snaps, snaps_next, widened, edges, velocity, start, carried_on, inner, *rest):
    pieces, (state, final, total, sem) = rest[:slabs], rest[slabs:]
    depth, shape = state.shape[1], state.shape[2:]
    last = lax.axis_index("tm") == slabs - 1

    @pl.when(last)
    def _():
        pltpu.sync_copy(start, state)

    @pl.when(jnp.logical_not(last))
    def _():
        def second_step(l):
            flow = flow_of(velocity, snaps_next[0, 0], l)
            here = layer_of(widened, l + 1)
            full_layer(layer_of(widened, l), here, layer_of(widened, l + 2), flow, shape, into(state, l))

        each(2, depth - 2, second_step)
        state[:, 0:2] = edges[:, 0:2]
        state[:, depth - 2 : depth] = edges[:, 2:4]

    def third_step(l):
        flow = flow_of(velocity, snaps[0, 1], l)
        here = layer_of(state, l)
        full_layer(layer_of(state, l - 1), here, layer_of(state, l + 1), flow, shape, into(carried_on, l))

    each(1, depth - 1, third_step)

    def fourth_step(l):
        def store(i, j, values):
            into(final, l - 2)(i, j, values)
            total[(l - 2,) + spot(i, j)] = carried_on[(0, l) + spot(i, j)] + values[0]

        flow = flow_of(velocity, snaps[0, 0], l)
        here = layer_of(carried_on, l)
        full_layer(layer_of(carried_on, l - 1), here, layer_of(carried_on, l + 1), flow, shape, store)

    each(2, depth - 2, fourth_step)
    copy = pltpu.make_async_copy(final, inner.at[:, pl.ds(2, depth - 4)], sem)
    copy.start()
    split_rows(total, pieces)
    copy.wait()


def last_steps(snaps, carried_on, outer, velocity, store, wanted):
    depth, shape = carried_on.shape[1], carried_on.shape[2:]
    ring = [layer_of(outer, 0), layer_of(outer, 1), layer_of(carried_on, 1), layer_of(carried_on, 2)]
    ring += [layer_of(carried_on, depth - 3), layer_of(carried_on, depth - 2), layer_of(outer, 2), layer_of(outer, 3)]
    for e, at in enumerate((1, 2, 5, 6)):
        l = e + (e // 2) * (depth - edge_count)
        flow = flow_of(velocity, snaps[0, 0], l)
        full_layer(ring[at - 1], ring[at], ring[at + 1], flow, shape, functools.partial(store, e, ring[at]), wanted)


def outer_kernel(blocks, slabs, snaps, edges, halo_one, halo_two, own_flow, other_flow, carried_on, widened, velocity,
                 *rest):
    parts, (inner_sum, outer, to_core), rest = rest[:slabs], rest[slabs : slabs + 3], rest[slabs + 3 :]
    pieces, (halos, total) = rest[:slabs], rest[slabs:]
    depth, shape = carried_on.shape[1], carried_on.shape[2:]
    slab = lax.axis_index("tm")
    inner_sum[...] = functools.reduce(jnp.add, [part[...] for part in parts])

    @pl.when(slab == slabs - 1)
    def _():
        total[...] = jnp.zeros_like(total)

    @pl.when(slab < slabs - 1)
    def _():
        take_halos(
            blocks, edges, halo_one, halo_two, own_flow, other_flow, snaps[0, 1], halos, outer, edge_count
        )
        flow = flow_of(velocity, snaps[0, 1], 0)
        full_layer(halo_at(halos, 0), layer_of(edges, 0), layer_of(edges, 1), flow, shape, into(outer, 1))
        flow = flow_of(velocity, snaps[0, 1], depth - 1)
        full_layer(layer_of(edges, 2), layer_of(edges, 3), halo_at(halos, 1), flow, shape, into(outer, 2))
        with_last = slab == slabs - 2

        def store(e, here, i, j, values):
            l = e + (e // 2) * (depth - edge_count)
            before = widened[(0, l + 1) + spot(i, j)] + edges[(0, e) + spot(i, j)]
            total[(e,) + spot(i, j)] = here(0, i, j) + values[0] + jnp.where(with_last, before, 0.0)

        last_steps(snaps, carried_on, outer, velocity, store, (0,))

    split_rows(total, pieces)
    rows = shape[0] // slabs
    for f in (0, 1):
        to_core[f * edge_count : (f + 1) * edge_count] = edges[f]
    for e in range(edge_count):
        to_core[2 * edge_count, e * rows : (e + 1) * rows] = pieces[1][e]


def finish_kernel(slabs, snaps, carried_on, outer, velocity, from_core, inner_sum, inner, inner_sum_out, out, final, sems):
    depth = carried_on.shape[1]

    def store(e, here, i, j, values):
        into(final, e)(i, j, values)

    last = lax.axis_index("tm") == slabs - 1

    @pl.when(last)
    def _():
        for f in (0, 1):
            final[f] = from_core[f * edge_count : (f + 1) * edge_count]

    @pl.when(jnp.logical_not(last))
    def _():
        last_steps(snaps, carried_on, outer, velocity, store, (0, 1))

    copies = [
        pltpu.make_async_copy(final.at[:, pl.ds(0, 2)], out.at[:, pl.ds(0, 2)], sems.at[0]),
        pltpu.make_async_copy(final.at[:, pl.ds(2, 2)], out.at[:, pl.ds(depth - 2, 2)], sems.at[1]),
    ]
    for copy in copies:
        copy.start()
    for copy in copies:
        copy.wait()


def sum_kernel(inner_sum, from_core, *refs):
    parts, out = refs[:-1], refs[-1]
    depth, rows = out.shape[:2]
    out[2 : depth - 2] = inner_sum[...]
    for e in range(edge_count):
        l = e + (e // 2) * (depth - edge_count)
        out[l] = functools.reduce(jnp.add, [part[e] for part in parts]) + from_core[2 * edge_count, pl.ds(e * rows, rows)]


def solution(mesh):
    slabs, blocks = mesh.shape["tm"], mesh.shape["space"]
    vmem, smem = pl.BlockSpec(memory_space=pltpu.VMEM), pl.BlockSpec(memory_space=pltpu.SMEM)
    hbm = pl.BlockSpec(memory_space=pltpu.HBM)
    sem = pltpu.SemaphoreType.DMA

    def params(mebibytes):
        return pltpu.CompilerParams(vmem_limit_bytes=mebibytes * 1024 * 1024)

    def cost(microseconds):
        return pl.CostEstimate(flops=0, bytes_accessed=int(microseconds * 3.6e6), transcendentals=0)

    def index(t, s):
        return (t % slabs) * blocks + s % blocks

    def moved(array, to):
        pairs = [(index(t, s), index(*to(t, s))) for t in range(slabs) for s in range(blocks)]
        return lax.ppermute(array, ("tm", "space"), pairs)

    def exchanged(array, by, earlier):
        part = slabs if earlier else slabs - 1

        def to(t, s):
            partner = ((s + by) ^ 1) - by
            if t >= part:
                return (t, s // 8 * 8 + (s + 2 - 4 * by) % 8)
            return (t - earlier, partner) if 0 <= partner < blocks else ((t + 1) % part, s)

        return moved(array, to)

    def fetched(t, s):
        source = s + 1 - 2 * (t % 2)
        return (t ^ 2, source) if 0 <= source < blocks else (t ^ 1, s)

    def body(slab_states, velocity, snap_of_step):
        start = slab_states[0]
        fields, depth, ny, nz = start.shape

        def shaped(*lead, rows=ny):
            return jax.ShapeDtypeStruct(lead + (rows, nz), jnp.float32)

        def room(*lead):
            return pltpu.VMEM(lead + (ny, nz), jnp.float32)

        layer = shaped(4)
        pieces = (shaped(4, rows=ny // slabs),) * slabs

        state = moved(start, lambda t, s: (t - 1, s))
        snaps_next = moved(snap_of_step, lambda t, s: (t - 1, s))
        message_one, message_two, flow_out = pl.pallas_call(
            start_kernel,
            out_shape=(layer, layer, shaped(velocity.shape[0])),
            in_specs=[hbm] * 3,
            out_specs=(vmem,) * 3,
            scratch_shapes=[
                pltpu.SMEM(snap_of_step.shape, jnp.int32),
                room(fields, edge_count),
                room(*velocity.shape[:2], 2),
                sem((5,)),
            ],
            compiler_params=params(56),
            cost_estimate=cost(2),
        )(snap_of_step, start, velocity)
        halo_one = exchanged(message_one, 0, 1)
        halo_two = exchanged(message_two, 1, 1)
        own_flow = moved(flow_out, fetched)
        other_flow = moved(own_flow, lambda t, s: (t ^ 1, s))
        widened, edges, message_one, message_two = pl.pallas_call(
            functools.partial(first_kernel, blocks, slabs),
            out_shape=(shaped(fields, depth + 2), shaped(fields, edge_count), layer, layer),
            in_specs=[smem, smem] + [vmem] * 6,
            out_specs=(vmem,) * 4,
            scratch_shapes=[room(2, fields)],
            compiler_params=params(32),
            cost_estimate=cost(2.5),
        )(snap_of_step, snaps_next, state, halo_one, halo_two, own_flow, other_flow, velocity)
        halo_one = exchanged(message_one, 0, 0)
        halo_two = exchanged(message_two, 1, 0)
        carried_on, inner, *inner_pieces = pl.pallas_call(
            functools.partial(inner_kernel, slabs),
            out_shape=(shaped(fields, depth), shaped(fields, depth)) + pieces,
            in_specs=[smem, smem, vmem, vmem, vmem, hbm],
            out_specs=(vmem, hbm) + (vmem,) * slabs,
            scratch_shapes=[room(fields, depth), room(fields, depth - 4), room(depth - 4), sem(())],
            compiler_params=params(32),
            cost_estimate=cost(3),
        )(snap_of_step, snaps_next, widened, edges, velocity, start)
        inner_parts = inner_pieces[:1] + [
            moved(inner_pieces[by], lambda t, s, by=by: (t ^ by, s)) for by in range(1, slabs)
        ]
        inner_sum, outer, to_core, *outer_pieces = pl.pallas_call(
            functools.partial(outer_kernel, blocks, slabs),
            out_shape=(pieces[0], shaped(fields, edge_count), shaped(2 * edge_count + 1)) + pieces,
            in_specs=[smem] + [vmem] * (8 + slabs),
            out_specs=(vmem,) * (3 + slabs),
            scratch_shapes=[room(2, fields), room(edge_count)],
            compiler_params=params(32),
            cost_estimate=cost(1),
        )(snap_of_step, edges, halo_one, halo_two, own_flow, other_flow, carried_on, widened, velocity, *inner_parts)
        across = [moved(outer_pieces[by], lambda t, s, by=by: (t ^ by, s)) for by in (2, 3)]
        from_core = moved(to_core, lambda t, s: (t ^ 1, s))
        inner_sum, final = pl.pallas_call(
            functools.partial(finish_kernel, slabs),
            out_shape=(pieces[0], shaped(fields, depth)),
            in_specs=[smem] + [vmem] * 5 + [hbm],
            out_specs=(vmem, hbm),
            scratch_shapes=[room(fields, edge_count), sem((2,))],
            input_output_aliases={5: 0, 6: 1},
            compiler_params=params(32),
            cost_estimate=cost(1),
        )(snap_of_step, carried_on, outer, velocity, from_core, inner_sum, inner)
        gradient = pl.pallas_call(
            sum_kernel,
            out_shape=shaped(depth, rows=ny // slabs),
            in_specs=[vmem] * 5,
            out_specs=vmem,
            compiler_params=params(16),
            cost_estimate=cost(0.5),
        )(inner_sum, from_core, outer_pieces[0], *across)
        return (final[None], gradient)

    return jax.shard_map(
        body,
        mesh=mesh,
        in_specs=(P("tm", None, "space", None, None), P(None, None, "space", None, None), P("tm", None)),
        out_specs=(P("tm", None, "space", None, None), P("space", "tm", None)),
        check_vma=False,
    )
```

```python
import functools

import jax
import jax.numpy as jnp
from jax import lax
from jax.experimental import pallas as pl
from jax.experimental.pallas import tpu as pltpu
from jax.sharding import PartitionSpec as P

coupling = 0.3
diffusion = (0.14, 0.06)
sub, lanes = 8, 128
edge_count = 4


def tiles(shape):
    rows, cols = shape
    return [(i, j) for i in range(rows // sub) for j in range(cols // lanes)]


def spot(i, j):
    return (pl.ds(i * sub, sub), pl.ds(j * lanes, lanes))


def neighbours(at, i, j, shape):
    rows, cols = shape
    centre = at(i, j)
    row = lax.broadcasted_iota(jnp.int32, (sub, lanes), 0)
    col = lax.broadcasted_iota(jnp.int32, (sub, lanes), 1)
    zero = jnp.zeros_like(centre)
    after = at(i + 1, j) if (i + 1) * sub < rows else zero
    before = at(i - 1, j) if i > 0 else zero
    north = pltpu.roll(jnp.where(row == 0, after, centre), sub - 1, 0)
    south = pltpu.roll(jnp.where(row == sub - 1, before, centre), 1, 0)
    after = at(i, j + 1) if (j + 1) * lanes < cols else zero
    before = at(i, j - 1) if j > 0 else zero
    upper = pltpu.roll(jnp.where(col == 0, after, centre), lanes - 1, 1)
    lower = pltpu.roll(jnp.where(col == lanes - 1, before, centre), 1, 1)
    return centre, (north + south) + (upper + lower), north - south, upper - lower


def advanced(fields, pairs, flow, i, j, shape, wanted=(0, 1)):
    u, v, w = flow
    out = []
    for f in wanted:
        centre, total, dy, dz = neighbours(functools.partial(fields, f), i, j, shape)
        side_sum, side_diff = pairs(f, i, j)
        c = diffusion[f]
        moved = u * side_diff + v * dy + w * dz
        new = ((1.0 - 6.0 * c) * centre + c * (side_sum + total)) + 0.25 * moved
        if f == 0:
            new = new + coupling * fields(1, i, j)
        out.append(new)
    return out


def layer_of(ref, l):
    return lambda f, i, j: ref[(f, l) + spot(i, j)]


def flow_of(velocity, snap, l):
    return lambda i, j: [velocity[(snap, d, l) + spot(i, j)] for d in range(3)]


def full_layer(below, here, above, flow, shape, store, wanted=(0, 1)):
    def pairs(f, i, j):
        hi, lo = above(f, i, j), below(f, i, j)
        return hi + lo, hi - lo

    for i, j in tiles(shape):
        store(i, j, advanced(here, pairs, flow(i, j), i, j, shape, wanted))


def into(ref, l):
    def store(i, j, values):
        for f, value in enumerate(values):
            ref[(f, l) + spot(i, j)] = value

    return store


def sides(depth):
    parity = lax.rem(lax.axis_index("space"), 2)
    even = parity == 0
    high = (jnp.where(even, depth - 1, 0), jnp.where(even, depth - 2, 1), jnp.where(even, -1.0, 1.0))
    low = (jnp.where(even, 0, depth - 1), jnp.where(even, 1, depth - 2), jnp.where(even, 1.0, -1.0))
    return parity, high, low


def pack(edges, velocity, snap, message, layer, inner, sign):
    shape = edges.shape[2:]
    at = (layer // (edge_count - 1)) * (velocity.shape[2] - 1)
    near, here, flow = layer_of(edges, inner), layer_of(edges, layer), flow_of(velocity, snap, at)

    def pairs(f, i, j):
        value = near(f, i, j)
        return value, sign * value

    for i, j in tiles(shape):
        out = advanced(here, pairs, flow(i, j), i, j, shape)
        for f in (0, 1):
            message[(f,) + spot(i, j)] = here(f, i, j)
            message[(2 + f,) + spot(i, j)] = out[f]


def pack_both(edges, velocity, snap, message_one, message_two):
    unused, one, two = sides(edge_count)
    pack(edges, velocity, snap, message_one, *one)
    pack(edges, velocity, snap, message_two, *two)


def take_halos(blocks, state, halo_one, halo_two, own_flow, other_flow, snap, halos, after, depth):
    shape = state.shape[2:]
    parity, one, two = sides(depth)
    place = lax.axis_index("space")
    inside = jnp.logical_and(place > 0, place < blocks - 1)
    outer = after.shape[1] - 1
    fetched = lax.rem(lax.axis_index("tm"), 2)
    for halo, (edge, unused, sign), shown, high in (
        (halo_one, one, None, 1 - parity),
        (halo_two, two, inside, parity),
    ):
        for i, j in tiles(shape):
            u = jnp.where(high == fetched, own_flow[(snap,) + spot(i, j)], other_flow[(snap,) + spot(i, j)])
            for f in (0, 1):
                now = halo[(f,) + spot(i, j)]
                own = state[(f, edge) + spot(i, j)]
                later = halo[(2 + f,) + spot(i, j)] + (diffusion[f] + (0.25 * sign) * u) * own
                if shown is not None:
                    now = jnp.where(shown, now, 0.0)
                    later = jnp.where(shown, later, 0.0)
                halos[(high, f) + spot(i, j)] = now
                after[(f, high * outer) + spot(i, j)] = later


def halo_at(halos, h):
    return lambda f, i, j: halos[(h, f) + spot(i, j)]


def split_rows(total, pieces):
    rows = total.shape[1] // len(pieces)
    for by, piece in enumerate(pieces):
        start = pl.multiple_of(lax.rem(lax.axis_index("tm") + by, len(pieces)) * rows, rows)
        piece[...] = total[:, pl.ds(start, rows), :] * 0.5


def each(low, high, run):
    def step(l, carry):
        run(l)
        return carry

    lax.fori_loop(low, high, step, 0)


def start_kernel(snaps, state, velocity, message_one, message_two, flow_out, scalars, edges, flows, sems):
    depth = state.shape[1]
    copies = [
        (snaps, scalars),
        (state.at[:, pl.ds(0, 2)], edges.at[:, pl.ds(0, 2)]),
        (state.at[:, pl.ds(depth - 2, 2)], edges.at[:, pl.ds(2, 2)]),
        (velocity.at[:, :, pl.ds(0, 1)], flows.at[:, :, pl.ds(0, 1)]),
        (velocity.at[:, :, pl.ds(depth - 1, 1)], flows.at[:, :, pl.ds(1, 1)]),
    ]
    copies = [pltpu.make_async_copy(*pair, sems.at[n]) for n, pair in enumerate(copies)]
    for copy in copies:
        copy.start()
    for copy in copies:
        copy.wait()
    pack_both(edges, flows, scalars[0, 1], message_one, message_two)
    flow_out[...] = flows[:, 0, 1 - lax.rem(lax.axis_index("tm"), 2)]


def share_kernel(slabs, core_state, start, *refs):
    both = refs[3]

    @pl.when(lax.axis_index("tm") == slabs - 1)
    def _():
        both[...] = core_state[1]

    @pl.when(lax.axis_index("tm") < slabs - 1)
    def _():
        pltpu.sync_copy(start.at[0], both)


def split_kernel(cross, *pieces):
    for n, piece in enumerate(pieces):
        piece[...] = cross[4 * n : 4 * n + 4]


def first_kernel(blocks, slabs, snaps, snaps_next, core_state, cross, halo_one, halo_two, own_flow, other_flow, velocity, start,
                 *rest):
    hops, (widened, edges, message_one, message_two, state, halos) = rest[:-6], rest[-6:]
    depth, shape = state.shape[1], state.shape[2:]
    crossed = lax.rem(lax.axis_index("tm"), 2) == 1

    @pl.when(crossed)
    def _():
        state[0] = cross[...]
        for n, hop in enumerate(hops):
            state[1, 4 * n : 4 * n + 4] = hop[...]

    @pl.when(jnp.logical_not(crossed))
    def _():
        state[...] = core_state[...]

    last = lax.axis_index("tm") == slabs - 1

    @pl.when(last)
    def _():
        pltpu.sync_copy(start.at[:, pl.ds(0, 2)], edges.at[:, pl.ds(0, 2)])
        pltpu.sync_copy(start.at[:, pl.ds(depth - 2, 2)], edges.at[:, pl.ds(2, 2)])

    @pl.when(jnp.logical_not(last))
    def _():
        take_halos(
            blocks, state, halo_one, halo_two, own_flow, other_flow, snaps_next[0, 1], halos, widened, depth
        )

        def first_step(l, below, above):
            flow = flow_of(velocity, snaps_next[0, 1], l)
            full_layer(below, layer_of(state, l), above, flow, shape, into(widened, l + 1))

        first_step(0, halo_at(halos, 0), layer_of(state, 1))
        first_step(depth - 1, layer_of(state, depth - 2), halo_at(halos, 1))
        each(1, depth - 1, lambda l: first_step(l, layer_of(state, l - 1), layer_of(state, l + 1)))

        def second_step(e):
            l = e + (e // 2) * (depth - edge_count)
            flow = flow_of(velocity, snaps_next[0, 0], l)
            here = layer_of(widened, l + 1)
            full_layer(layer_of(widened, l), here, layer_of(widened, l + 2), flow, shape, into(edges, e))

        each(0, edge_count, second_step)

    pack_both(edges, velocity, snaps[0, 1], message_one, message_two)


def inner_kernel(slabs, snaps, snaps_next, widened, edges, velocity, start, carried_on, inner, *rest):
    pieces, (state, final, total, sem) = rest[:slabs], rest[slabs:]
    depth, shape = state.shape[1], state.shape[2:]
    last = lax.axis_index("tm") == slabs - 1

    @pl.when(last)
    def _():
        pltpu.sync_copy(start, state)

    @pl.when(jnp.logical_not(last))
    def _():
        def second_step(l):
            flow = flow_of(velocity, snaps_next[0, 0], l)
            here = layer_of(widened, l + 1)
            full_layer(layer_of(widened, l), here, layer_of(widened, l + 2), flow, shape, into(state, l))

        each(2, depth - 2, second_step)
        state[:, 0:2] = edges[:, 0:2]
        state[:, depth - 2 : depth] = edges[:, 2:4]

    def third_step(l):
        flow = flow_of(velocity, snaps[0, 1], l)
        here = layer_of(state, l)
        full_layer(layer_of(state, l - 1), here, layer_of(state, l + 1), flow, shape, into(carried_on, l))

    each(1, depth - 1, third_step)

    def fourth_step(l):
        def store(i, j, values):
            into(final, l - 2)(i, j, values)
            total[(l - 2,) + spot(i, j)] = carried_on[(0, l) + spot(i, j)] + values[0]

        flow = flow_of(velocity, snaps[0, 0], l)
        here = layer_of(carried_on, l)
        full_layer(layer_of(carried_on, l - 1), here, layer_of(carried_on, l + 1), flow, shape, store)

    each(2, depth - 2, fourth_step)
    copy = pltpu.make_async_copy(final, inner.at[:, pl.ds(2, depth - 4)], sem)
    copy.start()
    split_rows(total, pieces)
    copy.wait()


def last_steps(snaps, carried_on, outer, velocity, store, wanted):
    depth, shape = carried_on.shape[1], carried_on.shape[2:]
    ring = [layer_of(outer, 0), layer_of(outer, 1), layer_of(carried_on, 1), layer_of(carried_on, 2)]
    ring += [layer_of(carried_on, depth - 3), layer_of(carried_on, depth - 2), layer_of(outer, 2), layer_of(outer, 3)]
    for e, at in enumerate((1, 2, 5, 6)):
        l = e + (e // 2) * (depth - edge_count)
        flow = flow_of(velocity, snaps[0, 0], l)
        full_layer(ring[at - 1], ring[at], ring[at + 1], flow, shape, functools.partial(store, e, ring[at]), wanted)


def outer_kernel(blocks, slabs, snaps, edges, halo_one, halo_two, own_flow, other_flow, carried_on, velocity,
                 outer, *rest):
    pieces, (halos, total) = rest[:slabs], rest[slabs:]
    depth, shape = carried_on.shape[1], carried_on.shape[2:]
    take_halos(
        blocks, edges, halo_one, halo_two, own_flow, other_flow, snaps[0, 1], halos, outer, edge_count
    )
    flow = flow_of(velocity, snaps[0, 1], 0)
    full_layer(halo_at(halos, 0), layer_of(edges, 0), layer_of(edges, 1), flow, shape, into(outer, 1))
    flow = flow_of(velocity, snaps[0, 1], depth - 1)
    full_layer(layer_of(edges, 2), layer_of(edges, 3), halo_at(halos, 1), flow, shape, into(outer, 2))

    def store(e, here, i, j, values):
        total[(e,) + spot(i, j)] = here(0, i, j) + values[0]

    last_steps(snaps, carried_on, outer, velocity, store, (0,))
    split_rows(total, pieces)


def finish_kernel(snaps, carried_on, outer, velocity, inner, out, final, sems):
    depth = carried_on.shape[1]

    def store(e, here, i, j, values):
        into(final, e)(i, j, values)

    last_steps(snaps, carried_on, outer, velocity, store, (0, 1))
    copies = [
        pltpu.make_async_copy(final.at[:, pl.ds(0, 2)], out.at[:, pl.ds(0, 2)], sems.at[0]),
        pltpu.make_async_copy(final.at[:, pl.ds(2, 2)], out.at[:, pl.ds(depth - 2, 2)], sems.at[1]),
    ]
    for copy in copies:
        copy.start()
    for copy in copies:
        copy.wait()


def sum_kernel(*refs):
    ins, out = refs[:-1], refs[-1]
    half = len(ins) // 2
    depth = out.shape[0]
    inner = functools.reduce(jnp.add, [ref[...] for ref in ins[:half]])
    outer = functools.reduce(jnp.add, [ref[...] for ref in ins[half:]])
    out[2 : depth - 2] = inner
    out[0:2] = outer[0:2]
    out[depth - 2 : depth] = outer[2:4]


def solution(mesh):
    slabs, blocks = mesh.shape["tm"], mesh.shape["space"]
    vmem, smem = pl.BlockSpec(memory_space=pltpu.VMEM), pl.BlockSpec(memory_space=pltpu.SMEM)
    hbm = pl.BlockSpec(memory_space=pltpu.HBM)
    sem = pltpu.SemaphoreType.DMA

    def params(mebibytes):
        return pltpu.CompilerParams(vmem_limit_bytes=mebibytes * 1024 * 1024)

    def cost(microseconds):
        return pl.CostEstimate(flops=0, bytes_accessed=int(microseconds * 3.6e6), transcendentals=0)

    def index(t, s):
        return (t % slabs) * blocks + s % blocks

    def moved(array, to):
        pairs = [(index(t, s), index(*to(t, s))) for t in range(slabs) for s in range(blocks)]
        return lax.ppermute(array, ("tm", "space"), pairs)

    def exchanged(array, by, earlier):
        def to(t, s):
            partner = ((s + by) ^ 1) - by
            return (t - earlier, partner) if 0 <= partner < blocks else (t ^ 1, s)

        return moved(array, to)

    def fetched(t, s):
        source = s + 1 - 2 * (t % 2)
        return (t ^ 2, source) if 0 <= source < blocks else (t ^ 1, s)

    def body(slab_states, velocity, snap_of_step):
        start = slab_states[0]
        fields, depth, ny, nz = start.shape

        def shaped(*lead, rows=ny):
            return jax.ShapeDtypeStruct(lead + (rows, nz), jnp.float32)

        def room(*lead):
            return pltpu.VMEM(lead + (ny, nz), jnp.float32)

        layer = shaped(4)
        pieces = (shaped(4, rows=ny // slabs),) * slabs

        core_state = moved(start, lambda t, s: (t ^ 1, s))
        snaps_next = moved(snap_of_step, lambda t, s: (t - 1, s))
        message_one, message_two, flow_out = pl.pallas_call(
            start_kernel,
            out_shape=(layer, layer, shaped(velocity.shape[0])),
            in_specs=[hbm] * 3,
            out_specs=(vmem,) * 3,
            scratch_shapes=[
                pltpu.SMEM(snap_of_step.shape, jnp.int32),
                room(fields, edge_count),
                room(*velocity.shape[:2], 2),
                sem((5,)),
            ],
            compiler_params=params(53),
            cost_estimate=cost(2),
        )(snap_of_step, start, velocity)
        both, message_one, message_two, flow_out = pl.pallas_call(
            functools.partial(share_kernel, slabs),
            out_shape=(shaped(depth), layer, layer, shaped(velocity.shape[0])),
            in_specs=[vmem] + [hbm] * 4,
            out_specs=(vmem,) + (hbm,) * 3,
            input_output_aliases={2: 1, 3: 2, 4: 3},
            compiler_params=params(32),
            cost_estimate=cost(0.5),
        )(core_state, start, message_one, message_two, flow_out)
        cross = moved(both, lambda t, s: (t ^ 3, s))
        halo_one = exchanged(message_one, 0, 1)
        halo_two = exchanged(message_two, 1, 1)
        own_flow = moved(flow_out, fetched)
        other_flow = moved(own_flow, lambda t, s: (t ^ 1, s))
        hops = pl.pallas_call(
            split_kernel,
            out_shape=(shaped(4),) * (depth // 4),
            in_specs=[vmem],
            out_specs=(vmem,) * (depth // 4),
            compiler_params=params(16),
            cost_estimate=cost(0.5),
        )(cross)
        hops = [moved(hop, lambda t, s: (t ^ 1, s)) for hop in hops]
        widened, edges, message_one, message_two = pl.pallas_call(
            functools.partial(first_kernel, blocks, slabs),
            out_shape=(shaped(fields, depth + 2), shaped(fields, edge_count), layer, layer),
            in_specs=[smem, smem] + [vmem] * 7 + [hbm] + [vmem] * len(hops),
            out_specs=(vmem,) * 4,
            scratch_shapes=[room(fields, depth), room(2, fields)],
            compiler_params=params(32),
            cost_estimate=cost(2.5),
        )(snap_of_step, snaps_next, core_state, cross, halo_one, halo_two, own_flow, other_flow, velocity, start, *hops)
        halo_one = exchanged(message_one, 0, 0)
        halo_two = exchanged(message_two, 1, 0)
        carried_on, inner, *inner_pieces = pl.pallas_call(
            functools.partial(inner_kernel, slabs),
            out_shape=(shaped(fields, depth), shaped(fields, depth)) + pieces,
            in_specs=[smem, smem, vmem, vmem, vmem, hbm],
            out_specs=(vmem, hbm) + (vmem,) * slabs,
            scratch_shapes=[room(fields, depth), room(fields, depth - 4), room(depth - 4), sem(())],
            compiler_params=params(32),
            cost_estimate=cost(3),
        )(snap_of_step, snaps_next, widened, edges, velocity, start)
        inner_parts = inner_pieces[:1] + [
            moved(inner_pieces[by], lambda t, s, by=by: (t + by, s)) for by in range(1, slabs)
        ]
        outer, *outer_pieces = pl.pallas_call(
            functools.partial(outer_kernel, blocks, slabs),
            out_shape=(shaped(fields, edge_count),) + pieces,
            in_specs=[smem] + [vmem] * 7,
            out_specs=(vmem,) * (1 + slabs),
            scratch_shapes=[room(2, fields), room(edge_count)],
            compiler_params=params(32),
            cost_estimate=cost(1),
        )(snap_of_step, edges, halo_one, halo_two, own_flow, other_flow, carried_on, velocity)
        outer_parts = outer_pieces[:1] + [
            moved(outer_pieces[by], lambda t, s, by=by: (t + by, s)) for by in range(1, slabs)
        ]
        final = pl.pallas_call(
            finish_kernel,
            out_shape=shaped(fields, depth),
            in_specs=[smem, vmem, vmem, vmem, hbm],
            out_specs=hbm,
            scratch_shapes=[room(fields, edge_count), sem((2,))],
            input_output_aliases={4: 0},
            compiler_params=params(32),
            cost_estimate=cost(1),
        )(snap_of_step, carried_on, outer, velocity, inner)
        gradient = pl.pallas_call(
            sum_kernel,
            out_shape=shaped(depth, rows=ny // slabs),
            in_specs=[vmem] * (2 * slabs),
            out_specs=vmem,
            compiler_params=params(16),
            cost_estimate=cost(0.5),
        )(*inner_parts, *outer_parts)
        return (final[None], gradient)

    return jax.shard_map(
        body,
        mesh=mesh,
        in_specs=(P("tm", None, "space", None, None), P(None, None, "space", None, None), P("tm", None)),
        out_specs=(P("tm", None, "space", None, None), P("space", "tm", None)),
        check_vma=False,
    )
```

```python
import functools

import jax
import jax.numpy as jnp
from jax import lax
from jax.experimental import pallas as pl
from jax.experimental.pallas import tpu as pltpu
from jax.sharding import PartitionSpec as P

coupling = 0.3
diffusion = (0.14, 0.06)
sub, lanes = 8, 128
edge_count = 4


def tiles(shape):
    rows, cols = shape
    return [(i, j) for i in range(rows // sub) for j in range(cols // lanes)]


def spot(i, j):
    return (pl.ds(i * sub, sub), pl.ds(j * lanes, lanes))


def neighbours(at, i, j, shape):
    rows, cols = shape
    centre = at(i, j)
    row = lax.broadcasted_iota(jnp.int32, (sub, lanes), 0)
    col = lax.broadcasted_iota(jnp.int32, (sub, lanes), 1)
    zero = jnp.zeros_like(centre)
    after = at(i + 1, j) if (i + 1) * sub < rows else zero
    before = at(i - 1, j) if i > 0 else zero
    north = pltpu.roll(jnp.where(row == 0, after, centre), sub - 1, 0)
    south = pltpu.roll(jnp.where(row == sub - 1, before, centre), 1, 0)
    after = at(i, j + 1) if (j + 1) * lanes < cols else zero
    before = at(i, j - 1) if j > 0 else zero
    upper = pltpu.roll(jnp.where(col == 0, after, centre), lanes - 1, 1)
    lower = pltpu.roll(jnp.where(col == lanes - 1, before, centre), 1, 1)
    return centre, (north + south) + (upper + lower), north - south, upper - lower


def advanced(fields, pairs, flow, i, j, shape, wanted=(0, 1)):
    u, v, w = flow
    out = []
    for f in wanted:
        centre, total, dy, dz = neighbours(functools.partial(fields, f), i, j, shape)
        side_sum, side_diff = pairs(f, i, j)
        c = diffusion[f]
        moved = u * side_diff + v * dy + w * dz
        new = ((1.0 - 6.0 * c) * centre + c * (side_sum + total)) + 0.25 * moved
        if f == 0:
            new = new + coupling * fields(1, i, j)
        out.append(new)
    return out


def layer_of(ref, l):
    return lambda f, i, j: ref[(f, l) + spot(i, j)]


def flow_of(velocity, snap, l):
    return lambda i, j: [velocity[(snap, d, l) + spot(i, j)] for d in range(3)]


def full_layer(below, here, above, flow, shape, store, wanted=(0, 1)):
    def pairs(f, i, j):
        hi, lo = above(f, i, j), below(f, i, j)
        return hi + lo, hi - lo

    for i, j in tiles(shape):
        store(i, j, advanced(here, pairs, flow(i, j), i, j, shape, wanted))


def into(ref, l):
    def store(i, j, values):
        for f, value in enumerate(values):
            ref[(f, l) + spot(i, j)] = value

    return store


def side_of(partner):
    parity = lax.rem(lax.axis_index("space"), 2)
    high = 1 - parity if partner == 0 else parity
    return high, (2 * high - 1).astype(jnp.float32)


def side_layer(outer, here, inner, flow, sign, shape, store, wanted=(0, 1)):
    def pairs(f, i, j):
        far, near = outer(f, i, j), inner(f, i, j)
        return far + near, far - near

    for i, j in tiles(shape):
        u, v, w = flow(i, j)
        store(i, j, advanced(here, pairs, (sign * u, v, w), i, j, shape, wanted))


def pack(here, inner, flow, sign, message, shape):
    def pairs(f, i, j):
        value = inner(f, i, j)
        return value, value

    for i, j in tiles(shape):
        u, v, w = flow(i, j)
        out = advanced(here, pairs, (-sign * u, v, w), i, j, shape)
        for f in (0, 1):
            message[(f,) + spot(i, j)] = here(f, i, j)
            message[(2 + f,) + spot(i, j)] = out[f]


def take_halo(blocks, partner, halo, own, own_flow, other_flow, snap, now, after, shape):
    high, sign = side_of(partner)
    place = lax.axis_index("space")
    inside = jnp.logical_and(place > 0, place < blocks - 1)
    fetched = lax.rem(lax.axis_index("tm"), 2)
    for i, j in tiles(shape):
        u = jnp.where(high == fetched, own_flow[(snap,) + spot(i, j)], other_flow[(snap,) + spot(i, j)])
        for f in (0, 1):
            current = halo[(f,) + spot(i, j)]
            later = halo[(2 + f,) + spot(i, j)] + (diffusion[f] - (0.25 * sign) * u) * own(f, i, j)
            if partner == 1:
                current = jnp.where(inside, current, 0.0)
                later = jnp.where(inside, later, 0.0)
            now[(f,) + spot(i, j)] = current
            after[(f, 0) + spot(i, j)] = later


def plain(ref):
    return lambda f, i, j: ref[(f,) + spot(i, j)]


def split_rows(total, pieces):
    rows = total.shape[1] // len(pieces)
    for by, piece in enumerate(pieces):
        start = pl.multiple_of(lax.rem(lax.axis_index("tm") + by, len(pieces)) * rows, rows)
        piece[...] = total[:, pl.ds(start, rows), :] * 0.5


def each(low, high, run):
    def step(l, carry):
        run(l)
        return carry

    lax.fori_loop(low, high, step, 0)


def start_kernel(snaps, state, velocity, message_one, message_two, flow_out, scalars, edges, flows, sems):
    depth = state.shape[1]
    copies = [
        (snaps, scalars),
        (state.at[:, pl.ds(0, 2)], edges.at[:, pl.ds(0, 2)]),
        (state.at[:, pl.ds(depth - 2, 2)], edges.at[:, pl.ds(2, 2)]),
        (velocity.at[:, :, pl.ds(0, 1)], flows.at[:, :, pl.ds(0, 1)]),
        (velocity.at[:, :, pl.ds(depth - 1, 1)], flows.at[:, :, pl.ds(1, 1)]),
    ]
    copies = [pltpu.make_async_copy(*pair, sems.at[n]) for n, pair in enumerate(copies)]
    for copy in copies:
        copy.start()
    for copy in copies:
        copy.wait()
    for partner, message in enumerate((message_one, message_two)):
        high, sign = side_of(partner)
        here, inner = layer_of(edges, 3 * high), layer_of(edges, 1 + high)
        pack(here, inner, flow_of(flows, scalars[0, 1], high), sign, message, edges.shape[2:])
    flow_out[...] = flows[:, 0, 1 - lax.rem(lax.axis_index("tm"), 2)]


def first_kernel(blocks, slabs, partner, snaps, snaps_next, state, halo, own_flow, other_flow, velocity, start,
                 widened, edges, message, now):
    depth, shape = state.shape[1], state.shape[2:]
    last = lax.axis_index("tm") == slabs - 1
    high, sign = side_of(partner)

    def at(k):
        return high * (depth - 1) + k * (1 - 2 * high)

    @pl.when(last)
    def _():
        pltpu.sync_copy(start.at[:, pl.ds(at(0), 1)], edges.at[:, pl.ds(0, 1)])
        pltpu.sync_copy(start.at[:, pl.ds(at(1), 1)], edges.at[:, pl.ds(1, 1)])

    @pl.when(jnp.logical_not(last))
    def _():
        snap = snaps_next[0, 1]
        take_halo(blocks, partner, halo, layer_of(state, at(0)), own_flow, other_flow, snap, now, widened, shape)
        for k in range(3):
            outer = plain(now) if k == 0 else layer_of(state, at(k - 1))
            here, inner, flow = layer_of(state, at(k)), layer_of(state, at(k + 1)), flow_of(velocity, snap, at(k))
            side_layer(outer, here, inner, flow, sign, shape, into(widened, k + 1))
        for k in range(2):
            outer, here, inner = [layer_of(widened, k + n) for n in range(3)]
            flow = flow_of(velocity, snaps_next[0, 0], at(k))
            side_layer(outer, here, inner, flow, sign, shape, into(edges, k))

    pack(layer_of(edges, 0), layer_of(edges, 1), flow_of(velocity, snaps[0, 1], at(0)), sign, message, shape)


def inner_kernel(slabs, snaps, snaps_next, before, widened_one, widened_two, edges_one, edges_two, velocity, start,
                 carried_on, inner, *rest):
    pieces, (state, widened, final, total, sem) = rest[:slabs], rest[slabs:]
    depth, shape = state.shape[1], state.shape[2:]
    last = lax.axis_index("tm") == slabs - 1

    @pl.when(last)
    def _():
        pltpu.sync_copy(start, state)

    @pl.when(jnp.logical_not(last))
    def _():
        for partner, wide, edges in ((0, widened_one, edges_one), (1, widened_two, edges_two)):
            high, unused = side_of(partner)
            for k in range(4):
                widened[:, high * (depth + 1) + k * (1 - 2 * high)] = wide[:, k]
            for k in range(2):
                state[:, high * (depth - 1) + k * (1 - 2 * high)] = edges[:, k]

        def first_step(l):
            flow = flow_of(velocity, snaps_next[0, 1], l)
            here = layer_of(before, l)
            full_layer(layer_of(before, l - 1), here, layer_of(before, l + 1), flow, shape, into(widened, l + 1))

        each(3, depth - 3, first_step)

        def second_step(l):
            flow = flow_of(velocity, snaps_next[0, 0], l)
            here = layer_of(widened, l + 1)
            full_layer(layer_of(widened, l), here, layer_of(widened, l + 2), flow, shape, into(state, l))

        each(2, depth - 2, second_step)

    def third_step(l):
        flow = flow_of(velocity, snaps[0, 1], l)
        here = layer_of(state, l)
        full_layer(layer_of(state, l - 1), here, layer_of(state, l + 1), flow, shape, into(carried_on, l))

    each(1, depth - 1, third_step)

    def fourth_step(l):
        def store(i, j, values):
            into(final, l - 2)(i, j, values)
            total[(l - 2,) + spot(i, j)] = carried_on[(0, l) + spot(i, j)] + values[0]

        flow = flow_of(velocity, snaps[0, 0], l)
        here = layer_of(carried_on, l)
        full_layer(layer_of(carried_on, l - 1), here, layer_of(carried_on, l + 1), flow, shape, store)

    each(2, depth - 2, fourth_step)
    copy = pltpu.make_async_copy(final, inner.at[:, pl.ds(2, depth - 4)], sem)
    copy.start()
    split_rows(total, pieces)
    copy.wait()


def last_steps(partner, snaps, carried_on, outer, velocity, store, wanted):
    depth, shape = carried_on.shape[1], carried_on.shape[2:]
    high, sign = side_of(partner)

    def at(k):
        return high * (depth - 1) + k * (1 - 2 * high)

    ring = [layer_of(outer, 0), layer_of(outer, 1), layer_of(carried_on, at(1)), layer_of(carried_on, at(2))]
    for k in range(2):
        flow = flow_of(velocity, snaps[0, 0], at(k))
        keep = functools.partial(store, k, ring[k + 1])
        side_layer(ring[k], ring[k + 1], ring[k + 2], flow, sign, shape, keep, wanted)


def outer_kernel(blocks, slabs, partner, snaps, edges, halo, own_flow, other_flow, carried_on, velocity, *rest):
    before, rest = rest[:partner], rest[partner:]
    if partner == 0:
        outer, total, now = rest
    else:
        outer, pieces, (now, total, whole) = rest[0], rest[1 : slabs + 1], rest[slabs + 1 :]
    depth, shape = carried_on.shape[1], carried_on.shape[2:]
    high, sign = side_of(partner)
    snap = snaps[0, 1]
    take_halo(blocks, partner, halo, layer_of(edges, 0), own_flow, other_flow, snap, now, outer, shape)
    flow = flow_of(velocity, snap, high * (depth - 1))
    side_layer(plain(now), layer_of(edges, 0), layer_of(edges, 1), flow, sign, shape, into(outer, 1))

    def store(k, here, i, j, values):
        total[(k,) + spot(i, j)] = here(0, i, j) + values[0]

    last_steps(partner, snaps, carried_on, outer, velocity, store, (0,))
    if partner == 1:
        for k in range(2):
            whole[high * (edge_count - 1) + k * (1 - 2 * high)] = total[k]
            whole[(1 - high) * (edge_count - 1) - k * (1 - 2 * high)] = before[0][k]
        split_rows(whole, pieces)


def finish_kernel(snaps, carried_on, outer_one, outer_two, velocity, inner, out, final, sems):
    depth = carried_on.shape[1]
    for partner, outer in enumerate((outer_one, outer_two)):
        high, unused = side_of(partner)

        def store(k, here, i, j, values, high=high):
            into(final, high * (edge_count - 1) + k * (1 - 2 * high))(i, j, values)

        last_steps(partner, snaps, carried_on, outer, velocity, store, (0, 1))
    copies = [
        pltpu.make_async_copy(final.at[:, pl.ds(0, 2)], out.at[:, pl.ds(0, 2)], sems.at[0]),
        pltpu.make_async_copy(final.at[:, pl.ds(2, 2)], out.at[:, pl.ds(depth - 2, 2)], sems.at[1]),
    ]
    for copy in copies:
        copy.start()
    for copy in copies:
        copy.wait()


def sum_kernel(*refs):
    ins, out = refs[:-1], refs[-1]
    half = len(ins) // 2
    depth = out.shape[0]
    inner = functools.reduce(jnp.add, [ref[...] for ref in ins[:half]])
    outer = functools.reduce(jnp.add, [ref[...] for ref in ins[half:]])
    out[2 : depth - 2] = inner
    out[0:2] = outer[0:2]
    out[depth - 2 : depth] = outer[2:4]


def solution(mesh):
    slabs, blocks = mesh.shape["tm"], mesh.shape["space"]
    vmem, smem = pl.BlockSpec(memory_space=pltpu.VMEM), pl.BlockSpec(memory_space=pltpu.SMEM)
    hbm = pl.BlockSpec(memory_space=pltpu.HBM)
    sem = pltpu.SemaphoreType.DMA

    def params(mebibytes):
        return pltpu.CompilerParams(vmem_limit_bytes=mebibytes * 1024 * 1024)

    def cost(microseconds):
        return pl.CostEstimate(flops=0, bytes_accessed=int(microseconds * 3.6e6), transcendentals=0)

    def index(t, s):
        return (t % slabs) * blocks + s % blocks

    def moved(array, to):
        pairs = [(index(t, s), index(*to(t, s))) for t in range(slabs) for s in range(blocks)]
        return lax.ppermute(array, ("tm", "space"), pairs)

    def exchanged(array, by, earlier):
        def to(t, s):
            partner = ((s + by) ^ 1) - by
            return (t - earlier, partner) if 0 <= partner < blocks else (t ^ 1, s)

        return moved(array, to)

    def fetched(t, s):
        source = s + 1 - 2 * (t % 2)
        return (t ^ 2, source) if 0 <= source < blocks else (t ^ 1, s)

    def body(slab_states, velocity, snap_of_step):
        start = slab_states[0]
        fields, depth, ny, nz = start.shape

        def shaped(*lead, rows=ny):
            return jax.ShapeDtypeStruct(lead + (rows, nz), jnp.float32)

        def room(*lead):
            return pltpu.VMEM(lead + (ny, nz), jnp.float32)

        layer = shaped(4)
        pieces = (shaped(4, rows=ny // slabs),) * slabs

        state = moved(start, lambda t, s: (t - 1, s))
        snaps_next = moved(snap_of_step, lambda t, s: (t - 1, s))
        message_one, message_two, flow_out = pl.pallas_call(
            start_kernel,
            out_shape=(layer, layer, shaped(velocity.shape[0])),
            in_specs=[hbm] * 3,
            out_specs=(vmem,) * 3,
            scratch_shapes=[
                pltpu.SMEM(snap_of_step.shape, jnp.int32),
                room(fields, edge_count),
                room(*velocity.shape[:2], 2),
                sem((5,)),
            ],
            compiler_params=params(56),
            cost_estimate=cost(2),
        )(snap_of_step, start, velocity)
        halo_one = exchanged(message_one, 0, 1)
        halo_two = exchanged(message_two, 1, 1)
        own_flow = moved(flow_out, fetched)
        other_flow = moved(own_flow, lambda t, s: (t ^ 1, s))
        widened, edges, halo = [None] * 2, [None] * 2, [halo_one, halo_two]
        for partner in (0, 1):
            widened[partner], edges[partner], message = pl.pallas_call(
                functools.partial(first_kernel, blocks, slabs, partner),
                out_shape=(shaped(fields, 4), shaped(fields, 2), layer),
                in_specs=[smem, smem] + [vmem] * 5 + [hbm],
                out_specs=(vmem,) * 3,
                scratch_shapes=[room(fields)],
                compiler_params=params(32),
                cost_estimate=cost(1.5),
            )(snap_of_step, snaps_next, state, halo[partner], own_flow, other_flow, velocity, start)
            halo[partner] = exchanged(message, partner, 0)
        carried_on, inner, *inner_pieces = pl.pallas_call(
            functools.partial(inner_kernel, slabs),
            out_shape=(shaped(fields, depth), shaped(fields, depth)) + pieces,
            in_specs=[smem, smem] + [vmem] * 6 + [hbm],
            out_specs=(vmem, hbm) + (vmem,) * slabs,
            scratch_shapes=[
                room(fields, depth), room(fields, depth + 2), room(fields, depth - 4), room(depth - 4), sem(()),
            ],
            compiler_params=params(32),
            cost_estimate=cost(3),
        )(snap_of_step, snaps_next, state, *widened, *edges, velocity, start)
        inner_parts = inner_pieces[:1] + [
            moved(inner_pieces[by], lambda t, s, by=by: (t + by, s)) for by in range(1, slabs)
        ]
        outer_one, total_one = pl.pallas_call(
            functools.partial(outer_kernel, blocks, slabs, 0),
            out_shape=(shaped(fields, 2), shaped(2)),
            in_specs=[smem] + [vmem] * 6,
            out_specs=(vmem,) * 2,
            scratch_shapes=[room(fields)],
            compiler_params=params(32),
            cost_estimate=cost(0.5),
        )(snap_of_step, edges[0], halo[0], own_flow, other_flow, carried_on, velocity)
        outer_two, *outer_pieces = pl.pallas_call(
            functools.partial(outer_kernel, blocks, slabs, 1),
            out_shape=(shaped(fields, 2),) + pieces,
            in_specs=[smem] + [vmem] * 7,
            out_specs=(vmem,) * (1 + slabs),
            scratch_shapes=[room(fields), room(2), room(edge_count)],
            compiler_params=params(32),
            cost_estimate=cost(0.5),
        )(snap_of_step, edges[1], halo[1], own_flow, other_flow, carried_on, velocity, total_one)
        outer_parts = outer_pieces[:1] + [
            moved(outer_pieces[by], lambda t, s, by=by: (t + by, s)) for by in range(1, slabs)
        ]
        final = pl.pallas_call(
            finish_kernel,
            out_shape=shaped(fields, depth),
            in_specs=[smem, vmem, vmem, vmem, vmem, hbm],
            out_specs=hbm,
            scratch_shapes=[room(fields, edge_count), sem((2,))],
            input_output_aliases={5: 0},
            compiler_params=params(32),
            cost_estimate=cost(1),
        )(snap_of_step, carried_on, outer_one, outer_two, velocity, inner)
        gradient = pl.pallas_call(
            sum_kernel,
            out_shape=shaped(depth, rows=ny // slabs),
            in_specs=[vmem] * (2 * slabs),
            out_specs=vmem,
            compiler_params=params(16),
            cost_estimate=cost(0.5),
        )(*inner_parts, *outer_parts)
        return (final[None], gradient)

    return jax.shard_map(
        body,
        mesh=mesh,
        in_specs=(P("tm", None, "space", None, None), P(None, None, "space", None, None), P("tm", None)),
        out_specs=(P("tm", None, "space", None, None), P("space", "tm", None)),
        check_vma=False,
    )
```

```python
import functools

import jax
import jax.numpy as jnp
from jax import lax
from jax.experimental import pallas as pl
from jax.experimental.pallas import tpu as pltpu
from jax.sharding import PartitionSpec as P

coupling = 0.3
diffusion = (0.14, 0.06)
sub, lanes = 8, 128
edge_count = 4


def tiles(shape):
    rows, cols = shape
    return [(i, j) for i in range(rows // sub) for j in range(cols // lanes)]


def spot(i, j):
    return (pl.ds(i * sub, sub), pl.ds(j * lanes, lanes))


def neighbours(at, i, j, shape):
    rows, cols = shape
    centre = at(i, j)
    row = lax.broadcasted_iota(jnp.int32, (sub, lanes), 0)
    col = lax.broadcasted_iota(jnp.int32, (sub, lanes), 1)
    zero = jnp.zeros_like(centre)
    after = at(i + 1, j) if (i + 1) * sub < rows else zero
    before = at(i - 1, j) if i > 0 else zero
    north = pltpu.roll(jnp.where(row == 0, after, centre), sub - 1, 0)
    south = pltpu.roll(jnp.where(row == sub - 1, before, centre), 1, 0)
    after = at(i, j + 1) if (j + 1) * lanes < cols else zero
    before = at(i, j - 1) if j > 0 else zero
    upper = pltpu.roll(jnp.where(col == 0, after, centre), lanes - 1, 1)
    lower = pltpu.roll(jnp.where(col == lanes - 1, before, centre), 1, 1)
    return centre, (north + south) + (upper + lower), north - south, upper - lower


def advanced(fields, pairs, flow, i, j, shape, wanted=(0, 1)):
    u, v, w = flow
    out = []
    for f in wanted:
        centre, total, dy, dz = neighbours(functools.partial(fields, f), i, j, shape)
        side_sum, side_diff = pairs(f, i, j)
        c = diffusion[f]
        moved = u * side_diff + v * dy + w * dz
        new = ((1.0 - 6.0 * c) * centre + c * (side_sum + total)) + 0.25 * moved
        if f == 0:
            new = new + coupling * fields(1, i, j)
        out.append(new)
    return out


def layer_of(ref, l):
    return lambda f, i, j: ref[(f, l) + spot(i, j)]


def flow_of(velocity, snap, l):
    return lambda i, j: [velocity[(snap, d, l) + spot(i, j)] for d in range(3)]


def full_layer(below, here, above, flow, shape, store, wanted=(0, 1)):
    def pairs(f, i, j):
        hi, lo = above(f, i, j), below(f, i, j)
        return hi + lo, hi - lo

    for i, j in tiles(shape):
        store(i, j, advanced(here, pairs, flow(i, j), i, j, shape, wanted))


def into(ref, l):
    def store(i, j, values):
        for f, value in enumerate(values):
            ref[(f, l) + spot(i, j)] = value

    return store


def side_of(partner):
    parity = lax.rem(lax.axis_index("space"), 2)
    high = 1 - parity if partner == 0 else parity
    return high, (2 * high - 1).astype(jnp.float32)


def side_layer(outer, here, inner, flow, sign, shape, store, wanted=(0, 1)):
    def pairs(f, i, j):
        far, near = outer(f, i, j), inner(f, i, j)
        return far + near, far - near

    for i, j in tiles(shape):
        u, v, w = flow(i, j)
        store(i, j, advanced(here, pairs, (sign * u, v, w), i, j, shape, wanted))


def pack(here, inner, flow, sign, message, shape):
    def pairs(f, i, j):
        value = inner(f, i, j)
        return value, value

    for i, j in tiles(shape):
        u, v, w = flow(i, j)
        out = advanced(here, pairs, (-sign * u, v, w), i, j, shape)
        for f in (0, 1):
            message[(f,) + spot(i, j)] = here(f, i, j)
            message[(2 + f,) + spot(i, j)] = out[f]


def take_halo(blocks, partner, halo, own, own_flow, other_flow, snap, now, after, shape):
    high, sign = side_of(partner)
    place = lax.axis_index("space")
    inside = jnp.logical_and(place > 0, place < blocks - 1)
    fetched = lax.rem(lax.axis_index("tm"), 2)
    for i, j in tiles(shape):
        u = jnp.where(high == fetched, own_flow[(snap,) + spot(i, j)], other_flow[(snap,) + spot(i, j)])
        for f in (0, 1):
            current = halo[(f,) + spot(i, j)]
            later = halo[(2 + f,) + spot(i, j)] + (diffusion[f] - (0.25 * sign) * u) * own(f, i, j)
            if partner == 1:
                current = jnp.where(inside, current, 0.0)
                later = jnp.where(inside, later, 0.0)
            now[(f,) + spot(i, j)] = current
            after[(f, 0) + spot(i, j)] = later


def plain(ref):
    return lambda f, i, j: ref[(f,) + spot(i, j)]


def split_rows(total, pieces):
    rows = total.shape[1] // len(pieces)
    for by, piece in enumerate(pieces):
        start = pl.multiple_of(lax.bitwise_xor(lax.axis_index("tm"), by) * rows, rows)
        piece[...] = total[:, pl.ds(start, rows), :] * 0.5


def each(low, high, run):
    def step(l, carry):
        run(l)
        return carry

    lax.fori_loop(low, high, step, 0)


def start_kernel(snaps, state, velocity, message_one, message_two, flow_out, scalars, edges, flows, sems):
    depth = state.shape[1]
    copies = [
        (snaps, scalars),
        (state.at[:, pl.ds(0, 2)], edges.at[:, pl.ds(0, 2)]),
        (state.at[:, pl.ds(depth - 2, 2)], edges.at[:, pl.ds(2, 2)]),
        (velocity.at[:, :, pl.ds(0, 1)], flows.at[:, :, pl.ds(0, 1)]),
        (velocity.at[:, :, pl.ds(depth - 1, 1)], flows.at[:, :, pl.ds(1, 1)]),
    ]
    copies = [pltpu.make_async_copy(*pair, sems.at[n]) for n, pair in enumerate(copies)]
    for copy in copies:
        copy.start()
    for copy in copies:
        copy.wait()
    for partner, message in enumerate((message_one, message_two)):
        high, sign = side_of(partner)
        here, inner = layer_of(edges, 3 * high), layer_of(edges, 1 + high)
        pack(here, inner, flow_of(flows, scalars[0, 1], high), sign, message, edges.shape[2:])
    flow_out[...] = flows[:, 0, 1 - lax.rem(lax.axis_index("tm"), 2)]


def first_kernel(blocks, slabs, partner, snaps, snaps_next, state, halo, own_flow, other_flow, velocity, start,
                 widened, edges, message, now):
    depth, shape = state.shape[1], state.shape[2:]
    last = lax.axis_index("tm") == slabs - 1
    high, sign = side_of(partner)

    def at(k):
        return high * (depth - 1) + k * (1 - 2 * high)

    @pl.when(last)
    def _():
        pltpu.sync_copy(start.at[:, pl.ds(at(0), 1)], edges.at[:, pl.ds(0, 1)])
        pltpu.sync_copy(start.at[:, pl.ds(at(1), 1)], edges.at[:, pl.ds(1, 1)])

    @pl.when(jnp.logical_not(last))
    def _():
        snap = snaps_next[0, 1]
        take_halo(blocks, partner, halo, layer_of(state, at(0)), own_flow, other_flow, snap, now, widened, shape)
        for k in range(3):
            outer = plain(now) if k == 0 else layer_of(state, at(k - 1))
            here, inner, flow = layer_of(state, at(k)), layer_of(state, at(k + 1)), flow_of(velocity, snap, at(k))
            side_layer(outer, here, inner, flow, sign, shape, into(widened, k + 1))
        for k in range(2):
            outer, here, inner = [layer_of(widened, k + n) for n in range(3)]
            flow = flow_of(velocity, snaps_next[0, 0], at(k))
            side_layer(outer, here, inner, flow, sign, shape, into(edges, k))

    pack(layer_of(edges, 0), layer_of(edges, 1), flow_of(velocity, snaps[0, 1], at(0)), sign, message, shape)


def inner_kernel(slabs, snaps, snaps_next, before, widened_one, widened_two, edges_one, edges_two, velocity, start,
                 carried_on, inner, kept, to_core, state, widened, final, total, sem):
    depth, shape = state.shape[1], state.shape[2:]
    last = lax.axis_index("tm") == slabs - 1

    @pl.when(last)
    def _():
        pltpu.sync_copy(start, state)

    @pl.when(jnp.logical_not(last))
    def _():
        for partner, wide, edges in ((0, widened_one, edges_one), (1, widened_two, edges_two)):
            high, unused = side_of(partner)
            for k in range(4):
                widened[:, high * (depth + 1) + k * (1 - 2 * high)] = wide[:, k]
            for k in range(2):
                state[:, high * (depth - 1) + k * (1 - 2 * high)] = edges[:, k]

        def first_step(l):
            flow = flow_of(velocity, snaps_next[0, 1], l)
            here = layer_of(before, l)
            full_layer(layer_of(before, l - 1), here, layer_of(before, l + 1), flow, shape, into(widened, l + 1))

        each(3, depth - 3, first_step)

        def second_step(l):
            flow = flow_of(velocity, snaps_next[0, 0], l)
            here = layer_of(widened, l + 1)
            full_layer(layer_of(widened, l), here, layer_of(widened, l + 2), flow, shape, into(state, l))

        each(2, depth - 2, second_step)

    def third_step(l):
        flow = flow_of(velocity, snaps[0, 1], l)
        here = layer_of(state, l)
        full_layer(layer_of(state, l - 1), here, layer_of(state, l + 1), flow, shape, into(carried_on, l))

    each(1, depth - 1, third_step)

    def fourth_step(l):
        def store(i, j, values):
            into(final, l - 2)(i, j, values)
            total[(l - 2,) + spot(i, j)] = carried_on[(0, l) + spot(i, j)] + values[0]

        flow = flow_of(velocity, snaps[0, 0], l)
        here = layer_of(carried_on, l)
        full_layer(layer_of(carried_on, l - 1), here, layer_of(carried_on, l + 1), flow, shape, store)

    each(2, depth - 2, fourth_step)
    copy = pltpu.make_async_copy(final, inner.at[:, pl.ds(2, depth - 4)], sem)
    copy.start()
    split_rows(total, [kept.at[0], to_core.at[0], kept.at[1], to_core.at[1]])
    copy.wait()


def chip_kernel(kept, from_core, own, across):
    own[...] = kept[0] + from_core[0]
    across[...] = kept[1] + from_core[1]


def last_steps(partner, snaps, carried_on, outer, velocity, store, wanted):
    depth, shape = carried_on.shape[1], carried_on.shape[2:]
    high, sign = side_of(partner)

    def at(k):
        return high * (depth - 1) + k * (1 - 2 * high)

    ring = [layer_of(outer, 0), layer_of(outer, 1), layer_of(carried_on, at(1)), layer_of(carried_on, at(2))]
    for k in range(2):
        flow = flow_of(velocity, snaps[0, 0], at(k))
        keep = functools.partial(store, k, ring[k + 1])
        side_layer(ring[k], ring[k + 1], ring[k + 2], flow, sign, shape, keep, wanted)


def outer_kernel(blocks, slabs, partner, snaps, edges, halo, own_flow, other_flow, carried_on, velocity, *rest):
    before, rest = rest[:partner], rest[partner:]
    if partner == 0:
        outer, total, now = rest
    else:
        outer, pieces, (now, total, whole) = rest[0], rest[1 : slabs + 1], rest[slabs + 1 :]
    depth, shape = carried_on.shape[1], carried_on.shape[2:]
    high, sign = side_of(partner)
    snap = snaps[0, 1]
    take_halo(blocks, partner, halo, layer_of(edges, 0), own_flow, other_flow, snap, now, outer, shape)
    flow = flow_of(velocity, snap, high * (depth - 1))
    side_layer(plain(now), layer_of(edges, 0), layer_of(edges, 1), flow, sign, shape, into(outer, 1))

    def store(k, here, i, j, values):
        total[(k,) + spot(i, j)] = here(0, i, j) + values[0]

    last_steps(partner, snaps, carried_on, outer, velocity, store, (0,))
    if partner == 1:
        for k in range(2):
            whole[high * (edge_count - 1) + k * (1 - 2 * high)] = total[k]
            whole[(1 - high) * (edge_count - 1) - k * (1 - 2 * high)] = before[0][k]
        split_rows(whole, pieces)


def finish_kernel(snaps, carried_on, outer_one, outer_two, velocity, inner, out, final, sems):
    depth = carried_on.shape[1]
    for partner, outer in enumerate((outer_one, outer_two)):
        high, unused = side_of(partner)

        def store(k, here, i, j, values, high=high):
            into(final, high * (edge_count - 1) + k * (1 - 2 * high))(i, j, values)

        last_steps(partner, snaps, carried_on, outer, velocity, store, (0, 1))
    copies = [
        pltpu.make_async_copy(final.at[:, pl.ds(0, 2)], out.at[:, pl.ds(0, 2)], sems.at[0]),
        pltpu.make_async_copy(final.at[:, pl.ds(2, 2)], out.at[:, pl.ds(depth - 2, 2)], sems.at[1]),
    ]
    for copy in copies:
        copy.start()
    for copy in copies:
        copy.wait()


def sum_kernel(inner, inner_across, *refs):
    parts, out = refs[:-1], refs[-1]
    depth = out.shape[0]
    outer = functools.reduce(jnp.add, [part[...] for part in parts])
    out[2 : depth - 2] = inner[...] + inner_across[...]
    out[0:2] = outer[0:2]
    out[depth - 2 : depth] = outer[2:4]


def solution(mesh):
    slabs, blocks = mesh.shape["tm"], mesh.shape["space"]
    vmem, smem = pl.BlockSpec(memory_space=pltpu.VMEM), pl.BlockSpec(memory_space=pltpu.SMEM)
    hbm = pl.BlockSpec(memory_space=pltpu.HBM)
    sem = pltpu.SemaphoreType.DMA

    def params(mebibytes):
        return pltpu.CompilerParams(vmem_limit_bytes=mebibytes * 1024 * 1024)

    def cost(microseconds):
        return pl.CostEstimate(flops=0, bytes_accessed=int(microseconds * 3.6e6), transcendentals=0)

    def index(t, s):
        return (t % slabs) * blocks + s % blocks

    def moved(array, to):
        pairs = [(index(t, s), index(*to(t, s))) for t in range(slabs) for s in range(blocks)]
        return lax.ppermute(array, ("tm", "space"), pairs)

    def exchanged(array, by, earlier):
        def to(t, s):
            partner = ((s + by) ^ 1) - by
            return (t - earlier, partner) if 0 <= partner < blocks else (t ^ 1, s)

        return moved(array, to)

    def fetched(t, s):
        source = s + 1 - 2 * (t % 2)
        return (t ^ 2, source) if 0 <= source < blocks else (t ^ 1, s)

    def body(slab_states, velocity, snap_of_step):
        start = slab_states[0]
        fields, depth, ny, nz = start.shape

        def shaped(*lead, rows=ny):
            return jax.ShapeDtypeStruct(lead + (rows, nz), jnp.float32)

        def room(*lead):
            return pltpu.VMEM(lead + (ny, nz), jnp.float32)

        layer = shaped(4)
        pieces = (shaped(4, rows=ny // slabs),) * slabs

        state = moved(start, lambda t, s: (t - 1, s))
        snaps_next = moved(snap_of_step, lambda t, s: (t - 1, s))
        message_one, message_two, flow_out = pl.pallas_call(
            start_kernel,
            out_shape=(layer, layer, shaped(velocity.shape[0])),
            in_specs=[hbm] * 3,
            out_specs=(vmem,) * 3,
            scratch_shapes=[
                pltpu.SMEM(snap_of_step.shape, jnp.int32),
                room(fields, edge_count),
                room(*velocity.shape[:2], 2),
                sem((5,)),
            ],
            compiler_params=params(56),
            cost_estimate=cost(2),
        )(snap_of_step, start, velocity)
        halo_one = exchanged(message_one, 0, 1)
        halo_two = exchanged(message_two, 1, 1)
        own_flow = moved(flow_out, fetched)
        other_flow = moved(own_flow, lambda t, s: (t ^ 1, s))
        widened, edges, halo = [None] * 2, [None] * 2, [halo_one, halo_two]
        for partner in (0, 1):
            widened[partner], edges[partner], message = pl.pallas_call(
                functools.partial(first_kernel, blocks, slabs, partner),
                out_shape=(shaped(fields, 4), shaped(fields, 2), layer),
                in_specs=[smem, smem] + [vmem] * 5 + [hbm],
                out_specs=(vmem,) * 3,
                scratch_shapes=[room(fields)],
                compiler_params=params(32),
                cost_estimate=cost(1.5),
            )(snap_of_step, snaps_next, state, halo[partner], own_flow, other_flow, velocity, start)
            halo[partner] = exchanged(message, partner, 0)
        pair = jax.ShapeDtypeStruct((2,) + pieces[0].shape, jnp.float32)
        carried_on, inner, kept, to_core = pl.pallas_call(
            functools.partial(inner_kernel, slabs),
            out_shape=(shaped(fields, depth), shaped(fields, depth), pair, pair),
            in_specs=[smem, smem] + [vmem] * 6 + [hbm],
            out_specs=(vmem, hbm, vmem, vmem),
            scratch_shapes=[
                room(fields, depth), room(fields, depth + 2), room(fields, depth - 4), room(depth - 4), sem(()),
            ],
            compiler_params=params(32),
            cost_estimate=cost(3),
        )(snap_of_step, snaps_next, state, *widened, *edges, velocity, start)
        inner_own, inner_across = pl.pallas_call(
            chip_kernel,
            out_shape=pieces[:2],
            in_specs=[vmem, vmem],
            out_specs=(vmem, vmem),
            compiler_params=params(16),
            cost_estimate=cost(0.5),
        )(kept, moved(to_core, lambda t, s: (t ^ 1, s)))
        inner_across = moved(inner_across, lambda t, s: (t ^ 2, s))
        outer_one, total_one = pl.pallas_call(
            functools.partial(outer_kernel, blocks, slabs, 0),
            out_shape=(shaped(fields, 2), shaped(2)),
            in_specs=[smem] + [vmem] * 6,
            out_specs=(vmem,) * 2,
            scratch_shapes=[room(fields)],
            compiler_params=params(32),
            cost_estimate=cost(0.5),
        )(snap_of_step, edges[0], halo[0], own_flow, other_flow, carried_on, velocity)
        outer_two, *outer_pieces = pl.pallas_call(
            functools.partial(outer_kernel, blocks, slabs, 1),
            out_shape=(shaped(fields, 2),) + pieces,
            in_specs=[smem] + [vmem] * 7,
            out_specs=(vmem,) * (1 + slabs),
            scratch_shapes=[room(fields), room(2), room(edge_count)],
            compiler_params=params(32),
            cost_estimate=cost(0.5),
        )(snap_of_step, edges[1], halo[1], own_flow, other_flow, carried_on, velocity, total_one)
        outer_parts = outer_pieces[:1] + [
            moved(outer_pieces[by], lambda t, s, by=by: (t ^ by, s)) for by in range(1, slabs)
        ]
        final = pl.pallas_call(
            finish_kernel,
            out_shape=shaped(fields, depth),
            in_specs=[smem, vmem, vmem, vmem, vmem, hbm],
            out_specs=hbm,
            scratch_shapes=[room(fields, edge_count), sem((2,))],
            input_output_aliases={5: 0},
            compiler_params=params(32),
            cost_estimate=cost(1),
        )(snap_of_step, carried_on, outer_one, outer_two, velocity, inner)
        gradient = pl.pallas_call(
            sum_kernel,
            out_shape=shaped(depth, rows=ny // slabs),
            in_specs=[vmem] * (2 + slabs),
            out_specs=vmem,
            compiler_params=params(16),
            cost_estimate=cost(0.5),
        )(inner_own, inner_across, *outer_parts)
        return (final[None], gradient)

    return jax.shard_map(
        body,
        mesh=mesh,
        in_specs=(P("tm", None, "space", None, None), P(None, None, "space", None, None), P("tm", None)),
        out_specs=(P("tm", None, "space", None, None), P("space", "tm", None)),
        check_vma=False,
    )
```

```python
import functools

import jax
import jax.numpy as jnp
from jax import lax
from jax.experimental import pallas as pl
from jax.experimental.pallas import tpu as pltpu
from jax.sharding import PartitionSpec as P

coupling = 0.3
diffusion = (0.14, 0.06)
sub, lanes = 8, 128
edge_count = 4


def tiles(shape):
    rows, cols = shape
    return [(i, j) for i in range(rows // sub) for j in range(cols // lanes)]


def spot(i, j):
    return (pl.ds(i * sub, sub), pl.ds(j * lanes, lanes))


def neighbours(at, i, j, shape):
    rows, cols = shape
    centre = at(i, j)
    row = lax.broadcasted_iota(jnp.int32, (sub, lanes), 0)
    col = lax.broadcasted_iota(jnp.int32, (sub, lanes), 1)
    zero = jnp.zeros_like(centre)
    after = at(i + 1, j) if (i + 1) * sub < rows else zero
    before = at(i - 1, j) if i > 0 else zero
    north = pltpu.roll(jnp.where(row == 0, after, centre), sub - 1, 0)
    south = pltpu.roll(jnp.where(row == sub - 1, before, centre), 1, 0)
    after = at(i, j + 1) if (j + 1) * lanes < cols else zero
    before = at(i, j - 1) if j > 0 else zero
    upper = pltpu.roll(jnp.where(col == 0, after, centre), lanes - 1, 1)
    lower = pltpu.roll(jnp.where(col == lanes - 1, before, centre), 1, 1)
    return centre, (north + south) + (upper + lower), north - south, upper - lower


def advanced(fields, pairs, flow, i, j, shape, wanted=(0, 1)):
    u, v, w = flow
    out = []
    for f in wanted:
        centre, total, dy, dz = neighbours(functools.partial(fields, f), i, j, shape)
        side_sum, side_diff = pairs(f, i, j)
        c = diffusion[f]
        moved = u * side_diff + v * dy + w * dz
        new = ((1.0 - 6.0 * c) * centre + c * (side_sum + total)) + 0.25 * moved
        if f == 0:
            new = new + coupling * fields(1, i, j)
        out.append(new)
    return out


def layer_of(ref, l):
    return lambda f, i, j: ref[(f, l) + spot(i, j)]


def flow_of(velocity, snap, l):
    return lambda i, j: [velocity[(snap, d, l) + spot(i, j)] for d in range(3)]


def full_layer(below, here, above, flow, shape, store, wanted=(0, 1)):
    def pairs(f, i, j):
        hi, lo = above(f, i, j), below(f, i, j)
        return hi + lo, hi - lo

    for i, j in tiles(shape):
        store(i, j, advanced(here, pairs, flow(i, j), i, j, shape, wanted))


def into(ref, l):
    def store(i, j, values):
        for f, value in enumerate(values):
            ref[(f, l) + spot(i, j)] = value

    return store


def side_of(partner):
    parity = lax.rem(lax.axis_index("space"), 2)
    high = 1 - parity if partner == 0 else parity
    return high, (2 * high - 1).astype(jnp.float32)


def side_layer(outer, here, inner, flow, sign, shape, store, wanted=(0, 1)):
    def pairs(f, i, j):
        far, near = outer(f, i, j), inner(f, i, j)
        return far + near, far - near

    for i, j in tiles(shape):
        u, v, w = flow(i, j)
        store(i, j, advanced(here, pairs, (sign * u, v, w), i, j, shape, wanted))


def pack(here, inner, flow, sign, message, shape, rest=None):
    def pairs(f, i, j):
        value = inner(f, i, j)
        return value, value

    for i, j in tiles(shape):
        u, v, w = flow(i, j)
        out = advanced(here, pairs, (-sign * u, v, w), i, j, shape)
        for f in (0, 1):
            message[(f,) + spot(i, j)] = here(f, i, j)
            into_message = message.at[2 + f] if f == 0 or rest is None else rest.at[0]
            into_message[spot(i, j)] = out[f]


def take_halo(blocks, partner, halo, own, own_flow, other_flow, snap, now, after, shape):
    high, sign = side_of(partner)
    place = lax.axis_index("space")
    inside = jnp.logical_and(place > 0, place < blocks - 1)
    fetched = lax.rem(lax.axis_index("tm"), 2)
    for i, j in tiles(shape):
        u = jnp.where(high == fetched, own_flow[(snap,) + spot(i, j)], other_flow[(snap,) + spot(i, j)])
        for f in (0, 1):
            current = halo[(f,) + spot(i, j)]
            if partner == 1:
                current = jnp.where(inside, current, 0.0)
            now[(f,) + spot(i, j)] = current
            if 2 + f < halo.shape[0]:
                later = halo[(2 + f,) + spot(i, j)] + (diffusion[f] - (0.25 * sign) * u) * own(f, i, j)
                if partner == 1:
                    later = jnp.where(inside, later, 0.0)
                after[(f, 0) + spot(i, j)] = later


def plain(ref):
    return lambda f, i, j: ref[(f,) + spot(i, j)]


def split_rows(total, pieces):
    rows = total.shape[1] // len(pieces)
    for by, piece in enumerate(pieces):
        start = pl.multiple_of(lax.bitwise_xor(lax.axis_index("tm"), by) * rows, rows)
        piece[...] = total[:, pl.ds(start, rows), :] * 0.5


def each(low, high, run):
    def step(l, carry):
        run(l)
        return carry

    lax.fori_loop(low, high, step, 0)


def start_kernel(snaps, state, velocity, message_one, message_two, flow_out, scalars, edges, flows, sems):
    depth = state.shape[1]
    copies = [
        (snaps, scalars),
        (state.at[:, pl.ds(0, 2)], edges.at[:, pl.ds(0, 2)]),
        (state.at[:, pl.ds(depth - 2, 2)], edges.at[:, pl.ds(2, 2)]),
        (velocity.at[:, :, pl.ds(0, 1)], flows.at[:, :, pl.ds(0, 1)]),
        (velocity.at[:, :, pl.ds(depth - 1, 1)], flows.at[:, :, pl.ds(1, 1)]),
    ]
    copies = [pltpu.make_async_copy(*pair, sems.at[n]) for n, pair in enumerate(copies)]
    for copy in copies:
        copy.start()
    for copy in copies:
        copy.wait()
    for partner, message in enumerate((message_one, message_two)):
        high, sign = side_of(partner)
        here, inner = layer_of(edges, 3 * high), layer_of(edges, 1 + high)
        pack(here, inner, flow_of(flows, scalars[0, 1], high), sign, message, edges.shape[2:])
    flow_out[...] = flows[:, 0, 1 - lax.rem(lax.axis_index("tm"), 2)]


def first_kernel(blocks, slabs, partner, snaps, snaps_next, state, halo, own_flow, other_flow, velocity, start,
                 widened, edges, message, rest, now):
    depth, shape = state.shape[1], state.shape[2:]
    last = lax.axis_index("tm") == slabs - 1
    high, sign = side_of(partner)

    def at(k):
        return high * (depth - 1) + k * (1 - 2 * high)

    @pl.when(last)
    def _():
        pltpu.sync_copy(start.at[:, pl.ds(at(0), 1)], edges.at[:, pl.ds(0, 1)])
        pltpu.sync_copy(start.at[:, pl.ds(at(1), 1)], edges.at[:, pl.ds(1, 1)])

    @pl.when(jnp.logical_not(last))
    def _():
        snap = snaps_next[0, 1]
        take_halo(blocks, partner, halo, layer_of(state, at(0)), own_flow, other_flow, snap, now, widened, shape)
        for k in range(3):
            outer = plain(now) if k == 0 else layer_of(state, at(k - 1))
            here, inner, flow = layer_of(state, at(k)), layer_of(state, at(k + 1)), flow_of(velocity, snap, at(k))
            side_layer(outer, here, inner, flow, sign, shape, into(widened, k + 1))
        for k in range(2):
            outer, here, inner = [layer_of(widened, k + n) for n in range(3)]
            flow = flow_of(velocity, snaps_next[0, 0], at(k))
            side_layer(outer, here, inner, flow, sign, shape, into(edges, k))

    pack(layer_of(edges, 0), layer_of(edges, 1), flow_of(velocity, snaps[0, 1], at(0)), sign, message, shape, rest)


def inner_kernel(slabs, snaps, snaps_next, before, widened_one, widened_two, edges_one, edges_two, velocity, start,
                 carried_on, inner, kept, to_core, state, widened, final, total, sem):
    depth, shape = state.shape[1], state.shape[2:]
    last = lax.axis_index("tm") == slabs - 1

    @pl.when(last)
    def _():
        pltpu.sync_copy(start, state)

    @pl.when(jnp.logical_not(last))
    def _():
        for partner, wide, edges in ((0, widened_one, edges_one), (1, widened_two, edges_two)):
            high, unused = side_of(partner)
            for k in range(4):
                widened[:, high * (depth + 1) + k * (1 - 2 * high)] = wide[:, k]
            for k in range(2):
                state[:, high * (depth - 1) + k * (1 - 2 * high)] = edges[:, k]

        def first_step(l):
            flow = flow_of(velocity, snaps_next[0, 1], l)
            here = layer_of(before, l)
            full_layer(layer_of(before, l - 1), here, layer_of(before, l + 1), flow, shape, into(widened, l + 1))

        each(3, depth - 3, first_step)

        def second_step(l):
            flow = flow_of(velocity, snaps_next[0, 0], l)
            here = layer_of(widened, l + 1)
            full_layer(layer_of(widened, l), here, layer_of(widened, l + 2), flow, shape, into(state, l))

        each(2, depth - 2, second_step)

    def third_step(l):
        flow = flow_of(velocity, snaps[0, 1], l)
        here = layer_of(state, l)
        full_layer(layer_of(state, l - 1), here, layer_of(state, l + 1), flow, shape, into(carried_on, l))

    each(1, depth - 1, third_step)

    def fourth_step(l):
        def store(i, j, values):
            into(final, l - 2)(i, j, values)
            total[(l - 2,) + spot(i, j)] = carried_on[(0, l) + spot(i, j)] + values[0]

        flow = flow_of(velocity, snaps[0, 0], l)
        here = layer_of(carried_on, l)
        full_layer(layer_of(carried_on, l - 1), here, layer_of(carried_on, l + 1), flow, shape, store)

    each(2, depth - 2, fourth_step)
    copy = pltpu.make_async_copy(final, inner.at[:, pl.ds(2, depth - 4)], sem)
    copy.start()
    split_rows(total, [kept.at[0], to_core.at[0], kept.at[1], to_core.at[1]])
    copy.wait()


def chip_kernel(kept, from_core, own, across):
    own[...] = kept[0] + from_core[0]
    across[...] = kept[1] + from_core[1]


def last_steps(partner, snaps, carried_on, outer, velocity, store, wanted, beyond=None):
    depth, shape = carried_on.shape[1], carried_on.shape[2:]
    high, sign = side_of(partner)

    def at(k):
        return high * (depth - 1) + k * (1 - 2 * high)

    ring = [layer_of(outer, 0), layer_of(outer, 1), layer_of(carried_on, at(1)), layer_of(carried_on, at(2))]
    if beyond is not None:
        ring[0] = beyond
    for k in range(2):
        flow = flow_of(velocity, snaps[0, 0], at(k))
        keep = functools.partial(store, k, ring[k + 1])
        side_layer(ring[k], ring[k + 1], ring[k + 2], flow, sign, shape, keep, wanted)


def outer_kernel(blocks, slabs, partner, snaps, edges, halo, own_flow, other_flow, carried_on, velocity, *rest):
    before, rest = rest[:partner], rest[partner:]
    if partner == 0:
        outer, total, now = rest
    else:
        outer, pieces, (now, total, whole) = rest[0], rest[1 : slabs + 1], rest[slabs + 1 :]
    depth, shape = carried_on.shape[1], carried_on.shape[2:]
    high, sign = side_of(partner)
    snap = snaps[0, 1]
    take_halo(blocks, partner, halo, layer_of(edges, 0), own_flow, other_flow, snap, now, outer, shape)
    flow = flow_of(velocity, snap, high * (depth - 1))
    side_layer(plain(now), layer_of(edges, 0), layer_of(edges, 1), flow, sign, shape, into(outer, 1))

    def store(k, here, i, j, values):
        total[(k,) + spot(i, j)] = here(0, i, j) + values[0]

    last_steps(partner, snaps, carried_on, outer, velocity, store, (0,))
    if partner == 1:
        for k in range(2):
            whole[high * (edge_count - 1) + k * (1 - 2 * high)] = total[k]
            whole[(1 - high) * (edge_count - 1) - k * (1 - 2 * high)] = before[0][k]
        split_rows(whole, pieces)


def finish_kernel(blocks, snaps, carried_on, outer_one, outer_two, edges_one, edges_two, rest_one, rest_two,
                  own_flow, other_flow, velocity, inner, out, final, later, sems):
    depth, shape = carried_on.shape[1], carried_on.shape[2:]
    place = lax.axis_index("space")
    inside = jnp.logical_and(place > 0, place < blocks - 1)
    fetched = lax.rem(lax.axis_index("tm"), 2)
    for partner, outer, edges, rest in ((0, outer_one, edges_one, rest_one), (1, outer_two, edges_two, rest_two)):
        high, sign = side_of(partner)
        for i, j in tiles(shape):
            at = (snaps[0, 1],) + spot(i, j)
            u = jnp.where(high == fetched, own_flow[at], other_flow[at])
            value = rest[(0,) + spot(i, j)] + (diffusion[1] - (0.25 * sign) * u) * edges[(1, 0) + spot(i, j)]
            later[(partner,) + spot(i, j)] = value if partner == 0 else jnp.where(inside, value, 0.0)

        def beyond(f, i, j, outer=outer, partner=partner):
            return later[(partner,) + spot(i, j)] if f == 1 else outer[(0, 0) + spot(i, j)]

        def store(k, here, i, j, values, high=high):
            into(final, high * (edge_count - 1) + k * (1 - 2 * high))(i, j, values)

        last_steps(partner, snaps, carried_on, outer, velocity, store, (0, 1), beyond)
    copies = [
        pltpu.make_async_copy(final.at[:, pl.ds(0, 2)], out.at[:, pl.ds(0, 2)], sems.at[0]),
        pltpu.make_async_copy(final.at[:, pl.ds(2, 2)], out.at[:, pl.ds(depth - 2, 2)], sems.at[1]),
    ]
    for copy in copies:
        copy.start()
    for copy in copies:
        copy.wait()


def sum_kernel(inner, inner_across, *refs):
    parts, out = refs[:-1], refs[-1]
    depth = out.shape[0]
    outer = functools.reduce(jnp.add, [part[...] for part in parts])
    out[2 : depth - 2] = inner[...] + inner_across[...]
    out[0:2] = outer[0:2]
    out[depth - 2 : depth] = outer[2:4]


def solution(mesh):
    slabs, blocks = mesh.shape["tm"], mesh.shape["space"]
    vmem, smem = pl.BlockSpec(memory_space=pltpu.VMEM), pl.BlockSpec(memory_space=pltpu.SMEM)
    hbm = pl.BlockSpec(memory_space=pltpu.HBM)
    sem = pltpu.SemaphoreType.DMA

    def params(mebibytes):
        return pltpu.CompilerParams(vmem_limit_bytes=mebibytes * 1024 * 1024)

    def cost(microseconds):
        return pl.CostEstimate(flops=0, bytes_accessed=int(microseconds * 3.6e6), transcendentals=0)

    def index(t, s):
        return (t % slabs) * blocks + s % blocks

    def moved(array, to):
        pairs = [(index(t, s), index(*to(t, s))) for t in range(slabs) for s in range(blocks)]
        return lax.ppermute(array, ("tm", "space"), pairs)

    def exchanged(array, by, earlier):
        def to(t, s):
            partner = ((s + by) ^ 1) - by
            return (t - earlier, partner) if 0 <= partner < blocks else (t ^ 1, s)

        return moved(array, to)

    def fetched(t, s):
        source = s + 1 - 2 * (t % 2)
        return (t ^ 2, source) if 0 <= source < blocks else (t ^ 1, s)

    def body(slab_states, velocity, snap_of_step):
        start = slab_states[0]
        fields, depth, ny, nz = start.shape

        def shaped(*lead, rows=ny):
            return jax.ShapeDtypeStruct(lead + (rows, nz), jnp.float32)

        def room(*lead):
            return pltpu.VMEM(lead + (ny, nz), jnp.float32)

        layer = shaped(4)
        pieces = (shaped(4, rows=ny // slabs),) * slabs

        state = moved(start, lambda t, s: (t - 1, s))
        snaps_next = moved(snap_of_step, lambda t, s: (t - 1, s))
        message_one, message_two, flow_out = pl.pallas_call(
            start_kernel,
            out_shape=(layer, layer, shaped(velocity.shape[0])),
            in_specs=[hbm] * 3,
            out_specs=(vmem,) * 3,
            scratch_shapes=[
                pltpu.SMEM(snap_of_step.shape, jnp.int32),
                room(fields, edge_count),
                room(*velocity.shape[:2], 2),
                sem((5,)),
            ],
            compiler_params=params(56),
            cost_estimate=cost(2),
        )(snap_of_step, start, velocity)
        halo_one = exchanged(message_one, 0, 1)
        halo_two = exchanged(message_two, 1, 1)
        own_flow = moved(flow_out, fetched)
        other_flow = moved(own_flow, lambda t, s: (t ^ 1, s))
        widened, edges, halo, halo_rest = [None] * 2, [None] * 2, [halo_one, halo_two], [None] * 2
        for partner in (0, 1):
            widened[partner], edges[partner], message, rest = pl.pallas_call(
                functools.partial(first_kernel, blocks, slabs, partner),
                out_shape=(shaped(fields, 4), shaped(fields, 2), shaped(3), shaped(1)),
                in_specs=[smem, smem] + [vmem] * 5 + [hbm],
                out_specs=(vmem,) * 4,
                scratch_shapes=[room(fields)],
                compiler_params=params(32),
                cost_estimate=cost(1.5),
            )(snap_of_step, snaps_next, state, halo[partner], own_flow, other_flow, velocity, start)
            halo[partner] = exchanged(message, partner, 0)
            halo_rest[partner] = exchanged(rest, partner, 0)
        pair = jax.ShapeDtypeStruct((2,) + pieces[0].shape, jnp.float32)
        carried_on, inner, kept, to_core = pl.pallas_call(
            functools.partial(inner_kernel, slabs),
            out_shape=(shaped(fields, depth), shaped(fields, depth), pair, pair),
            in_specs=[smem, smem] + [vmem] * 6 + [hbm],
            out_specs=(vmem, hbm, vmem, vmem),
            scratch_shapes=[
                room(fields, depth), room(fields, depth + 2), room(fields, depth - 4), room(depth - 4), sem(()),
            ],
            compiler_params=params(32),
            cost_estimate=cost(3),
        )(snap_of_step, snaps_next, state, *widened, *edges, velocity, start)
        inner_own, inner_across = pl.pallas_call(
            chip_kernel,
            out_shape=pieces[:2],
            in_specs=[vmem, vmem],
            out_specs=(vmem, vmem),
            compiler_params=params(16),
            cost_estimate=cost(0.5),
        )(kept, moved(to_core, lambda t, s: (t ^ 1, s)))
        inner_across = moved(inner_across, lambda t, s: (t ^ 2, s))
        outer_one, total_one = pl.pallas_call(
            functools.partial(outer_kernel, blocks, slabs, 0),
            out_shape=(shaped(fields, 2), shaped(2)),
            in_specs=[smem] + [vmem] * 6,
            out_specs=(vmem,) * 2,
            scratch_shapes=[room(fields)],
            compiler_params=params(32),
            cost_estimate=cost(0.5),
        )(snap_of_step, edges[0], halo[0], own_flow, other_flow, carried_on, velocity)
        outer_two, *outer_pieces = pl.pallas_call(
            functools.partial(outer_kernel, blocks, slabs, 1),
            out_shape=(shaped(fields, 2),) + pieces,
            in_specs=[smem] + [vmem] * 7,
            out_specs=(vmem,) * (1 + slabs),
            scratch_shapes=[room(fields), room(2), room(edge_count)],
            compiler_params=params(32),
            cost_estimate=cost(0.5),
        )(snap_of_step, edges[1], halo[1], own_flow, other_flow, carried_on, velocity, total_one)
        outer_parts = outer_pieces[:1] + [
            moved(outer_pieces[by], lambda t, s, by=by: (t ^ by, s)) for by in range(1, slabs)
        ]
        final = pl.pallas_call(
            functools.partial(finish_kernel, blocks),
            out_shape=shaped(fields, depth),
            in_specs=[smem] + [vmem] * 10 + [hbm],
            out_specs=hbm,
            scratch_shapes=[room(fields, edge_count), room(2), sem((2,))],
            input_output_aliases={11: 0},
            compiler_params=params(32),
            cost_estimate=cost(1),
        )(snap_of_step, carried_on, outer_one, outer_two, *edges, *halo_rest, own_flow, other_flow, velocity, inner)
        gradient = pl.pallas_call(
            sum_kernel,
            out_shape=shaped(depth, rows=ny // slabs),
            in_specs=[vmem] * (2 + slabs),
            out_specs=vmem,
            compiler_params=params(16),
            cost_estimate=cost(0.5),
        )(inner_own, inner_across, *outer_parts)
        return (final[None], gradient)

    return jax.shard_map(
        body,
        mesh=mesh,
        in_specs=(P("tm", None, "space", None, None), P(None, None, "space", None, None), P("tm", None)),
        out_specs=(P("tm", None, "space", None, None), P("space", "tm", None)),
        check_vma=False,
    )
```

```python
import functools

import jax
import jax.numpy as jnp
from jax import lax
from jax.experimental import pallas as pl
from jax.experimental.pallas import tpu as pltpu
from jax.sharding import PartitionSpec as P

coupling = 0.3
diffusion = (0.14, 0.06)
sub, lanes = 8, 128
edge_count = 4


def tiles(shape):
    rows, cols = shape
    return [(i, j) for i in range(rows // sub) for j in range(cols // lanes)]


def spot(i, j):
    return (pl.ds(i * sub, sub), pl.ds(j * lanes, lanes))


def neighbours(at, i, j, shape):
    rows, cols = shape
    centre = at(i, j)
    row = lax.broadcasted_iota(jnp.int32, (sub, lanes), 0)
    col = lax.broadcasted_iota(jnp.int32, (sub, lanes), 1)
    zero = jnp.zeros_like(centre)
    after = at(i + 1, j) if (i + 1) * sub < rows else zero
    before = at(i - 1, j) if i > 0 else zero
    north = pltpu.roll(jnp.where(row == 0, after, centre), sub - 1, 0)
    south = pltpu.roll(jnp.where(row == sub - 1, before, centre), 1, 0)
    after = at(i, j + 1) if (j + 1) * lanes < cols else zero
    before = at(i, j - 1) if j > 0 else zero
    upper = pltpu.roll(jnp.where(col == 0, after, centre), lanes - 1, 1)
    lower = pltpu.roll(jnp.where(col == lanes - 1, before, centre), 1, 1)
    return centre, (north + south) + (upper + lower), north - south, upper - lower


def advanced(fields, pairs, flow, i, j, shape, wanted=(0, 1)):
    u, v, w = flow
    out = []
    for f in wanted:
        centre, total, dy, dz = neighbours(functools.partial(fields, f), i, j, shape)
        side_sum, side_diff = pairs(f, i, j)
        c = diffusion[f]
        moved = u * side_diff + v * dy + w * dz
        new = ((1.0 - 6.0 * c) * centre + c * (side_sum + total)) + 0.25 * moved
        if f == 0:
            new = new + coupling * fields(1, i, j)
        out.append(new)
    return out


def layer_of(ref, l):
    return lambda f, i, j: ref[(f, l) + spot(i, j)]


def flow_of(velocity, snap, l):
    return lambda i, j: [velocity[(snap, d, l) + spot(i, j)] for d in range(3)]


def full_layer(below, here, above, flow, shape, store, wanted=(0, 1)):
    def pairs(f, i, j):
        hi, lo = above(f, i, j), below(f, i, j)
        return hi + lo, hi - lo

    for i, j in tiles(shape):
        store(i, j, advanced(here, pairs, flow(i, j), i, j, shape, wanted))


def into(ref, l):
    def store(i, j, values):
        for f, value in enumerate(values):
            ref[(f, l) + spot(i, j)] = value

    return store


def side_of(partner):
    parity = lax.rem(lax.axis_index("space"), 2)
    high = 1 - parity if partner == 0 else parity
    return high, (2 * high - 1).astype(jnp.float32)


def side_layer(outer, here, inner, flow, sign, shape, store, wanted=(0, 1)):
    def pairs(f, i, j):
        far, near = outer(f, i, j), inner(f, i, j)
        return far + near, far - near

    for i, j in tiles(shape):
        u, v, w = flow(i, j)
        store(i, j, advanced(here, pairs, (sign * u, v, w), i, j, shape, wanted))


def pack(here, inner, flow, sign, message, shape, rest=None):
    def pairs(f, i, j):
        value = inner(f, i, j)
        return value, value

    for i, j in tiles(shape):
        u, v, w = flow(i, j)
        out = advanced(here, pairs, (-sign * u, v, w), i, j, shape)
        for f in (0, 1):
            message[(f,) + spot(i, j)] = here(f, i, j)
            into_message = message.at[2 + f] if f == 0 or rest is None else rest.at[0]
            into_message[spot(i, j)] = out[f]


def take_halo(blocks, partner, halo, own, own_flow, other_flow, snap, now, after, shape):
    high, sign = side_of(partner)
    place = lax.axis_index("space")
    inside = jnp.logical_and(place > 0, place < blocks - 1)
    fetched = lax.rem(lax.axis_index("tm"), 2)
    for i, j in tiles(shape):
        u = jnp.where(high == fetched, own_flow[(snap,) + spot(i, j)], other_flow[(snap,) + spot(i, j)])
        for f in (0, 1):
            current = halo[(f,) + spot(i, j)]
            if partner == 1:
                current = jnp.where(inside, current, 0.0)
            now[(f,) + spot(i, j)] = current
            if 2 + f < halo.shape[0]:
                later = halo[(2 + f,) + spot(i, j)] + (diffusion[f] - (0.25 * sign) * u) * own(f, i, j)
                if partner == 1:
                    later = jnp.where(inside, later, 0.0)
                after[(f, 0) + spot(i, j)] = later


def plain(ref):
    return lambda f, i, j: ref[(f,) + spot(i, j)]


def split_rows(total, pieces):
    rows = total.shape[1] // len(pieces)
    for by, piece in enumerate(pieces):
        start = pl.multiple_of(lax.bitwise_xor(lax.axis_index("tm"), by) * rows, rows)
        piece[...] = total[:, pl.ds(start, rows), :] * 0.5


def each(low, high, run):
    def step(l, carry):
        run(l)
        return carry

    lax.fori_loop(low, high, step, 0)


def start_kernel(snaps, state, velocity, message_one, message_two, flow_out, scalars, edges, flows, sems):
    depth = state.shape[1]
    copies = [
        (snaps, scalars),
        (state.at[:, pl.ds(0, 2)], edges.at[:, pl.ds(0, 2)]),
        (state.at[:, pl.ds(depth - 2, 2)], edges.at[:, pl.ds(2, 2)]),
        (velocity.at[:, :, pl.ds(0, 1)], flows.at[:, :, pl.ds(0, 1)]),
        (velocity.at[:, :, pl.ds(depth - 1, 1)], flows.at[:, :, pl.ds(1, 1)]),
    ]
    copies = [pltpu.make_async_copy(*pair, sems.at[n]) for n, pair in enumerate(copies)]
    for copy in copies:
        copy.start()
    for copy in copies:
        copy.wait()
    for partner, message in enumerate((message_one, message_two)):
        high, sign = side_of(partner)
        here, inner = layer_of(edges, 3 * high), layer_of(edges, 1 + high)
        pack(here, inner, flow_of(flows, scalars[0, 1], high), sign, message, edges.shape[2:])
    flow_out[...] = flows[:, 0, 1 - lax.rem(lax.axis_index("tm"), 2)]


def first_kernel(blocks, slabs, partner, snaps, snaps_next, state, halo, own_flow, other_flow, velocity, start,
                 widened, edges, message, *scratch):
    rest, now = scratch if partner == 0 else (None, scratch[0])
    depth, shape = state.shape[1], state.shape[2:]
    last = lax.axis_index("tm") == slabs - 1
    high, sign = side_of(partner)

    def at(k):
        return high * (depth - 1) + k * (1 - 2 * high)

    @pl.when(last)
    def _():
        pltpu.sync_copy(start.at[:, pl.ds(at(0), 1)], edges.at[:, pl.ds(0, 1)])
        pltpu.sync_copy(start.at[:, pl.ds(at(1), 1)], edges.at[:, pl.ds(1, 1)])

    @pl.when(jnp.logical_not(last))
    def _():
        snap = snaps_next[0, 1]
        take_halo(blocks, partner, halo, layer_of(state, at(0)), own_flow, other_flow, snap, now, widened, shape)
        for k in range(3):
            outer = plain(now) if k == 0 else layer_of(state, at(k - 1))
            here, inner, flow = layer_of(state, at(k)), layer_of(state, at(k + 1)), flow_of(velocity, snap, at(k))
            side_layer(outer, here, inner, flow, sign, shape, into(widened, k + 1))
        for k in range(2):
            outer, here, inner = [layer_of(widened, k + n) for n in range(3)]
            flow = flow_of(velocity, snaps_next[0, 0], at(k))
            side_layer(outer, here, inner, flow, sign, shape, into(edges, k))

    pack(layer_of(edges, 0), layer_of(edges, 1), flow_of(velocity, snaps[0, 1], at(0)), sign, message, shape, rest)


def inner_kernel(slabs, snaps, snaps_next, before, widened_one, widened_two, edges_one, edges_two, velocity, start,
                 carried_on, inner, kept, to_core, state, widened, final, total, sem):
    depth, shape = state.shape[1], state.shape[2:]
    last = lax.axis_index("tm") == slabs - 1

    @pl.when(last)
    def _():
        pltpu.sync_copy(start, state)

    @pl.when(jnp.logical_not(last))
    def _():
        for partner, wide, edges in ((0, widened_one, edges_one), (1, widened_two, edges_two)):
            high, unused = side_of(partner)
            for k in range(4):
                widened[:, high * (depth + 1) + k * (1 - 2 * high)] = wide[:, k]
            for k in range(2):
                state[:, high * (depth - 1) + k * (1 - 2 * high)] = edges[:, k]

        def first_step(l):
            flow = flow_of(velocity, snaps_next[0, 1], l)
            here = layer_of(before, l)
            full_layer(layer_of(before, l - 1), here, layer_of(before, l + 1), flow, shape, into(widened, l + 1))

        each(3, depth - 3, first_step)

        def second_step(l):
            flow = flow_of(velocity, snaps_next[0, 0], l)
            here = layer_of(widened, l + 1)
            full_layer(layer_of(widened, l), here, layer_of(widened, l + 2), flow, shape, into(state, l))

        each(2, depth - 2, second_step)

    def third_step(l):
        flow = flow_of(velocity, snaps[0, 1], l)
        here = layer_of(state, l)
        full_layer(layer_of(state, l - 1), here, layer_of(state, l + 1), flow, shape, into(carried_on, l))

    each(1, depth - 1, third_step)

    def fourth_step(l):
        def store(i, j, values):
            into(final, l - 2)(i, j, values)
            total[(l - 2,) + spot(i, j)] = carried_on[(0, l) + spot(i, j)] + values[0]

        flow = flow_of(velocity, snaps[0, 0], l)
        here = layer_of(carried_on, l)
        full_layer(layer_of(carried_on, l - 1), here, layer_of(carried_on, l + 1), flow, shape, store)

    each(2, depth - 2, fourth_step)
    copy = pltpu.make_async_copy(final, inner.at[:, pl.ds(2, depth - 4)], sem)
    copy.start()
    split_rows(total, [kept.at[0], to_core.at[0], kept.at[1], to_core.at[1]])
    copy.wait()


def chip_kernel(kept, from_core, own, across):
    own[...] = kept[0] + from_core[0]
    across[...] = kept[1] + from_core[1]


def last_steps(partner, snaps, carried_on, outer, velocity, store, wanted, beyond=None):
    depth, shape = carried_on.shape[1], carried_on.shape[2:]
    high, sign = side_of(partner)

    def at(k):
        return high * (depth - 1) + k * (1 - 2 * high)

    ring = [layer_of(outer, 0), layer_of(outer, 1), layer_of(carried_on, at(1)), layer_of(carried_on, at(2))]
    if beyond is not None:
        ring[0] = beyond
    for k in range(2):
        flow = flow_of(velocity, snaps[0, 0], at(k))
        keep = functools.partial(store, k, ring[k + 1])
        side_layer(ring[k], ring[k + 1], ring[k + 2], flow, sign, shape, keep, wanted)


def outer_kernel(blocks, slabs, partner, snaps, edges, halo, own_flow, other_flow, carried_on, velocity, *rest):
    before, rest = rest[:partner], rest[partner:]
    if partner == 0:
        outer, total, now = rest
    else:
        outer, pieces, (now, total, whole) = rest[0], rest[1 : slabs + 1], rest[slabs + 1 :]
    depth, shape = carried_on.shape[1], carried_on.shape[2:]
    high, sign = side_of(partner)
    snap = snaps[0, 1]
    take_halo(blocks, partner, halo, layer_of(edges, 0), own_flow, other_flow, snap, now, outer, shape)
    flow = flow_of(velocity, snap, high * (depth - 1))
    side_layer(plain(now), layer_of(edges, 0), layer_of(edges, 1), flow, sign, shape, into(outer, 1))

    def store(k, here, i, j, values):
        total[(k,) + spot(i, j)] = here(0, i, j) + values[0]

    last_steps(partner, snaps, carried_on, outer, velocity, store, (0,))
    if partner == 1:
        for k in range(2):
            whole[high * (edge_count - 1) + k * (1 - 2 * high)] = total[k]
            whole[(1 - high) * (edge_count - 1) - k * (1 - 2 * high)] = before[0][k]
        split_rows(whole, pieces)


def finish_kernel(snaps, carried_on, outer_one, outer_two, edges, rest, own_flow, other_flow, velocity, inner,
                  out, final, later, sems):
    depth, shape = carried_on.shape[1], carried_on.shape[2:]
    fetched = lax.rem(lax.axis_index("tm"), 2)
    high, sign = side_of(0)
    for i, j in tiles(shape):
        at = (snaps[0, 1],) + spot(i, j)
        u = jnp.where(high == fetched, own_flow[at], other_flow[at])
        later[spot(i, j)] = rest[(0,) + spot(i, j)] + (diffusion[1] - (0.25 * sign) * u) * edges[(1, 0) + spot(i, j)]

    def beyond(f, i, j):
        return later[spot(i, j)] if f == 1 else outer_one[(0, 0) + spot(i, j)]

    for partner, outer in enumerate((outer_one, outer_two)):
        high, unused = side_of(partner)

        def store(k, here, i, j, values, high=high):
            into(final, high * (edge_count - 1) + k * (1 - 2 * high))(i, j, values)

        last_steps(partner, snaps, carried_on, outer, velocity, store, (0, 1), None if partner else beyond)
    copies = [
        pltpu.make_async_copy(final.at[:, pl.ds(0, 2)], out.at[:, pl.ds(0, 2)], sems.at[0]),
        pltpu.make_async_copy(final.at[:, pl.ds(2, 2)], out.at[:, pl.ds(depth - 2, 2)], sems.at[1]),
    ]
    for copy in copies:
        copy.start()
    for copy in copies:
        copy.wait()


def sum_kernel(inner, inner_across, *refs):
    parts, out = refs[:-1], refs[-1]
    depth = out.shape[0]
    outer = functools.reduce(jnp.add, [part[...] for part in parts])
    out[2 : depth - 2] = inner[...] + inner_across[...]
    out[0:2] = outer[0:2]
    out[depth - 2 : depth] = outer[2:4]


def solution(mesh):
    slabs, blocks = mesh.shape["tm"], mesh.shape["space"]
    vmem, smem = pl.BlockSpec(memory_space=pltpu.VMEM), pl.BlockSpec(memory_space=pltpu.SMEM)
    hbm = pl.BlockSpec(memory_space=pltpu.HBM)
    sem = pltpu.SemaphoreType.DMA

    def params(mebibytes):
        return pltpu.CompilerParams(vmem_limit_bytes=mebibytes * 1024 * 1024)

    def cost(microseconds):
        return pl.CostEstimate(flops=0, bytes_accessed=int(microseconds * 3.6e6), transcendentals=0)

    def index(t, s):
        return (t % slabs) * blocks + s % blocks

    def moved(array, to):
        pairs = [(index(t, s), index(*to(t, s))) for t in range(slabs) for s in range(blocks)]
        return lax.ppermute(array, ("tm", "space"), pairs)

    def exchanged(array, by, earlier):
        def to(t, s):
            partner = ((s + by) ^ 1) - by
            return (t - earlier, partner) if 0 <= partner < blocks else (t ^ 1, s)

        return moved(array, to)

    def fetched(t, s):
        source = s + 1 - 2 * (t % 2)
        return (t ^ 2, source) if 0 <= source < blocks else (t ^ 1, s)

    def body(slab_states, velocity, snap_of_step):
        start = slab_states[0]
        fields, depth, ny, nz = start.shape

        def shaped(*lead, rows=ny):
            return jax.ShapeDtypeStruct(lead + (rows, nz), jnp.float32)

        def room(*lead):
            return pltpu.VMEM(lead + (ny, nz), jnp.float32)

        layer = shaped(4)
        pieces = (shaped(4, rows=ny // slabs),) * slabs

        state = moved(start, lambda t, s: (t - 1, s))
        snaps_next = moved(snap_of_step, lambda t, s: (t - 1, s))
        message_one, message_two, flow_out = pl.pallas_call(
            start_kernel,
            out_shape=(layer, layer, shaped(velocity.shape[0])),
            in_specs=[hbm] * 3,
            out_specs=(vmem,) * 3,
            scratch_shapes=[
                pltpu.SMEM(snap_of_step.shape, jnp.int32),
                room(fields, edge_count),
                room(*velocity.shape[:2], 2),
                sem((5,)),
            ],
            compiler_params=params(56),
            cost_estimate=cost(2),
        )(snap_of_step, start, velocity)
        halo_one = exchanged(message_one, 0, 1)
        halo_two = exchanged(message_two, 1, 1)
        own_flow = moved(flow_out, fetched)
        other_flow = moved(own_flow, lambda t, s: (t ^ 1, s))
        widened, edges, halo, halo_rest = [None] * 2, [None] * 2, [halo_one, halo_two], []
        for partner in (0, 1):
            widened[partner], edges[partner], message, *rest = pl.pallas_call(
                functools.partial(first_kernel, blocks, slabs, partner),
                out_shape=(shaped(fields, 4), shaped(fields, 2)) + ((layer,) if partner else (shaped(3), shaped(1))),
                in_specs=[smem, smem] + [vmem] * 5 + [hbm],
                out_specs=(vmem,) * (4 - partner),
                scratch_shapes=[room(fields)],
                compiler_params=params(32),
                cost_estimate=cost(1.5),
            )(snap_of_step, snaps_next, state, halo[partner], own_flow, other_flow, velocity, start)
            halo[partner] = exchanged(message, partner, 0)
            halo_rest += [exchanged(part, partner, 0) for part in rest]
        pair = jax.ShapeDtypeStruct((2,) + pieces[0].shape, jnp.float32)
        carried_on, inner, kept, to_core = pl.pallas_call(
            functools.partial(inner_kernel, slabs),
            out_shape=(shaped(fields, depth), shaped(fields, depth), pair, pair),
            in_specs=[smem, smem] + [vmem] * 6 + [hbm],
            out_specs=(vmem, hbm, vmem, vmem),
            scratch_shapes=[
                room(fields, depth), room(fields, depth + 2), room(fields, depth - 4), room(depth - 4), sem(()),
            ],
            compiler_params=params(32),
            cost_estimate=cost(3),
        )(snap_of_step, snaps_next, state, *widened, *edges, velocity, start)
        inner_own, inner_across = pl.pallas_call(
            chip_kernel,
            out_shape=pieces[:2],
            in_specs=[vmem, vmem],
            out_specs=(vmem, vmem),
            compiler_params=params(16),
            cost_estimate=cost(0.5),
        )(kept, moved(to_core, lambda t, s: (t ^ 1, s)))
        inner_across = moved(inner_across, lambda t, s: (t ^ 2, s))
        outer_one, total_one = pl.pallas_call(
            functools.partial(outer_kernel, blocks, slabs, 0),
            out_shape=(shaped(fields, 2), shaped(2)),
            in_specs=[smem] + [vmem] * 6,
            out_specs=(vmem,) * 2,
            scratch_shapes=[room(fields)],
            compiler_params=params(32),
            cost_estimate=cost(0.5),
        )(snap_of_step, edges[0], halo[0], own_flow, other_flow, carried_on, velocity)
        outer_two, *outer_pieces = pl.pallas_call(
            functools.partial(outer_kernel, blocks, slabs, 1),
            out_shape=(shaped(fields, 2),) + pieces,
            in_specs=[smem] + [vmem] * 7,
            out_specs=(vmem,) * (1 + slabs),
            scratch_shapes=[room(fields), room(2), room(edge_count)],
            compiler_params=params(32),
            cost_estimate=cost(0.5),
        )(snap_of_step, edges[1], halo[1], own_flow, other_flow, carried_on, velocity, total_one)
        outer_parts = outer_pieces[:1] + [
            moved(outer_pieces[by], lambda t, s, by=by: (t ^ by, s)) for by in range(1, slabs)
        ]
        final = pl.pallas_call(
            finish_kernel,
            out_shape=shaped(fields, depth),
            in_specs=[smem] + [vmem] * 8 + [hbm],
            out_specs=hbm,
            scratch_shapes=[room(fields, edge_count), room(), sem((2,))],
            input_output_aliases={9: 0},
            compiler_params=params(32),
            cost_estimate=cost(1),
        )(snap_of_step, carried_on, outer_one, outer_two, edges[0], *halo_rest, own_flow, other_flow, velocity, inner)
        gradient = pl.pallas_call(
            sum_kernel,
            out_shape=shaped(depth, rows=ny // slabs),
            in_specs=[vmem] * (2 + slabs),
            out_specs=vmem,
            compiler_params=params(16),
            cost_estimate=cost(0.5),
        )(inner_own, inner_across, *outer_parts)
        return (final[None], gradient)

    return jax.shard_map(
        body,
        mesh=mesh,
        in_specs=(P("tm", None, "space", None, None), P(None, None, "space", None, None), P("tm", None)),
        out_specs=(P("tm", None, "space", None, None), P("space", "tm", None)),
        check_vma=False,
    )
```

```python
import functools

import jax
import jax.numpy as jnp
from jax import lax
from jax.experimental import pallas as pl
from jax.experimental.pallas import tpu as pltpu
from jax.sharding import PartitionSpec as P

coupling = 0.3
diffusion = (0.14, 0.06)
sub, lanes = 8, 128
edge_count = 4


def tiles(shape):
    rows, cols = shape
    return [(i, j) for i in range(rows // sub) for j in range(cols // lanes)]


def spot(i, j):
    return (pl.ds(i * sub, sub), pl.ds(j * lanes, lanes))


def neighbours(at, i, j, shape):
    rows, cols = shape
    centre = at(i, j)
    row = lax.broadcasted_iota(jnp.int32, (sub, lanes), 0)
    col = lax.broadcasted_iota(jnp.int32, (sub, lanes), 1)
    zero = jnp.zeros_like(centre)
    after = at(i + 1, j) if (i + 1) * sub < rows else zero
    before = at(i - 1, j) if i > 0 else zero
    north = pltpu.roll(jnp.where(row == 0, after, centre), sub - 1, 0)
    south = pltpu.roll(jnp.where(row == sub - 1, before, centre), 1, 0)
    after = at(i, j + 1) if (j + 1) * lanes < cols else zero
    before = at(i, j - 1) if j > 0 else zero
    upper = pltpu.roll(jnp.where(col == 0, after, centre), lanes - 1, 1)
    lower = pltpu.roll(jnp.where(col == lanes - 1, before, centre), 1, 1)
    return centre, (north + south) + (upper + lower), north - south, upper - lower


def advanced(fields, pairs, flow, i, j, shape, wanted=(0, 1)):
    u, v, w = flow
    out = []
    for f in wanted:
        centre, total, dy, dz = neighbours(functools.partial(fields, f), i, j, shape)
        side_sum, side_diff = pairs(f, i, j)
        c = diffusion[f]
        moved = u * side_diff + v * dy + w * dz
        new = ((1.0 - 6.0 * c) * centre + c * (side_sum + total)) + 0.25 * moved
        if f == 0:
            new = new + coupling * fields(1, i, j)
        out.append(new)
    return out


def layer_of(ref, l):
    return lambda f, i, j: ref[(f, l) + spot(i, j)]


def flow_of(velocity, snap, l):
    return lambda i, j: [velocity[(snap, d, l) + spot(i, j)] for d in range(3)]


def full_layer(below, here, above, flow, shape, store, wanted=(0, 1)):
    def pairs(f, i, j):
        hi, lo = above(f, i, j), below(f, i, j)
        return hi + lo, hi - lo

    for i, j in tiles(shape):
        store(i, j, advanced(here, pairs, flow(i, j), i, j, shape, wanted))


def into(ref, l):
    def store(i, j, values):
        for f, value in enumerate(values):
            ref[(f, l) + spot(i, j)] = value

    return store


def side_of(partner):
    parity = lax.rem(lax.axis_index("space"), 2)
    high = 1 - parity if partner == 0 else parity
    return high, (2 * high - 1).astype(jnp.float32)


def side_layer(outer, here, inner, flow, sign, shape, store, wanted=(0, 1)):
    def pairs(f, i, j):
        far, near = outer(f, i, j), inner(f, i, j)
        return far + near, far - near

    for i, j in tiles(shape):
        u, v, w = flow(i, j)
        store(i, j, advanced(here, pairs, (sign * u, v, w), i, j, shape, wanted))


def pack(here, inner, flow, sign, message, shape):
    def pairs(f, i, j):
        value = inner(f, i, j)
        return value, value

    for i, j in tiles(shape):
        u, v, w = flow(i, j)
        out = advanced(here, pairs, (-sign * u, v, w), i, j, shape)
        for f in (0, 1):
            message[(f,) + spot(i, j)] = here(f, i, j)
            message[(2 + f,) + spot(i, j)] = out[f]


def take_halo(blocks, partner, halo, own, own_flow, other_flow, snap, now, after, shape):
    high, sign = side_of(partner)
    place = lax.axis_index("space")
    inside = jnp.logical_and(place > 0, place < blocks - 1)
    fetched = lax.rem(lax.axis_index("tm"), 2)
    for i, j in tiles(shape):
        u = jnp.where(high == fetched, own_flow[(snap,) + spot(i, j)], other_flow[(snap,) + spot(i, j)])
        for f in (0, 1):
            current = halo[(f,) + spot(i, j)]
            later = halo[(2 + f,) + spot(i, j)] + (diffusion[f] - (0.25 * sign) * u) * own(f, i, j)
            if partner == 1:
                current = jnp.where(inside, current, 0.0)
                later = jnp.where(inside, later, 0.0)
            now[(f,) + spot(i, j)] = current
            after[(f, 0) + spot(i, j)] = later


def plain(ref):
    return lambda f, i, j: ref[(f,) + spot(i, j)]


def split_rows(total, pieces):
    rows = total.shape[1] // len(pieces)
    for by, piece in enumerate(pieces):
        start = pl.multiple_of(lax.rem(lax.axis_index("tm") + by, len(pieces)) * rows, rows)
        piece[...] = total[:, pl.ds(start, rows), :] * 0.5


def each(low, high, run):
    def step(l, carry):
        run(l)
        return carry

    lax.fori_loop(low, high, step, 0)


def start_kernel(snaps, state, velocity, message_one, message_two, flow_out, scalars, edges, flows, sems):
    depth = state.shape[1]
    copies = [
        (snaps, scalars),
        (state.at[:, pl.ds(0, 2)], edges.at[:, pl.ds(0, 2)]),
        (state.at[:, pl.ds(depth - 2, 2)], edges.at[:, pl.ds(2, 2)]),
        (velocity.at[:, :, pl.ds(0, 1)], flows.at[:, :, pl.ds(0, 1)]),
        (velocity.at[:, :, pl.ds(depth - 1, 1)], flows.at[:, :, pl.ds(1, 1)]),
    ]
    copies = [pltpu.make_async_copy(*pair, sems.at[n]) for n, pair in enumerate(copies)]
    for copy in copies:
        copy.start()
    for copy in copies:
        copy.wait()
    for partner, message in enumerate((message_one, message_two)):
        high, sign = side_of(partner)
        here, inner = layer_of(edges, 3 * high), layer_of(edges, 1 + high)
        pack(here, inner, flow_of(flows, scalars[0, 1], high), sign, message, edges.shape[2:])
    flow_out[...] = flows[:, 0, 1 - lax.rem(lax.axis_index("tm"), 2)]


def first_kernel(blocks, slabs, partner, snaps, snaps_next, state, halo, own_flow, other_flow, velocity, start,
                 widened, edges, message, now):
    depth, shape = state.shape[1], state.shape[2:]
    last = lax.axis_index("tm") == slabs - 1
    high, sign = side_of(partner)

    def at(k):
        return high * (depth - 1) + k * (1 - 2 * high)

    @pl.when(last)
    def _():
        pltpu.sync_copy(start.at[:, pl.ds(at(0), 1)], edges.at[:, pl.ds(0, 1)])
        pltpu.sync_copy(start.at[:, pl.ds(at(1), 1)], edges.at[:, pl.ds(1, 1)])

    @pl.when(jnp.logical_not(last))
    def _():
        snap = snaps_next[0, 1]
        take_halo(blocks, partner, halo, layer_of(state, at(0)), own_flow, other_flow, snap, now, widened, shape)
        for k in range(3):
            outer = plain(now) if k == 0 else layer_of(state, at(k - 1))
            here, inner, flow = layer_of(state, at(k)), layer_of(state, at(k + 1)), flow_of(velocity, snap, at(k))
            side_layer(outer, here, inner, flow, sign, shape, into(widened, k + 1))
        for k in range(2):
            outer, here, inner = [layer_of(widened, k + n) for n in range(3)]
            flow = flow_of(velocity, snaps_next[0, 0], at(k))
            side_layer(outer, here, inner, flow, sign, shape, into(edges, k))

    pack(layer_of(edges, 0), layer_of(edges, 1), flow_of(velocity, snaps[0, 1], at(0)), sign, message, shape)


def inner_kernel(slabs, snaps, snaps_next, before, widened_one, widened_two, edges_one, edges_two, velocity, start,
                 carried_on, inner, *rest):
    pieces, (state, widened, final, total, sem) = rest[:slabs], rest[slabs:]
    depth, shape = state.shape[1], state.shape[2:]
    last = lax.axis_index("tm") == slabs - 1

    @pl.when(last)
    def _():
        pltpu.sync_copy(start, state)

    @pl.when(jnp.logical_not(last))
    def _():
        for partner, wide, edges in ((0, widened_one, edges_one), (1, widened_two, edges_two)):
            high, unused = side_of(partner)
            for k in range(4):
                widened[:, high * (depth + 1) + k * (1 - 2 * high)] = wide[:, k]
            for k in range(2):
                state[:, high * (depth - 1) + k * (1 - 2 * high)] = edges[:, k]

        def first_step(l):
            flow = flow_of(velocity, snaps_next[0, 1], l)
            here = layer_of(before, l)
            full_layer(layer_of(before, l - 1), here, layer_of(before, l + 1), flow, shape, into(widened, l + 1))

        each(3, depth - 3, first_step)

        def second_step(l):
            flow = flow_of(velocity, snaps_next[0, 0], l)
            here = layer_of(widened, l + 1)
            full_layer(layer_of(widened, l), here, layer_of(widened, l + 2), flow, shape, into(state, l))

        each(2, depth - 2, second_step)

    def third_step(l):
        flow = flow_of(velocity, snaps[0, 1], l)
        here = layer_of(state, l)
        full_layer(layer_of(state, l - 1), here, layer_of(state, l + 1), flow, shape, into(carried_on, l))

    each(1, depth - 1, third_step)

    def fourth_step(l):
        def store(i, j, values):
            into(final, l - 2)(i, j, values)
            total[(l - 2,) + spot(i, j)] = carried_on[(0, l) + spot(i, j)] + values[0]

        flow = flow_of(velocity, snaps[0, 0], l)
        here = layer_of(carried_on, l)
        full_layer(layer_of(carried_on, l - 1), here, layer_of(carried_on, l + 1), flow, shape, store)

    each(2, depth - 2, fourth_step)
    copy = pltpu.make_async_copy(final, inner.at[:, pl.ds(2, depth - 4)], sem)
    copy.start()
    split_rows(total, pieces)
    copy.wait()


def last_steps(partner, snaps, carried_on, outer, velocity, store, wanted):
    depth, shape = carried_on.shape[1], carried_on.shape[2:]
    high, sign = side_of(partner)

    def at(k):
        return high * (depth - 1) + k * (1 - 2 * high)

    ring = [layer_of(outer, 0), layer_of(outer, 1), layer_of(carried_on, at(1)), layer_of(carried_on, at(2))]
    for k in range(2):
        flow = flow_of(velocity, snaps[0, 0], at(k))
        keep = functools.partial(store, k, ring[k + 1])
        side_layer(ring[k], ring[k + 1], ring[k + 2], flow, sign, shape, keep, wanted)


def outer_kernel(blocks, slabs, partner, snaps, edges, halo, own_flow, other_flow, carried_on, velocity, *rest):
    before, rest = rest[:partner], rest[partner:]
    if partner == 0:
        outer, total, now = rest
    else:
        outer, pieces, (now, total, whole) = rest[0], rest[1 : slabs + 1], rest[slabs + 1 :]
    depth, shape = carried_on.shape[1], carried_on.shape[2:]
    high, sign = side_of(partner)
    snap = snaps[0, 1]
    take_halo(blocks, partner, halo, layer_of(edges, 0), own_flow, other_flow, snap, now, outer, shape)
    flow = flow_of(velocity, snap, high * (depth - 1))
    side_layer(plain(now), layer_of(edges, 0), layer_of(edges, 1), flow, sign, shape, into(outer, 1))

    def store(k, here, i, j, values):
        total[(k,) + spot(i, j)] = here(0, i, j) + values[0]

    last_steps(partner, snaps, carried_on, outer, velocity, store, (0,))
    if partner == 1:
        for k in range(2):
            whole[high * (edge_count - 1) + k * (1 - 2 * high)] = total[k]
            whole[(1 - high) * (edge_count - 1) - k * (1 - 2 * high)] = before[0][k]
        split_rows(whole, pieces)


def finish_kernel(snaps, carried_on, outer_one, outer_two, velocity, inner, out, final, sems):
    depth = carried_on.shape[1]
    for partner, outer in enumerate((outer_one, outer_two)):
        high, unused = side_of(partner)

        def store(k, here, i, j, values, high=high):
            into(final, high * (edge_count - 1) + k * (1 - 2 * high))(i, j, values)

        last_steps(partner, snaps, carried_on, outer, velocity, store, (0, 1))
    copies = [
        pltpu.make_async_copy(final.at[:, pl.ds(0, 2)], out.at[:, pl.ds(0, 2)], sems.at[0]),
        pltpu.make_async_copy(final.at[:, pl.ds(2, 2)], out.at[:, pl.ds(depth - 2, 2)], sems.at[1]),
    ]
    for copy in copies:
        copy.start()
    for copy in copies:
        copy.wait()


def sum_kernel(*refs):
    ins, out = refs[:-1], refs[-1]
    half = len(ins) // 2
    depth = out.shape[0]
    inner = functools.reduce(jnp.add, [ref[...] for ref in ins[:half]])
    outer = functools.reduce(jnp.add, [ref[...] for ref in ins[half:]])
    out[2 : depth - 2] = inner
    out[0:2] = outer[0:2]
    out[depth - 2 : depth] = outer[2:4]


def solution(mesh):
    slabs, blocks = mesh.shape["tm"], mesh.shape["space"]
    vmem, smem = pl.BlockSpec(memory_space=pltpu.VMEM), pl.BlockSpec(memory_space=pltpu.SMEM)
    hbm = pl.BlockSpec(memory_space=pltpu.HBM)
    sem = pltpu.SemaphoreType.DMA

    def params(mebibytes):
        return pltpu.CompilerParams(vmem_limit_bytes=mebibytes * 1024 * 1024)

    def cost(microseconds):
        return pl.CostEstimate(flops=0, bytes_accessed=int(microseconds * 3.6e6), transcendentals=0)

    def index(t, s):
        return (t % slabs) * blocks + s % blocks

    def moved(array, to):
        pairs = [(index(t, s), index(*to(t, s))) for t in range(slabs) for s in range(blocks)]
        return lax.ppermute(array, ("tm", "space"), pairs)

    def exchanged(array, by, earlier):
        def to(t, s):
            partner = ((s + by) ^ 1) - by
            return (t - earlier, partner) if 0 <= partner < blocks else (t ^ 1, s)

        return moved(array, to)

    def fetched(t, s):
        source = s + 1 - 2 * (t % 2)
        return (t ^ 2, source) if 0 <= source < blocks else (t ^ 1, s)

    def body(slab_states, velocity, snap_of_step):
        start = slab_states[0]
        fields, depth, ny, nz = start.shape

        def shaped(*lead, rows=ny):
            return jax.ShapeDtypeStruct(lead + (rows, nz), jnp.float32)

        def room(*lead):
            return pltpu.VMEM(lead + (ny, nz), jnp.float32)

        layer = shaped(4)
        pieces = (shaped(4, rows=ny // slabs),) * slabs

        state = moved(start, lambda t, s: (t - 1, s))
        snaps_next = moved(snap_of_step, lambda t, s: (t - 1, s))
        message_one, message_two, flow_out = pl.pallas_call(
            start_kernel,
            out_shape=(layer, layer, shaped(velocity.shape[0])),
            in_specs=[hbm] * 3,
            out_specs=(vmem,) * 3,
            scratch_shapes=[
                pltpu.SMEM(snap_of_step.shape, jnp.int32),
                room(fields, edge_count),
                room(*velocity.shape[:2], 2),
                sem((5,)),
            ],
            compiler_params=params(53),
            cost_estimate=cost(2),
        )(snap_of_step, start, velocity)
        halo_one = exchanged(message_one, 0, 1)
        halo_two = exchanged(message_two, 1, 1)
        own_flow = moved(flow_out, fetched)
        other_flow = moved(own_flow, lambda t, s: (t ^ 1, s))
        widened, edges, halo = [None] * 2, [None] * 2, [halo_one, halo_two]
        for partner in (0, 1):
            widened[partner], edges[partner], message = pl.pallas_call(
                functools.partial(first_kernel, blocks, slabs, partner),
                out_shape=(shaped(fields, 4), shaped(fields, 2), layer),
                in_specs=[smem, smem] + [vmem] * 5 + [hbm],
                out_specs=(vmem,) * 3,
                scratch_shapes=[room(fields)],
                compiler_params=params(32),
                cost_estimate=cost(1.5),
            )(snap_of_step, snaps_next, state, halo[partner], own_flow, other_flow, velocity, start)
            halo[partner] = exchanged(message, partner, 0)
        carried_on, inner, *inner_pieces = pl.pallas_call(
            functools.partial(inner_kernel, slabs),
            out_shape=(shaped(fields, depth), shaped(fields, depth)) + pieces,
            in_specs=[smem, smem] + [vmem] * 6 + [hbm],
            out_specs=(vmem, hbm) + (vmem,) * slabs,
            scratch_shapes=[
                room(fields, depth), room(fields, depth + 2), room(fields, depth - 4), room(depth - 4), sem(()),
            ],
            compiler_params=params(32),
            cost_estimate=cost(3),
        )(snap_of_step, snaps_next, state, *widened, *edges, velocity, start)
        inner_parts = inner_pieces[:1] + [
            moved(inner_pieces[by], lambda t, s, by=by: (t + by, s)) for by in range(1, slabs)
        ]
        outer_one, total_one = pl.pallas_call(
            functools.partial(outer_kernel, blocks, slabs, 0),
            out_shape=(shaped(fields, 2), shaped(2)),
            in_specs=[smem] + [vmem] * 6,
            out_specs=(vmem,) * 2,
            scratch_shapes=[room(fields)],
            compiler_params=params(32),
            cost_estimate=cost(0.5),
        )(snap_of_step, edges[0], halo[0], own_flow, other_flow, carried_on, velocity)
        outer_two, *outer_pieces = pl.pallas_call(
            functools.partial(outer_kernel, blocks, slabs, 1),
            out_shape=(shaped(fields, 2),) + pieces,
            in_specs=[smem] + [vmem] * 7,
            out_specs=(vmem,) * (1 + slabs),
            scratch_shapes=[room(fields), room(2), room(edge_count)],
            compiler_params=params(32),
            cost_estimate=cost(0.5),
        )(snap_of_step, edges[1], halo[1], own_flow, other_flow, carried_on, velocity, total_one)
        outer_parts = outer_pieces[:1] + [
            moved(outer_pieces[by], lambda t, s, by=by: (t + by, s)) for by in range(1, slabs)
        ]
        final = pl.pallas_call(
            finish_kernel,
            out_shape=shaped(fields, depth),
            in_specs=[smem, vmem, vmem, vmem, vmem, hbm],
            out_specs=hbm,
            scratch_shapes=[room(fields, edge_count), sem((2,))],
            input_output_aliases={5: 0},
            compiler_params=params(32),
            cost_estimate=cost(1),
        )(snap_of_step, carried_on, outer_one, outer_two, velocity, inner)
        gradient = pl.pallas_call(
            sum_kernel,
            out_shape=shaped(depth, rows=ny // slabs),
            in_specs=[vmem] * (2 * slabs),
            out_specs=vmem,
            compiler_params=params(16),
            cost_estimate=cost(0.5),
        )(*inner_parts, *outer_parts)
        return (final[None], gradient)

    return jax.shard_map(
        body,
        mesh=mesh,
        in_specs=(P("tm", None, "space", None, None), P(None, None, "space", None, None), P("tm", None)),
        out_specs=(P("tm", None, "space", None, None), P("space", "tm", None)),
        check_vma=False,
    )
```

```python
import functools

import jax
import jax.numpy as jnp
from jax import lax
from jax.experimental import pallas as pl
from jax.experimental.pallas import tpu as pltpu
from jax.sharding import PartitionSpec as P

coupling = 0.3
diffusion = (0.14, 0.06)
sub, lanes = 8, 128
edge_count = 4


def tiles(shape):
    rows, cols = shape
    return [(i, j) for i in range(rows // sub) for j in range(cols // lanes)]


def spot(i, j):
    return (pl.ds(i * sub, sub), pl.ds(j * lanes, lanes))


def neighbours(at, i, j, shape):
    rows, cols = shape
    centre = at(i, j)
    row = lax.broadcasted_iota(jnp.int32, (sub, lanes), 0)
    col = lax.broadcasted_iota(jnp.int32, (sub, lanes), 1)
    zero = jnp.zeros_like(centre)
    after = at(i + 1, j) if (i + 1) * sub < rows else zero
    before = at(i - 1, j) if i > 0 else zero
    north = pltpu.roll(jnp.where(row == 0, after, centre), sub - 1, 0)
    south = pltpu.roll(jnp.where(row == sub - 1, before, centre), 1, 0)
    after = at(i, j + 1) if (j + 1) * lanes < cols else zero
    before = at(i, j - 1) if j > 0 else zero
    upper = pltpu.roll(jnp.where(col == 0, after, centre), lanes - 1, 1)
    lower = pltpu.roll(jnp.where(col == lanes - 1, before, centre), 1, 1)
    return centre, (north + south) + (upper + lower), north - south, upper - lower


def advanced(fields, pairs, flow, i, j, shape, wanted=(0, 1)):
    u, v, w = flow
    out = []
    for f in wanted:
        centre, total, dy, dz = neighbours(functools.partial(fields, f), i, j, shape)
        side_sum, side_diff = pairs(f, i, j)
        c = diffusion[f]
        moved = u * side_diff + v * dy + w * dz
        new = ((1.0 - 6.0 * c) * centre + c * (side_sum + total)) + 0.25 * moved
        if f == 0:
            new = new + coupling * fields(1, i, j)
        out.append(new)
    return out


def layer_of(ref, l):
    return lambda f, i, j: ref[(f, l) + spot(i, j)]


def flow_of(velocity, snap, l):
    return lambda i, j: [velocity[(snap, d, l) + spot(i, j)] for d in range(3)]


def full_layer(below, here, above, flow, shape, store, wanted=(0, 1)):
    def pairs(f, i, j):
        hi, lo = above(f, i, j), below(f, i, j)
        return hi + lo, hi - lo

    for i, j in tiles(shape):
        store(i, j, advanced(here, pairs, flow(i, j), i, j, shape, wanted))


def into(ref, l):
    def store(i, j, values):
        for f, value in enumerate(values):
            ref[(f, l) + spot(i, j)] = value

    return store


def side_of(partner):
    parity = lax.rem(lax.axis_index("space"), 2)
    high = 1 - parity if partner == 0 else parity
    return high, (2 * high - 1).astype(jnp.float32)


def side_layer(outer, here, inner, flow, sign, shape, store, wanted=(0, 1)):
    def pairs(f, i, j):
        far, near = outer(f, i, j), inner(f, i, j)
        return far + near, far - near

    for i, j in tiles(shape):
        u, v, w = flow(i, j)
        store(i, j, advanced(here, pairs, (sign * u, v, w), i, j, shape, wanted))


def pack(here, inner, flow, sign, message, shape, rest=None):
    def pairs(f, i, j):
        value = inner(f, i, j)
        return value, value

    for i, j in tiles(shape):
        u, v, w = flow(i, j)
        out = advanced(here, pairs, (-sign * u, v, w), i, j, shape)
        for f in (0, 1):
            message[(f,) + spot(i, j)] = here(f, i, j)
            into_message = message.at[2 + f] if f == 0 or rest is None else rest.at[0]
            into_message[spot(i, j)] = out[f]


def take_halo(blocks, partner, halo, own, own_flow, other_flow, snap, now, after, shape):
    high, sign = side_of(partner)
    place = lax.axis_index("space")
    inside = jnp.logical_and(place > 0, place < blocks - 1)
    fetched = lax.rem(lax.axis_index("tm"), 2)
    for i, j in tiles(shape):
        u = jnp.where(high == fetched, own_flow[(snap,) + spot(i, j)], other_flow[(snap,) + spot(i, j)])
        for f in (0, 1):
            current = halo[(f,) + spot(i, j)]
            if partner == 1:
                current = jnp.where(inside, current, 0.0)
            now[(f,) + spot(i, j)] = current
            if 2 + f < halo.shape[0]:
                later = halo[(2 + f,) + spot(i, j)] + (diffusion[f] - (0.25 * sign) * u) * own(f, i, j)
                if partner == 1:
                    later = jnp.where(inside, later, 0.0)
                after[(f, 0) + spot(i, j)] = later


def plain(ref):
    return lambda f, i, j: ref[(f,) + spot(i, j)]


def split_rows(total, pieces):
    rows = total.shape[1] // len(pieces)
    for by, piece in enumerate(pieces):
        start = pl.multiple_of(lax.bitwise_xor(lax.axis_index("tm"), by) * rows, rows)
        piece[...] = total[:, pl.ds(start, rows), :] * 0.5


def each(low, high, run):
    def step(l, carry):
        run(l)
        return carry

    lax.fori_loop(low, high, step, 0)


def start_kernel(snaps, state, velocity, message_one, message_two, flow_out, scalars, edges, flows, sems):
    depth = state.shape[1]
    copies = [
        (snaps, scalars),
        (state.at[:, pl.ds(0, 2)], edges.at[:, pl.ds(0, 2)]),
        (state.at[:, pl.ds(depth - 2, 2)], edges.at[:, pl.ds(2, 2)]),
        (velocity.at[:, :, pl.ds(0, 1)], flows.at[:, :, pl.ds(0, 1)]),
        (velocity.at[:, :, pl.ds(depth - 1, 1)], flows.at[:, :, pl.ds(1, 1)]),
    ]
    copies = [pltpu.make_async_copy(*pair, sems.at[n]) for n, pair in enumerate(copies)]
    for copy in copies:
        copy.start()
    for copy in copies:
        copy.wait()
    for partner, message in enumerate((message_one, message_two)):
        high, sign = side_of(partner)
        here, inner = layer_of(edges, 3 * high), layer_of(edges, 1 + high)
        pack(here, inner, flow_of(flows, scalars[0, 1], high), sign, message, edges.shape[2:])
    flow_out[...] = flows[:, 0, 1 - lax.rem(lax.axis_index("tm"), 2)]


def first_kernel(blocks, slabs, partner, snaps, snaps_next, state, halo, own_flow, other_flow, velocity, start,
                 widened, edges, message, *scratch):
    rest, now = scratch if partner == 1 else (None, scratch[0])
    depth, shape = state.shape[1], state.shape[2:]
    last = lax.axis_index("tm") == slabs - 1
    high, sign = side_of(partner)

    def at(k):
        return high * (depth - 1) + k * (1 - 2 * high)

    @pl.when(last)
    def _():
        pltpu.sync_copy(start.at[:, pl.ds(at(0), 1)], edges.at[:, pl.ds(0, 1)])
        pltpu.sync_copy(start.at[:, pl.ds(at(1), 1)], edges.at[:, pl.ds(1, 1)])

    @pl.when(jnp.logical_not(last))
    def _():
        snap = snaps_next[0, 1]
        take_halo(blocks, partner, halo, layer_of(state, at(0)), own_flow, other_flow, snap, now, widened, shape)
        for k in range(3):
            outer = plain(now) if k == 0 else layer_of(state, at(k - 1))
            here, inner, flow = layer_of(state, at(k)), layer_of(state, at(k + 1)), flow_of(velocity, snap, at(k))
            side_layer(outer, here, inner, flow, sign, shape, into(widened, k + 1))
        for k in range(2):
            outer, here, inner = [layer_of(widened, k + n) for n in range(3)]
            flow = flow_of(velocity, snaps_next[0, 0], at(k))
            side_layer(outer, here, inner, flow, sign, shape, into(edges, k))

    pack(layer_of(edges, 0), layer_of(edges, 1), flow_of(velocity, snaps[0, 1], at(0)), sign, message, shape, rest)


def inner_kernel(slabs, snaps, snaps_next, before, widened_one, widened_two, edges_one, edges_two, velocity, start,
                 carried_on, inner, kept, to_core, state, widened, final, total, sem):
    depth, shape = state.shape[1], state.shape[2:]
    last = lax.axis_index("tm") == slabs - 1

    @pl.when(last)
    def _():
        pltpu.sync_copy(start, state)

    @pl.when(jnp.logical_not(last))
    def _():
        for partner, wide, edges in ((0, widened_one, edges_one), (1, widened_two, edges_two)):
            high, unused = side_of(partner)
            for k in range(4):
                widened[:, high * (depth + 1) + k * (1 - 2 * high)] = wide[:, k]
            for k in range(2):
                state[:, high * (depth - 1) + k * (1 - 2 * high)] = edges[:, k]

        def first_step(l):
            flow = flow_of(velocity, snaps_next[0, 1], l)
            here = layer_of(before, l)
            full_layer(layer_of(before, l - 1), here, layer_of(before, l + 1), flow, shape, into(widened, l + 1))

        each(3, depth - 3, first_step)

        def second_step(l):
            flow = flow_of(velocity, snaps_next[0, 0], l)
            here = layer_of(widened, l + 1)
            full_layer(layer_of(widened, l), here, layer_of(widened, l + 2), flow, shape, into(state, l))

        each(2, depth - 2, second_step)

    def third_step(l):
        flow = flow_of(velocity, snaps[0, 1], l)
        here = layer_of(state, l)
        full_layer(layer_of(state, l - 1), here, layer_of(state, l + 1), flow, shape, into(carried_on, l))

    each(1, depth - 1, third_step)

    def fourth_step(l):
        def store(i, j, values):
            into(final, l - 2)(i, j, values)
            total[(l - 2,) + spot(i, j)] = carried_on[(0, l) + spot(i, j)] + values[0]

        flow = flow_of(velocity, snaps[0, 0], l)
        here = layer_of(carried_on, l)
        full_layer(layer_of(carried_on, l - 1), here, layer_of(carried_on, l + 1), flow, shape, store)

    each(2, depth - 2, fourth_step)
    copy = pltpu.make_async_copy(final, inner.at[:, pl.ds(2, depth - 4)], sem)
    copy.start()
    split_rows(total, [kept.at[0], to_core.at[0], kept.at[1], to_core.at[1]])
    copy.wait()


def chip_kernel(kept, from_core, own, across):
    own[...] = kept[0] + from_core[0]
    across[...] = kept[1] + from_core[1]


def last_steps(partner, snaps, carried_on, outer, velocity, store, wanted, beyond=None):
    depth, shape = carried_on.shape[1], carried_on.shape[2:]
    high, sign = side_of(partner)

    def at(k):
        return high * (depth - 1) + k * (1 - 2 * high)

    ring = [layer_of(outer, 0), layer_of(outer, 1), layer_of(carried_on, at(1)), layer_of(carried_on, at(2))]
    if beyond is not None:
        ring[0] = beyond
    for k in range(2):
        flow = flow_of(velocity, snaps[0, 0], at(k))
        keep = functools.partial(store, k, ring[k + 1])
        side_layer(ring[k], ring[k + 1], ring[k + 2], flow, sign, shape, keep, wanted)


def outer_kernel(blocks, slabs, partner, snaps, edges, halo, own_flow, other_flow, carried_on, velocity, *rest):
    before, rest = rest[:partner], rest[partner:]
    if partner == 0:
        outer, total, now = rest
    else:
        outer, pieces, (now, total, whole) = rest[0], rest[1 : slabs + 1], rest[slabs + 1 :]
    depth, shape = carried_on.shape[1], carried_on.shape[2:]
    high, sign = side_of(partner)
    snap = snaps[0, 1]
    take_halo(blocks, partner, halo, layer_of(edges, 0), own_flow, other_flow, snap, now, outer, shape)
    flow = flow_of(velocity, snap, high * (depth - 1))
    side_layer(plain(now), layer_of(edges, 0), layer_of(edges, 1), flow, sign, shape, into(outer, 1))

    def store(k, here, i, j, values):
        total[(k,) + spot(i, j)] = here(0, i, j) + values[0]

    last_steps(partner, snaps, carried_on, outer, velocity, store, (0,))
    if partner == 1:
        for k in range(2):
            whole[high * (edge_count - 1) + k * (1 - 2 * high)] = total[k]
            whole[(1 - high) * (edge_count - 1) - k * (1 - 2 * high)] = before[0][k]
        split_rows(whole, pieces)


def finish_kernel(blocks, snaps, carried_on, outer_one, outer_two, edges, rest, own_flow, other_flow, velocity, inner,
                  out, final, later, sems):
    depth, shape = carried_on.shape[1], carried_on.shape[2:]
    fetched = lax.rem(lax.axis_index("tm"), 2)
    place = lax.axis_index("space")
    inside = jnp.logical_and(place > 0, place < blocks - 1)
    high, sign = side_of(1)
    for i, j in tiles(shape):
        at = (snaps[0, 1],) + spot(i, j)
        u = jnp.where(high == fetched, own_flow[at], other_flow[at])
        value = rest[(0,) + spot(i, j)] + (diffusion[1] - (0.25 * sign) * u) * edges[(1, 0) + spot(i, j)]
        later[spot(i, j)] = jnp.where(inside, value, 0.0)

    def beyond(f, i, j):
        return later[spot(i, j)] if f == 1 else outer_two[(0, 0) + spot(i, j)]

    for partner, outer in enumerate((outer_one, outer_two)):
        high, unused = side_of(partner)

        def store(k, here, i, j, values, high=high):
            into(final, high * (edge_count - 1) + k * (1 - 2 * high))(i, j, values)

        last_steps(partner, snaps, carried_on, outer, velocity, store, (0, 1), beyond if partner else None)
    copies = [
        pltpu.make_async_copy(final.at[:, pl.ds(0, 2)], out.at[:, pl.ds(0, 2)], sems.at[0]),
        pltpu.make_async_copy(final.at[:, pl.ds(2, 2)], out.at[:, pl.ds(depth - 2, 2)], sems.at[1]),
    ]
    for copy in copies:
        copy.start()
    for copy in copies:
        copy.wait()


def sum_kernel(inner, inner_across, *refs):
    parts, out = refs[:-1], refs[-1]
    depth = out.shape[0]
    outer = functools.reduce(jnp.add, [part[...] for part in parts])
    out[2 : depth - 2] = inner[...] + inner_across[...]
    out[0:2] = outer[0:2]
    out[depth - 2 : depth] = outer[2:4]


def solution(mesh):
    slabs, blocks = mesh.shape["tm"], mesh.shape["space"]
    vmem, smem = pl.BlockSpec(memory_space=pltpu.VMEM), pl.BlockSpec(memory_space=pltpu.SMEM)
    hbm = pl.BlockSpec(memory_space=pltpu.HBM)
    sem = pltpu.SemaphoreType.DMA

    def params(mebibytes):
        return pltpu.CompilerParams(vmem_limit_bytes=mebibytes * 1024 * 1024)

    def cost(microseconds):
        return pl.CostEstimate(flops=0, bytes_accessed=int(microseconds * 3.6e6), transcendentals=0)

    def index(t, s):
        return (t % slabs) * blocks + s % blocks

    def moved(array, to):
        pairs = [(index(t, s), index(*to(t, s))) for t in range(slabs) for s in range(blocks)]
        return lax.ppermute(array, ("tm", "space"), pairs)

    def exchanged(array, by, earlier):
        def to(t, s):
            partner = ((s + by) ^ 1) - by
            return (t - earlier, partner) if 0 <= partner < blocks else (t ^ 1, s)

        return moved(array, to)

    def fetched(t, s):
        source = s + 1 - 2 * (t % 2)
        return (t ^ 2, source) if 0 <= source < blocks else (t ^ 1, s)

    def body(slab_states, velocity, snap_of_step):
        start = slab_states[0]
        fields, depth, ny, nz = start.shape

        def shaped(*lead, rows=ny):
            return jax.ShapeDtypeStruct(lead + (rows, nz), jnp.float32)

        def room(*lead):
            return pltpu.VMEM(lead + (ny, nz), jnp.float32)

        layer = shaped(4)
        pieces = (shaped(4, rows=ny // slabs),) * slabs

        state = moved(start, lambda t, s: (t - 1, s))
        snaps_next = moved(snap_of_step, lambda t, s: (t - 1, s))
        message_one, message_two, flow_out = pl.pallas_call(
            start_kernel,
            out_shape=(layer, layer, shaped(velocity.shape[0])),
            in_specs=[hbm] * 3,
            out_specs=(vmem,) * 3,
            scratch_shapes=[
                pltpu.SMEM(snap_of_step.shape, jnp.int32),
                room(fields, edge_count),
                room(*velocity.shape[:2], 2),
                sem((5,)),
            ],
            compiler_params=params(56),
            cost_estimate=cost(2),
        )(snap_of_step, start, velocity)
        halo_one = exchanged(message_one, 0, 1)
        halo_two = exchanged(message_two, 1, 1)
        own_flow = moved(flow_out, fetched)
        other_flow = moved(own_flow, lambda t, s: (t ^ 1, s))
        widened, edges, halo, halo_rest = [None] * 2, [None] * 2, [halo_one, halo_two], []
        for partner in (0, 1):
            widened[partner], edges[partner], message, *rest = pl.pallas_call(
                functools.partial(first_kernel, blocks, slabs, partner),
                out_shape=(shaped(fields, 4), shaped(fields, 2)) + ((shaped(3), shaped(1)) if partner else (layer,)),
                in_specs=[smem, smem] + [vmem] * 5 + [hbm],
                out_specs=(vmem,) * (3 + partner),
                scratch_shapes=[room(fields)],
                compiler_params=params(32),
                cost_estimate=cost(1.5),
            )(snap_of_step, snaps_next, state, halo[partner], own_flow, other_flow, velocity, start)
            halo[partner] = exchanged(message, partner, 0)
            halo_rest += [exchanged(part, partner, 0) for part in rest]
        pair = jax.ShapeDtypeStruct((2,) + pieces[0].shape, jnp.float32)
        carried_on, inner, kept, to_core = pl.pallas_call(
            functools.partial(inner_kernel, slabs),
            out_shape=(shaped(fields, depth), shaped(fields, depth), pair, pair),
            in_specs=[smem, smem] + [vmem] * 6 + [hbm],
            out_specs=(vmem, hbm, vmem, vmem),
            scratch_shapes=[
                room(fields, depth), room(fields, depth + 2), room(fields, depth - 4), room(depth - 4), sem(()),
            ],
            compiler_params=params(32),
            cost_estimate=cost(3),
        )(snap_of_step, snaps_next, state, *widened, *edges, velocity, start)
        inner_own, inner_across = pl.pallas_call(
            chip_kernel,
            out_shape=pieces[:2],
            in_specs=[vmem, vmem],
            out_specs=(vmem, vmem),
            compiler_params=params(16),
            cost_estimate=cost(0.5),
        )(kept, moved(to_core, lambda t, s: (t ^ 1, s)))
        inner_across = moved(inner_across, lambda t, s: (t ^ 2, s))
        outer_one, total_one = pl.pallas_call(
            functools.partial(outer_kernel, blocks, slabs, 0),
            out_shape=(shaped(fields, 2), shaped(2)),
            in_specs=[smem] + [vmem] * 6,
            out_specs=(vmem,) * 2,
            scratch_shapes=[room(fields)],
            compiler_params=params(32),
            cost_estimate=cost(0.5),
        )(snap_of_step, edges[0], halo[0], own_flow, other_flow, carried_on, velocity)
        outer_two, *outer_pieces = pl.pallas_call(
            functools.partial(outer_kernel, blocks, slabs, 1),
            out_shape=(shaped(fields, 2),) + pieces,
            in_specs=[smem] + [vmem] * 7,
            out_specs=(vmem,) * (1 + slabs),
            scratch_shapes=[room(fields), room(2), room(edge_count)],
            compiler_params=params(32),
            cost_estimate=cost(0.5),
        )(snap_of_step, edges[1], halo[1], own_flow, other_flow, carried_on, velocity, total_one)
        outer_parts = outer_pieces[:1] + [
            moved(outer_pieces[by], lambda t, s, by=by: (t ^ by, s)) for by in range(1, slabs)
        ]
        final = pl.pallas_call(
            functools.partial(finish_kernel, blocks),
            out_shape=shaped(fields, depth),
            in_specs=[smem] + [vmem] * 8 + [hbm],
            out_specs=hbm,
            scratch_shapes=[room(fields, edge_count), room(), sem((2,))],
            input_output_aliases={9: 0},
            compiler_params=params(32),
            cost_estimate=cost(1),
        )(snap_of_step, carried_on, outer_one, outer_two, edges[1], *halo_rest, own_flow, other_flow, velocity, inner)
        gradient = pl.pallas_call(
            sum_kernel,
            out_shape=shaped(depth, rows=ny // slabs),
            in_specs=[vmem] * (2 + slabs),
            out_specs=vmem,
            compiler_params=params(16),
            cost_estimate=cost(0.5),
        )(inner_own, inner_across, *outer_parts)
        return (final[None], gradient)

    return jax.shard_map(
        body,
        mesh=mesh,
        in_specs=(P("tm", None, "space", None, None), P(None, None, "space", None, None), P("tm", None)),
        out_specs=(P("tm", None, "space", None, None), P("space", "tm", None)),
        check_vma=False,
    )
```
